32 devices in a mesh: lon: 8 (over z, y), lat: 4 (over x, core).
Axes of the slice: x: 2, y: 2, z: 4, core: 2. Of those that a mesh axis runs over, the one named last changes fastest.
Arguments:
- inputs: bfloat16 [32, 512, 384], P('lat', 'lon'), may hold values from -6 to 6
- conv1_weight: bfloat16 [3, 3, 384, 384], replicated, may hold values from -0.109375 to 0.109375
- conv2_weight: bfloat16 [3, 3, 384, 384], replicated, may hold values from -0.109375 to 0.109375
- cotangent: bfloat16 [32, 512, 384], P('lat', 'lon'), may hold values from -6 to 6
Outputs:
- output: bfloat16 [32, 512, 384], P('lat', 'lon')
- input_grad: bfloat16 [32, 512, 384], P('lat', 'lon')
- conv1_grad: float32 [3, 3, 384, 384], P(None, None, 'lon', 'lat')
- conv2_grad: float32 [3, 3, 384, 384], P(None, None, 'lon', 'lat')
The draws below stay inside these ranges and needn't reach their ends.
All inputs are finite; a program needn't handle non-finite values.
Results may differ from the reference program's by a relative error of at most 0.0033.
Values may be sent and summed in bfloat16 or wider, within the bound.
No kernel may reach another device: no remote copies, remote signals or barrier semaphores. Data moves between devices by JAX's collectives and lax.ppermute only.
A program may use at most 128 MiB of HBM per device.

```python
import jax
import jax.numpy as jnp
from jax import lax

C = 384
KERNEL_SPREAD = 64
LAT = 32
LON = 512


def spiked(drawn, own_key, source, target, shards_of, factor):
    owner, partner = [(jnp.arange(drawn.shape[position]) // (drawn.shape[position] // shards_of)).reshape([-1 if axis == position else 1 for axis in range(drawn.ndim)]) for position in (source, target)]
    chosen = jax.random.permutation(own_key, shards_of)[partner]
    strong = (owner == chosen) | (owner == (partner + shards_of // 2) % shards_of)
    return jnp.where(strong, factor * drawn, drawn)


def block_levels(stream_key, dims, shards, smallest, high):
    gain, own = 1.0, jax.random.fold_in(stream_key, 6)
    for axis_at, parts in shards:
        steps = jnp.exp(jax.random.uniform(jax.random.fold_in(own, axis_at), (parts,), jnp.float32, smallest / len(shards), high / len(shards)))
        gain = gain * jnp.repeat(steps, dims[axis_at] // parts).reshape([-1 if axis == axis_at else 1 for axis in range(len(dims))])
    return gain


def noise(stream_key, dims, scale, limit, cuts=(), dtype=jnp.bfloat16):
    loudness = block_levels(stream_key, dims, cuts, -0.22, 0.18) if cuts else 1.0
    entries = jax.random.normal(stream_key, dims, jnp.float32) * scale * loudness
    return jnp.minimum(jnp.maximum(entries, -limit), limit).astype(dtype)


def noise_with(stream_key, extent, scale, limit, cuts, heavy, kind=jnp.bfloat16):
    result = scale * jax.random.normal(stream_key, extent, jnp.float32)
    if cuts:
        result = result * block_levels(stream_key, extent, cuts, -0.22, 0.18)
    return jnp.clip(spiked(result, jax.random.fold_in(stream_key, 3), *heavy), -limit, limit).astype(kind)


def setup_inputs(seed: int = 0) -> dict:
    key_of = jax.random.split(jax.random.key(seed), 5)
    inputs = noise_with(key_of[0], (LAT, LON, C), 1.0, 6.0, ((0, 4), (1, 8)), (1, 2, 8, 2.0))
    conv1_weight = noise(key_of[1], (3, 3, C, C), (9 * C) ** -0.5, 0.109375)
    conv2_weight = noise(key_of[2], (3, 3, C, C), (9 * C) ** -0.5, 0.109375)
    cotangent = noise_with(key_of[3], (LAT, LON, C), 1.0, 6.0, ((0, 4), (1, 8)), (1, 2, 8, 2.0))
    return dict(inputs=inputs, conv1_weight=conv1_weight, conv2_weight=conv2_weight, cotangent=cotangent)


def shifted(field, lat_step, longitude_stride):
    padded_field = jnp.pad(field, ((1, 1), (0, 0), (0, 0)))
    part = padded_field[1 + lat_step:1 + lat_step + LAT]
    return jnp.roll(part, -KERNEL_SPREAD * longitude_stride, axis=1)

def convolve(field, weight, direction):
    total = jnp.zeros((LAT * LON, C), jnp.float32)
    for lat_step in (-1, 0, 1):
        for longitude_stride in (-1, 0, 1):
            tap = weight[lat_step + 1, longitude_stride + 1].astype(jnp.float32)
            if direction < 0:
                tap = tap.T
            moved = shifted(field, direction * lat_step, direction * longitude_stride).reshape(LAT * LON, C)
            total = total + jnp.dot(moved, tap, precision=lax.Precision.HIGHEST)
    return total

def kernel_grad(field, grad, scale):
    rows = []
    for lat_step in (-1, 0, 1):
        row = []
        for longitude_stride in (-1, 0, 1):
            moved = shifted(field, lat_step, longitude_stride).reshape(LAT * LON, C)
            row.append(jnp.dot(moved.T, grad, precision=lax.Precision.HIGHEST) * scale)
        rows.append(jnp.stack(row))
    return jnp.stack(rows)

def reference(inputs, conv1_weight, conv2_weight, cotangent):
    scale = (LAT * LON) ** (-0.5)
    source = inputs.astype(jnp.float32)
    first = convolve(source, conv1_weight, 1)
    cdf = 0.5 * (1.0 + jax.scipy.special.erf(first / jnp.sqrt(2.0)))
    hidden = (first * cdf).astype(jnp.bfloat16)
    hidden_field = hidden.astype(jnp.float32).reshape(LAT, LON, C)
    second = convolve(hidden_field, conv2_weight, 1)
    output = (source.reshape(LAT * LON, C) + second).astype(jnp.bfloat16).reshape(LAT, LON, C)
    upward = cotangent.astype(jnp.float32)
    upstream = convolve(upward, conv2_weight, -1)
    density = jnp.exp(-0.5 * first * first) / jnp.sqrt(2.0 * jnp.pi)
    pre_grad = (upstream * (cdf + first * density)).astype(jnp.bfloat16)
    pre_field = pre_grad.astype(jnp.float32).reshape(LAT, LON, C)
    back = convolve(pre_field, conv1_weight, -1)
    input_grad = (upward.reshape(LAT * LON, C) + back).astype(jnp.bfloat16).reshape(LAT, LON, C)
    conv2_grad = kernel_grad(hidden_field, upward.reshape(LAT * LON, C), scale)
    conv1_grad = kernel_grad(source, pre_grad.astype(jnp.float32), scale)
    return (output, input_grad, conv1_grad, conv2_grad)
```

```python
import functools

import jax
import jax.numpy as jnp
from jax import lax
from jax.experimental import pallas as pl
from jax.experimental.pallas import tpu as pltpu
from jax.sharding import PartitionSpec as P

F32, BF16 = jnp.float32, jnp.bfloat16


def passed_along(shard, axis, by):
    length = lax.axis_size(axis)
    return lax.ppermute(shard, axis, [(i, (i + by) % length) for i in range(length)])


def padded(shard, sides, width):
    for axis, dim in sides:
        size, length = (lax.axis_size(axis), shard.shape[dim])
        up = [(i, (i + 1) % size) for i in range(size - 1)]
        down = [(j, i) for i, j in up]
        last = lax.slice_in_dim(shard, length - width, length, axis=dim)
        initial = lax.slice_in_dim(shard, 0, width, axis=dim)
        before = lax.ppermute(last, axis, up)
        after = lax.ppermute(initial, axis, down)
        shard = jnp.concatenate([before, shard, after], axis=dim)
    return shard


def extend(field):
    western = passed_along(field, "lon", 1)
    eastern = passed_along(field, "lon", -1)
    widened = jnp.concatenate([western, field, eastern], axis=1)
    return padded(widened, (("lat", 0),), 1)


def windows(padded_field, count_of_rows, lon_width, channels, direction):
    pieces = []
    for lat_step in (-1, 0, 1):
        for longitude_stride in (-1, 0, 1):
            row_start = 1 + direction * lat_step
            column_begin = lon_width + direction * lon_width * longitude_stride
            pieces.append(
                padded_field[
                    row_start : row_start + count_of_rows, column_begin : column_begin + lon_width
                ]
            )
    stacked = jnp.concatenate(pieces, axis=2)
    return stacked.reshape(count_of_rows * lon_width, 9 * channels)


def full_terms(stacked, grad, scale, channels):
    product = lax.dot_general(
        stacked, grad, (((0,), (0,)), ((), ())), preferred_element_type=jnp.float32
    )
    return (product * scale).reshape(9, channels, channels)


def local(inputs, conv1_weight, conv2_weight, cotangent):
    count_of_rows, lon_width, channels = inputs.shape
    cells = count_of_rows * lon_width
    lon_count = lax.axis_size("lon")
    latitude_count = lax.axis_size("lat")
    scale = (count_of_rows * latitude_count * lon_width * lon_count) ** (-0.5)
    forward_one = conv1_weight.reshape(9 * channels, channels)
    forward_two = conv2_weight.reshape(9 * channels, channels)
    turned_one = jnp.swapaxes(conv1_weight, 2, 3).reshape(9 * channels, channels)
    turned_two = jnp.swapaxes(conv2_weight, 2, 3).reshape(9 * channels, channels)
    source_field, cot_field = (inputs, cotangent)

    def stack_of(field, direction):
        return windows(extend(field), count_of_rows, lon_width, channels, direction)

    def as_field(flat):
        return flat.reshape(count_of_rows, lon_width, channels)

    stack_input = stack_of(source_field, 1)
    first = jnp.dot(stack_input, forward_one, preferred_element_type=jnp.float32)
    cdf = 0.5 * (1.0 + jax.scipy.special.erf(first / jnp.sqrt(2.0)))
    hidden = (first * cdf).astype(jnp.bfloat16)
    stack_hidden = stack_of(as_field(hidden), 1)
    second = jnp.dot(stack_hidden, forward_two, preferred_element_type=jnp.float32)
    flat_input = source_field.reshape(cells, channels)
    output = (flat_input.astype(jnp.float32) + second).astype(jnp.bfloat16)
    flat_cot = cot_field.reshape(cells, channels)
    stacked_cotangent = stack_of(cot_field, -1)
    upstream = jnp.dot(stacked_cotangent, turned_two, preferred_element_type=jnp.float32)
    density = jnp.exp(-0.5 * first * first) / jnp.sqrt(2.0 * jnp.pi)
    pre_grad = (upstream * (cdf + first * density)).astype(jnp.bfloat16)
    stack_pre = stack_of(as_field(pre_grad), -1)
    back = jnp.dot(stack_pre, turned_one, preferred_element_type=jnp.float32)
    input_grad = (flat_cot.astype(jnp.float32) + back).astype(jnp.bfloat16)
    output = output.reshape(count_of_rows, lon_width, channels)
    input_grad = input_grad.reshape(count_of_rows, lon_width, channels)
    in_part = channels // lon_count
    out_part = channels // latitude_count
    terms_one = full_terms(stack_input, pre_grad, scale, channels)
    terms_two = full_terms(stack_hidden, flat_cot, scale, channels)
    partly = (
        lax.psum_scatter(terms_one, "lon", scatter_dimension=1, tiled=True),
        lax.psum_scatter(terms_two, "lon", scatter_dimension=1, tiled=True),
    )
    grad_one, grad_two = (
        lax.psum_scatter(partly[0], "lat", scatter_dimension=2, tiled=True),
        lax.psum_scatter(partly[1], "lat", scatter_dimension=2, tiled=True),
    )
    conv1_grad = grad_one.reshape(3, 3, in_part, out_part)
    conv2_grad = grad_two.reshape(3, 3, in_part, out_part)
    return (output, input_grad, conv1_grad, conv2_grad)


def write_stack(field, stack_ref, band, step):
    cells, channels = field.shape
    wide = field.astype(F32)
    place = lax.broadcasted_iota(jnp.int32, (cells, channels), 0) % band
    above = jnp.where(place >= step, pltpu.roll(wide, step, 0), 0.0).astype(BF16)
    below = jnp.where(place < band - step, pltpu.roll(wide, cells - step, 0), 0.0).astype(BF16)
    for at, part in enumerate((above, field, below)):
        columns = slice(at * channels, (at + 1) * channels)
        stack_ref[band : band + cells, columns] = part
        stack_ref[0:band, columns] = part[cells - band :]
        stack_ref[band + cells :, columns] = part[0:band]


def convolved(stack_ref, weight_ref, band, cells):
    total = None
    for b in range(3):
        channels = weight_ref.shape[2]
        tap = weight_ref[:, b].reshape(3 * channels, channels)
        term = jnp.dot(stack_ref[b * band : b * band + cells, :], tap, preferred_element_type=F32)
        total = term if total is None else total + term
    return total


def convolved_back(stack_ref, weight_ref, band, cells):
    total = None
    for b in range(3):
        tap = jnp.concatenate([weight_ref[2 - a, 2 - b] for a in range(3)], axis=1)
        term = lax.dot_general(
            stack_ref[b * band : b * band + cells, :],
            tap,
            (((1,), (1,)), ((), ())),
            preferred_element_type=F32,
        )
        total = term if total is None else total + term
    return total


def inner_kernel(band, step, place_ref, own_ref, other_ref, one_ref, two_ref,
                 hidden_ref, pre_ref, keep_ref, give_ref,
                 stack_ref, grad_stack_ref, turned_ref, first_ref, up_ref, act_ref, sums_ref):
    chip, core = place_ref[0], place_ref[1]
    cells, channels = first_ref.shape
    rows = 32
    for group, fields_ref in enumerate((own_ref, other_ref)):
        source = fields_ref[:, 0].reshape(cells, channels)
        cot = fields_ref[:, 1].reshape(cells, channels)
        write_stack(source, stack_ref, band, step)
        write_stack(cot, grad_stack_ref.at[group], band, step)
        first_ref[...] = convolved(stack_ref, one_ref, band, cells)
        up_ref[...] = convolved_back(grad_stack_ref.at[group], two_ref, band, cells)

        def activate(at, carry):
            span = pl.ds(pl.multiple_of(at * rows, rows), rows)
            first = first_ref[span, :]
            cdf = 0.5 * (1.0 + lax.erf(first * (0.5**0.5)))
            density = jnp.exp(-0.5 * first * first) * ((2.0 * jnp.pi) ** -0.5)
            act_ref[0, span, :] = (first * cdf).astype(BF16)
            act_ref[1, span, :] = (up_ref[span, :] * (cdf + first * density)).astype(BF16)
            return carry

        lax.fori_loop(0, cells // rows, activate, 0)
        if group == 0:
            hidden_ref[...] = act_ref[0]
            pre_ref[...] = act_ref[1]

        @pl.when(core == 0)
        def _():
            write_stack(act_ref[1], grad_stack_ref.at[group], band, step)
            turned_ref[group] = source.T

        @pl.when(core == 1)
        def _():
            turned_ref[group] = act_ref[0].T

    for b in range(3):
        span = slice(b * band, b * band + cells)
        terms = [
            jnp.dot(turned_ref[group], grad_stack_ref[group, span, :], preferred_element_type=F32)
            for group in range(2)
        ]
        total = terms[0] + terms[1]
        for a in range(3):
            sums_ref[(2 - a) * 3 + 2 - b] = total[:, a * channels : (a + 1) * channels]

    half, part = channels // 2, keep_ref.shape[0]
    deep = channels // part

    def packed(west, east, at, depth):
        low = jnp.concatenate([west[:, :half], east[:, :half]], axis=1)
        high = jnp.concatenate([west[:, half:], east[:, half:]], axis=1)
        span = slice(at, at + depth)
        return span, jnp.where(chip == 0, low, high), jnp.where(chip == 0, high, low)

    for piece in range(part):
        begin = piece * deep
        for tap in range(4):
            span, mine, others = packed(
                sums_ref[tap, begin : begin + deep, :],
                sums_ref[5 + tap, begin : begin + deep, :],
                tap * deep,
                deep,
            )
            keep_ref[piece, span, :] = mine.astype(BF16)
            give_ref[piece, span, :] = others.astype(BF16)
        short = deep // 2
        rest = jnp.zeros((32 - short, channels), F32)
        span, mine, others = packed(
            jnp.concatenate([sums_ref[4, begin : begin + short, :], rest], axis=0),
            jnp.concatenate([sums_ref[4, begin + short : begin + deep, :], rest], axis=0),
            4 * deep,
            32,
        )
        keep_ref[piece, span, :] = mine.astype(BF16)
        give_ref[piece, span, :] = others.astype(BF16)


def outer_kernel(band, step, own_ref, hidden_ref, pre_ref, one_ref, two_ref, out_ref, stack_ref):
    cells, channels = hidden_ref.shape
    shape = (out_ref.shape[0],) + out_ref.shape[2:]
    write_stack(hidden_ref[...], stack_ref, band, step)
    second = convolved(stack_ref, two_ref, band, cells)
    source = own_ref[:, 0].reshape(cells, channels)
    out_ref[:, 0] = (source.astype(F32) + second).astype(BF16).reshape(shape)
    write_stack(pre_ref[...], stack_ref, band, step)
    back = convolved_back(stack_ref, one_ref, band, cells)
    cot = own_ref[:, 1].reshape(cells, channels)
    out_ref[:, 1] = (cot.astype(F32) + back).astype(BF16).reshape(shape)


def fast_local(inputs, conv1_weight, conv2_weight, cotangent):
    rows, width, channels = inputs.shape
    lon, lat = lax.axis_size("lon"), lax.axis_size("lat")
    devices = lon * lat
    step = width // devices
    cells = rows * width
    band = rows * lat * step
    scale = (rows * lat * width * lon) ** (-0.5)
    place = lax.axis_index("lat")
    chip, core = place // 2, place % 2

    both = jnp.stack([inputs, cotangent]).reshape(2, rows, devices, step, channels)
    both = both.transpose(2, 0, 1, 3, 4).reshape(devices, 2, rows * step, channels)
    own = lax.all_to_all(both, ("lon", "lat"), 0, 0, tiled=True)
    other = lax.ppermute(own, "lat", [(i, i ^ 1) for i in range(lat)])

    vmem = pl.BlockSpec(memory_space=pltpu.VMEM)
    params = pltpu.CompilerParams(vmem_limit_bytes=52 * 2**20)
    deep = channels // lon
    height = 4 * deep + 32
    flops = 2 * 9 * cells * channels * channels
    field = jax.ShapeDtypeStruct((cells, channels), BF16)
    wire = jax.ShapeDtypeStruct((lon, height, channels), BF16)
    hidden, pre_grad, keep, give = pl.pallas_call(
        functools.partial(inner_kernel, band, step),
        out_shape=(field, field, wire, wire),
        in_specs=[pl.BlockSpec(memory_space=pltpu.SMEM)] + [vmem] * 4,
        out_specs=(vmem,) * 4,
        scratch_shapes=[
            pltpu.VMEM((cells + 2 * band, 3 * channels), BF16),
            pltpu.VMEM((2, cells + 2 * band, 3 * channels), BF16),
            pltpu.VMEM((2, channels, cells), BF16),
            pltpu.VMEM((cells, channels), F32),
            pltpu.VMEM((cells, channels), F32),
            pltpu.VMEM((2, cells, channels), BF16),
            pltpu.VMEM((9, channels, channels), F32),
        ],
        compiler_params=params,
        cost_estimate=pl.CostEstimate(flops=6 * flops, bytes_accessed=12 * 2**20, transcendentals=0),
    )(jnp.stack([chip, core]).astype(jnp.int32), own, other, conv1_weight, conv2_weight)

    given = lax.ppermute(give, "lat", [(i, i ^ 2) for i in range(lat)])
    fields = pl.pallas_call(
        functools.partial(outer_kernel, band, step),
        out_shape=jax.ShapeDtypeStruct((devices, 2, rows * step, channels), BF16),
        in_specs=[vmem] * 5,
        out_specs=vmem,
        scratch_shapes=[pltpu.VMEM((cells + 2 * band, 3 * channels), BF16)],
        compiler_params=params,
        cost_estimate=pl.CostEstimate(flops=2 * flops, bytes_accessed=8 * 2**20, transcendentals=0),
    )(own, hidden, pre_grad, conv1_weight, conv2_weight)
    fields = lax.all_to_all(fields, ("lon", "lat"), 0, 0, tiled=True)
    fields = fields.reshape(devices, 2, rows, step, channels).transpose(1, 2, 0, 3, 4)
    output, input_grad = fields.reshape(2, rows, width, channels)

    pair = (keep.astype(F32) + given.astype(F32)).astype(BF16)
    parts = lax.all_to_all(pair, "lon", 0, 0, tiled=True)
    total = jnp.sum(parts.astype(F32), axis=0) * scale
    half, short = channels // 2, deep // 2
    west, east = total[:, :half], total[:, half:]
    middle = slice(4 * deep, 4 * deep + short)
    whole = jnp.concatenate([west[: 4 * deep], west[middle], east[middle], east[: 4 * deep]], axis=0)
    whole = whole.reshape(9, deep, half)
    quarter = half // 2
    low, high = whole[:, :, :quarter], whole[:, :, quarter:]
    mine = jnp.where(core == 0, low, high)
    theirs = lax.ppermute(
        jnp.where(core == 0, high, low), "lat", [(i, i ^ 1) for i in range(lat)]
    )
    shape = (3, 3, deep, quarter)
    conv1_grad = jnp.where(core == 0, mine, theirs).reshape(shape)
    conv2_grad = jnp.where(core == 0, theirs, mine).reshape(shape)
    return (output, input_grad, conv1_grad, conv2_grad)


def is_fast(mesh):
    return dict(mesh.shape) == {"lon": 8, "lat": 4}


def solution(mesh):
    in_specs = (P("lat", "lon", None), P(), P(), P("lat", "lon", None))
    out_specs = (
        P("lat", "lon", None),
        P("lat", "lon", None),
        P(None, None, "lon", "lat"),
        P(None, None, "lon", "lat"),
    )
    body = fast_local if is_fast(mesh) else local
    return jax.shard_map(body, mesh=mesh, in_specs=in_specs, out_specs=out_specs, check_vma=False)
```

```python
import functools

import jax
import jax.numpy as jnp
from jax import lax
from jax.experimental import pallas as pl
from jax.experimental.pallas import tpu as pltpu
from jax.sharding import PartitionSpec as P

F32, BF16 = jnp.float32, jnp.bfloat16


def passed_along(shard, axis, by):
    length = lax.axis_size(axis)
    return lax.ppermute(shard, axis, [(i, (i + by) % length) for i in range(length)])


def padded(shard, sides, width):
    for axis, dim in sides:
        size, length = (lax.axis_size(axis), shard.shape[dim])
        up = [(i, (i + 1) % size) for i in range(size - 1)]
        down = [(j, i) for i, j in up]
        last = lax.slice_in_dim(shard, length - width, length, axis=dim)
        initial = lax.slice_in_dim(shard, 0, width, axis=dim)
        before = lax.ppermute(last, axis, up)
        after = lax.ppermute(initial, axis, down)
        shard = jnp.concatenate([before, shard, after], axis=dim)
    return shard


def extend(field):
    western = passed_along(field, "lon", 1)
    eastern = passed_along(field, "lon", -1)
    widened = jnp.concatenate([western, field, eastern], axis=1)
    return padded(widened, (("lat", 0),), 1)


def windows(padded_field, count_of_rows, lon_width, channels, direction):
    pieces = []
    for lat_step in (-1, 0, 1):
        for longitude_stride in (-1, 0, 1):
            row_start = 1 + direction * lat_step
            column_begin = lon_width + direction * lon_width * longitude_stride
            pieces.append(
                padded_field[
                    row_start : row_start + count_of_rows, column_begin : column_begin + lon_width
                ]
            )
    stacked = jnp.concatenate(pieces, axis=2)
    return stacked.reshape(count_of_rows * lon_width, 9 * channels)


def full_terms(stacked, grad, scale, channels):
    product = lax.dot_general(
        stacked, grad, (((0,), (0,)), ((), ())), preferred_element_type=jnp.float32
    )
    return (product * scale).reshape(9, channels, channels)


def local(inputs, conv1_weight, conv2_weight, cotangent):
    count_of_rows, lon_width, channels = inputs.shape
    cells = count_of_rows * lon_width
    lon_count = lax.axis_size("lon")
    latitude_count = lax.axis_size("lat")
    scale = (count_of_rows * latitude_count * lon_width * lon_count) ** (-0.5)
    forward_one = conv1_weight.reshape(9 * channels, channels)
    forward_two = conv2_weight.reshape(9 * channels, channels)
    turned_one = jnp.swapaxes(conv1_weight, 2, 3).reshape(9 * channels, channels)
    turned_two = jnp.swapaxes(conv2_weight, 2, 3).reshape(9 * channels, channels)
    source_field, cot_field = (inputs, cotangent)

    def stack_of(field, direction):
        return windows(extend(field), count_of_rows, lon_width, channels, direction)

    def as_field(flat):
        return flat.reshape(count_of_rows, lon_width, channels)

    stack_input = stack_of(source_field, 1)
    first = jnp.dot(stack_input, forward_one, preferred_element_type=jnp.float32)
    cdf = 0.5 * (1.0 + jax.scipy.special.erf(first / jnp.sqrt(2.0)))
    hidden = (first * cdf).astype(jnp.bfloat16)
    stack_hidden = stack_of(as_field(hidden), 1)
    second = jnp.dot(stack_hidden, forward_two, preferred_element_type=jnp.float32)
    flat_input = source_field.reshape(cells, channels)
    output = (flat_input.astype(jnp.float32) + second).astype(jnp.bfloat16)
    flat_cot = cot_field.reshape(cells, channels)
    stacked_cotangent = stack_of(cot_field, -1)
    upstream = jnp.dot(stacked_cotangent, turned_two, preferred_element_type=jnp.float32)
    density = jnp.exp(-0.5 * first * first) / jnp.sqrt(2.0 * jnp.pi)
    pre_grad = (upstream * (cdf + first * density)).astype(jnp.bfloat16)
    stack_pre = stack_of(as_field(pre_grad), -1)
    back = jnp.dot(stack_pre, turned_one, preferred_element_type=jnp.float32)
    input_grad = (flat_cot.astype(jnp.float32) + back).astype(jnp.bfloat16)
    output = output.reshape(count_of_rows, lon_width, channels)
    input_grad = input_grad.reshape(count_of_rows, lon_width, channels)
    in_part = channels // lon_count
    out_part = channels // latitude_count
    terms_one = full_terms(stack_input, pre_grad, scale, channels)
    terms_two = full_terms(stack_hidden, flat_cot, scale, channels)
    partly = (
        lax.psum_scatter(terms_one, "lon", scatter_dimension=1, tiled=True),
        lax.psum_scatter(terms_two, "lon", scatter_dimension=1, tiled=True),
    )
    grad_one, grad_two = (
        lax.psum_scatter(partly[0], "lat", scatter_dimension=2, tiled=True),
        lax.psum_scatter(partly[1], "lat", scatter_dimension=2, tiled=True),
    )
    conv1_grad = grad_one.reshape(3, 3, in_part, out_part)
    conv2_grad = grad_two.reshape(3, 3, in_part, out_part)
    return (output, input_grad, conv1_grad, conv2_grad)


def write_stack(field, stack_ref, band, step):
    cells, channels = field.shape
    wide = field.astype(F32)
    place = lax.broadcasted_iota(jnp.int32, (cells, channels), 0) % band
    above = jnp.where(place >= step, pltpu.roll(wide, step, 0), 0.0).astype(BF16)
    below = jnp.where(place < band - step, pltpu.roll(wide, cells - step, 0), 0.0).astype(BF16)
    for at, part in enumerate((above, field, below)):
        columns = slice(at * channels, (at + 1) * channels)
        stack_ref[band : band + cells, columns] = part
        stack_ref[0:band, columns] = part[cells - band :]
        stack_ref[band + cells :, columns] = part[0:band]


def convolved(stack_ref, weight_ref, band, cells):
    total = None
    for b in range(3):
        channels = weight_ref.shape[2]
        tap = weight_ref[:, b].reshape(3 * channels, channels)
        term = jnp.dot(stack_ref[b * band : b * band + cells, :], tap, preferred_element_type=F32)
        total = term if total is None else total + term
    return total


def convolved_back(stack_ref, weight_ref, band, cells):
    total = None
    for b in range(3):
        tap = jnp.concatenate([weight_ref[2 - a, 2 - b] for a in range(3)], axis=1)
        term = lax.dot_general(
            stack_ref[b * band : b * band + cells, :],
            tap,
            (((1,), (1,)), ((), ())),
            preferred_element_type=F32,
        )
        total = term if total is None else total + term
    return total


def forward_kernel(band, step, source_ref, weight_ref, hidden_ref, slope_ref, send_ref, stack_ref, first_ref):
    cells, channels = first_ref.shape
    rows = 32
    source = source_ref[...].reshape(cells, channels)
    write_stack(source, stack_ref, band, step)
    first_ref[...] = convolved(stack_ref, weight_ref, band, cells)

    def activate(at, carry):
        span = pl.ds(pl.multiple_of(at * rows, rows), rows)
        first = first_ref[span, :]
        cdf = 0.5 * (1.0 + lax.erf(first * (0.5**0.5)))
        density = jnp.exp(-0.5 * first * first) * ((2.0 * jnp.pi) ** -0.5)
        hidden_ref[span, :] = (first * cdf).astype(BF16)
        slope_ref[span, :] = cdf + first * density
        return carry

    lax.fori_loop(0, cells // rows, activate, 0)
    half = send_ref.shape[1]
    deep = half // 4
    for core, turned in enumerate((source.T, hidden_ref[...].T)):
        for y in range(2):
            for z in range(4):
                begin = (2 * z + y) * deep
                for x in range(2):
                    send_ref[y * 4 + x * 2 + core, z * deep : (z + 1) * deep, :] = turned[begin : begin + deep]


def backward_kernel(band, step, cot_ref, slope_ref, weight_ref, pre_ref, send_ref, stack_ref):
    cells, channels = slope_ref.shape
    cot = cot_ref[...].reshape(cells, channels)
    write_stack(cot, stack_ref, band, step)
    pre_ref[...] = (slope_ref[...] * convolved_back(stack_ref, weight_ref, band, cells)).astype(BF16)
    half, upper = channels // 2, cells // 2
    for core, field in enumerate((pre_ref[...], cot)):
        field = field.astype(F32)
        for x in range(2):
            part = field[:, x * half : (x + 1) * half]
            part = jnp.concatenate([part[:upper], part[upper:]], axis=1).astype(BF16)
            for y in range(2):
                send_ref[y * 4 + x * 2 + core] = part


def outer_kernel(band, step, source_ref, cot_ref, hidden_ref, pre_ref, one_ref, two_ref, out_ref, stack_ref):
    cells, channels = hidden_ref.shape
    shape = (out_ref.shape[0],) + out_ref.shape[2:]
    write_stack(hidden_ref[...], stack_ref, band, step)
    second = convolved(stack_ref, two_ref, band, cells)
    source = source_ref[...].reshape(cells, channels)
    out_ref[:, 0] = (source.astype(F32) + second).astype(BF16).reshape(shape)
    write_stack(pre_ref[...], stack_ref, band, step)
    back = convolved_back(stack_ref, one_ref, band, cells)
    cot = cot_ref[...].reshape(cells, channels)
    out_ref[:, 1] = (cot.astype(F32) + back).astype(BF16).reshape(shape)


def units(deep):
    count = deep // 16
    for unit in range(9 * count):
        yield unit // count, (unit % count) * 16, (unit // 4) * 16, unit % 4


def grads_kernel(band, step, left_ref, right_ref, send_ref, turned_ref, moved_ref, sums_ref):
    sources, half, cells = left_ref.shape
    upper = cells // 2
    place = lax.broadcasted_iota(jnp.int32, (half, cells), 1) % band
    for at in range(sources):
        columns = slice(at * cells, (at + 1) * cells)
        field = left_ref[at]
        wide = field.astype(F32)
        turned_ref[0:half, columns] = jnp.where(place >= step, pltpu.roll(wide, step, 1), 0.0).astype(BF16)
        turned_ref[half : 2 * half, columns] = field
        turned_ref[2 * half :, columns] = jnp.where(
            place < band - step, pltpu.roll(wide, cells - step, 1), 0.0
        ).astype(BF16)
        packed = right_ref[at].astype(F32)
        grad = jnp.concatenate([packed[:, :half], packed[:, half:]], axis=0).astype(BF16)
        begin = at * cells
        moved_ref[1, begin : begin + cells, :] = grad
        moved_ref[2, begin + band : begin + cells, :] = grad[: cells - band]
        moved_ref[2, begin : begin + band, :] = grad[cells - band :]
        moved_ref[0, begin : begin + cells - band, :] = grad[band:]
        moved_ref[0, begin + cells - band : begin + cells, :] = grad[:band]
    for b in range(3):
        sums_ref[b] = jnp.dot(turned_ref[...], moved_ref[b], preferred_element_type=F32)
    deep, quarter = half // 4, half // 2
    height = send_ref.shape[1]
    for z in range(4):
        for core in range(2):
            blocks = [[] for _ in range(height // 16)]
            for tap, row, to, _ in units(deep):
                begin = (tap // 3) * half + z * deep + row
                blocks[to // 16].append(
                    sums_ref[tap % 3, begin : begin + 16, core * quarter : (core + 1) * quarter]
                )
            for to, parts in enumerate(blocks):
                while len(parts) < 4:
                    parts.append(jnp.zeros((16, quarter), F32))
                send_ref[z * 2 + core, to * 16 : (to + 1) * 16, :] = jnp.concatenate(parts, axis=1).astype(BF16)


def finish_kernel(scale, parts_ref, one_ref, two_ref):
    deep, quarter = one_ref.shape[2:]
    for core, out_ref in enumerate((one_ref, two_ref)):
        total = parts_ref[core].astype(F32)
        for z in range(1, parts_ref.shape[0] // 2):
            total = total + parts_ref[z * 2 + core].astype(F32)
        total = total * scale
        for tap, row, begin, slot in units(deep):
            out_ref[tap // 3, tap % 3, row : row + 16, :] = total[
                begin : begin + 16, slot * quarter : (slot + 1) * quarter
            ]


def fast_local(inputs, conv1_weight, conv2_weight, cotangent):
    rows, width, channels = inputs.shape
    every, plane, line = ("z", "y", "x", "core"), ("y", "x", "core"), ("z", "core")
    devices = lax.axis_size(every)
    step = width // devices
    cells = rows * width
    lat = lax.axis_size("x") * lax.axis_size("core")
    lon = devices // lat
    band = rows * lat * step
    half, deep = channels // 2, channels // lon
    height = -(-9 * (deep // 16) // 4) * 16
    scale = (rows * lat * width * lon) ** (-0.5)
    field = jax.ShapeDtypeStruct((cells, channels), BF16)
    stack = pltpu.VMEM((cells + 2 * band, 3 * channels), BF16)
    flops = 2 * 9 * cells * channels * channels

    def kernel(body, arguments, out_shape, scratch_shapes, work, megabytes):
        return pl.pallas_call(
            body,
            out_shape=out_shape,
            in_specs=[pl.BlockSpec(memory_space=pltpu.VMEM)] * len(arguments),
            out_specs=jax.tree.map(lambda _: pl.BlockSpec(memory_space=pltpu.VMEM), out_shape),
            scratch_shapes=scratch_shapes,
            compiler_params=pltpu.CompilerParams(vmem_limit_bytes=40 * 2**20),
            cost_estimate=pl.CostEstimate(flops=work, bytes_accessed=megabytes * 2**20, transcendentals=0),
        )(*arguments)

    def dealt(block):
        block = block.reshape(rows, devices, step, channels).transpose(1, 0, 2, 3)
        return lax.all_to_all(block.reshape(devices, rows * step, channels), every, 0, 0, tiled=True)

    source, cot = dealt(inputs), dealt(cotangent)
    hidden, slope, left = kernel(
        functools.partial(forward_kernel, band, step),
        (source, conv1_weight),
        (field, jax.ShapeDtypeStruct((cells, channels), F32), jax.ShapeDtypeStruct((8, half, cells), BF16)),
        [stack, pltpu.VMEM((cells, channels), F32)],
        flops,
        8,
    )
    left = lax.all_to_all(left, plane, 0, 0, tiled=True)
    pre_grad, right = kernel(
        functools.partial(backward_kernel, band, step),
        (cot, slope, conv2_weight),
        (field, jax.ShapeDtypeStruct((8, cells // 2, channels), BF16)),
        [stack],
        flops,
        8,
    )
    right = lax.all_to_all(right, plane, 0, 0, tiled=True)
    fields = kernel(
        functools.partial(outer_kernel, band, step),
        (source, cot, hidden, pre_grad, conv1_weight, conv2_weight),
        jax.ShapeDtypeStruct((devices, 2, rows * step, channels), BF16),
        [stack],
        2 * flops,
        9,
    )
    fields = lax.all_to_all(fields, every, 0, 0, tiled=True)
    fields = fields.reshape(devices, 2, rows, step, channels).transpose(1, 2, 0, 3, 4)
    output, input_grad = fields.reshape(2, rows, width, channels)

    terms = kernel(
        functools.partial(grads_kernel, band, step),
        (left, right),
        jax.ShapeDtypeStruct((8, height, channels), BF16),
        [
            pltpu.VMEM((3 * half, 8 * cells), BF16),
            pltpu.VMEM((3, 8 * cells, half), BF16),
            pltpu.VMEM((3, 3 * half, half), F32),
        ],
        2 * flops,
        6,
    )
    terms = lax.all_to_all(terms, line, 0, 0, tiled=True)
    grad = jax.ShapeDtypeStruct((3, 3, deep, half // 2), F32)
    conv1_grad, conv2_grad = kernel(
        functools.partial(finish_kernel, scale), (terms,), (grad, grad), [], 10**6, 2
    )
    return (output, input_grad, conv1_grad, conv2_grad)


def is_fast(mesh):
    return dict(mesh.shape) == {"lon": 8, "lat": 4}


def solution(mesh):
    body, lon, lat = local, "lon", "lat"
    if is_fast(mesh):
        lon, lat = ("z", "y"), ("x", "core")
        mesh = jax.sharding.Mesh(mesh.devices.reshape(4, 2, 2, 2), lon + lat)
        body = fast_local
    field, grad = P(lat, lon, None), P(None, None, lon, lat)
    return jax.shard_map(
        body,
        mesh=mesh,
        in_specs=(field, P(), P(), field),
        out_specs=(field, field, grad, grad),
        check_vma=False,
    )
```

```python
import functools

import jax
import jax.numpy as jnp
from jax import lax
from jax.experimental import pallas as pl
from jax.experimental.pallas import tpu as pltpu
from jax.sharding import PartitionSpec as P

F32, BF16 = jnp.float32, jnp.bfloat16


def passed_along(shard, axis, by):
    length = lax.axis_size(axis)
    return lax.ppermute(shard, axis, [(i, (i + by) % length) for i in range(length)])


def padded(shard, sides, width):
    for axis, dim in sides:
        size, length = (lax.axis_size(axis), shard.shape[dim])
        up = [(i, (i + 1) % size) for i in range(size - 1)]
        down = [(j, i) for i, j in up]
        last = lax.slice_in_dim(shard, length - width, length, axis=dim)
        initial = lax.slice_in_dim(shard, 0, width, axis=dim)
        before = lax.ppermute(last, axis, up)
        after = lax.ppermute(initial, axis, down)
        shard = jnp.concatenate([before, shard, after], axis=dim)
    return shard


def extend(field):
    western = passed_along(field, "lon", 1)
    eastern = passed_along(field, "lon", -1)
    widened = jnp.concatenate([western, field, eastern], axis=1)
    return padded(widened, (("lat", 0),), 1)


def windows(padded_field, count_of_rows, lon_width, channels, direction):
    pieces = []
    for lat_step in (-1, 0, 1):
        for longitude_stride in (-1, 0, 1):
            row_start = 1 + direction * lat_step
            column_begin = lon_width + direction * lon_width * longitude_stride
            pieces.append(
                padded_field[
                    row_start : row_start + count_of_rows, column_begin : column_begin + lon_width
                ]
            )
    stacked = jnp.concatenate(pieces, axis=2)
    return stacked.reshape(count_of_rows * lon_width, 9 * channels)


def full_terms(stacked, grad, scale, channels):
    product = lax.dot_general(
        stacked, grad, (((0,), (0,)), ((), ())), preferred_element_type=jnp.float32
    )
    return (product * scale).reshape(9, channels, channels)


def local(inputs, conv1_weight, conv2_weight, cotangent):
    count_of_rows, lon_width, channels = inputs.shape
    cells = count_of_rows * lon_width
    lon_count = lax.axis_size("lon")
    latitude_count = lax.axis_size("lat")
    scale = (count_of_rows * latitude_count * lon_width * lon_count) ** (-0.5)
    forward_one = conv1_weight.reshape(9 * channels, channels)
    forward_two = conv2_weight.reshape(9 * channels, channels)
    turned_one = jnp.swapaxes(conv1_weight, 2, 3).reshape(9 * channels, channels)
    turned_two = jnp.swapaxes(conv2_weight, 2, 3).reshape(9 * channels, channels)
    source_field, cot_field = (inputs, cotangent)

    def stack_of(field, direction):
        return windows(extend(field), count_of_rows, lon_width, channels, direction)

    def as_field(flat):
        return flat.reshape(count_of_rows, lon_width, channels)

    stack_input = stack_of(source_field, 1)
    first = jnp.dot(stack_input, forward_one, preferred_element_type=jnp.float32)
    cdf = 0.5 * (1.0 + jax.scipy.special.erf(first / jnp.sqrt(2.0)))
    hidden = (first * cdf).astype(jnp.bfloat16)
    stack_hidden = stack_of(as_field(hidden), 1)
    second = jnp.dot(stack_hidden, forward_two, preferred_element_type=jnp.float32)
    flat_input = source_field.reshape(cells, channels)
    output = (flat_input.astype(jnp.float32) + second).astype(jnp.bfloat16)
    flat_cot = cot_field.reshape(cells, channels)
    stacked_cotangent = stack_of(cot_field, -1)
    upstream = jnp.dot(stacked_cotangent, turned_two, preferred_element_type=jnp.float32)
    density = jnp.exp(-0.5 * first * first) / jnp.sqrt(2.0 * jnp.pi)
    pre_grad = (upstream * (cdf + first * density)).astype(jnp.bfloat16)
    stack_pre = stack_of(as_field(pre_grad), -1)
    back = jnp.dot(stack_pre, turned_one, preferred_element_type=jnp.float32)
    input_grad = (flat_cot.astype(jnp.float32) + back).astype(jnp.bfloat16)
    output = output.reshape(count_of_rows, lon_width, channels)
    input_grad = input_grad.reshape(count_of_rows, lon_width, channels)
    in_part = channels // lon_count
    out_part = channels // latitude_count
    terms_one = full_terms(stack_input, pre_grad, scale, channels)
    terms_two = full_terms(stack_hidden, flat_cot, scale, channels)
    partly = (
        lax.psum_scatter(terms_one, "lon", scatter_dimension=1, tiled=True),
        lax.psum_scatter(terms_two, "lon", scatter_dimension=1, tiled=True),
    )
    grad_one, grad_two = (
        lax.psum_scatter(partly[0], "lat", scatter_dimension=2, tiled=True),
        lax.psum_scatter(partly[1], "lat", scatter_dimension=2, tiled=True),
    )
    conv1_grad = grad_one.reshape(3, 3, in_part, out_part)
    conv2_grad = grad_two.reshape(3, 3, in_part, out_part)
    return (output, input_grad, conv1_grad, conv2_grad)


def write_stack(field, stack_ref, band, step):
    cells, channels = field.shape
    wide = field.astype(F32)
    place = lax.broadcasted_iota(jnp.int32, (cells, channels), 0) % band
    above = jnp.where(place >= step, pltpu.roll(wide, step, 0), 0.0).astype(BF16)
    below = jnp.where(place < band - step, pltpu.roll(wide, cells - step, 0), 0.0).astype(BF16)
    for at, part in enumerate((above, field, below)):
        columns = slice(at * channels, (at + 1) * channels)
        stack_ref[band : band + cells, columns] = part
        stack_ref[0:band, columns] = part[cells - band :]
        stack_ref[band + cells :, columns] = part[0:band]


def convolved(stack_ref, weight_ref, band, cells):
    total = None
    for b in range(3):
        channels = weight_ref.shape[2]
        tap = weight_ref[:, b].reshape(3 * channels, channels)
        term = jnp.dot(stack_ref[b * band : b * band + cells, :], tap, preferred_element_type=F32)
        total = term if total is None else total + term
    return total


def convolved_back(stack_ref, weight_ref, band, cells):
    total = None
    for b in range(3):
        tap = jnp.concatenate([weight_ref[2 - a, 2 - b] for a in range(3)], axis=1)
        term = lax.dot_general(
            stack_ref[b * band : b * band + cells, :],
            tap,
            (((1,), (1,)), ((), ())),
            preferred_element_type=F32,
        )
        total = term if total is None else total + term
    return total


def one_hot_rows(cells, step, devices, back):
    to = lax.broadcasted_iota(jnp.int32, (cells, cells), 1 if back else 0)
    source = lax.broadcasted_iota(jnp.int32, (cells, cells), 0 if back else 1)
    rows = cells // (devices * step)
    device, row, column = to // (rows * step), (to // step) % rows, to % step
    return (source == (row * devices + device) * step + column).astype(BF16)


def deal_kernel(step, inputs_ref, cot_ref, out_ref):
    devices, _, rows, channels = out_ref.shape
    cells = devices * rows
    chosen = one_hot_rows(cells, step, devices, False)
    for at, ref in enumerate((inputs_ref, cot_ref)):
        field = ref[...].reshape(cells, channels)
        dealt = jnp.dot(chosen, field, preferred_element_type=F32).astype(BF16)
        out_ref[:, at] = dealt.reshape(devices, rows, channels)


def gather_kernel(step, fields_ref, output_ref, grad_ref):
    devices, _, rows, channels = fields_ref.shape
    cells = devices * rows
    chosen = one_hot_rows(cells, step, devices, True)
    for at, ref in enumerate((output_ref, grad_ref)):
        field = fields_ref[:, at].reshape(cells, channels)
        ref[...] = jnp.dot(chosen, field, preferred_element_type=F32).astype(BF16).reshape(ref.shape)


def fetched(pairs, sems):
    copies = [pltpu.make_async_copy(source, to, sems.at[at]) for at, (source, to) in enumerate(pairs)]
    for copy in copies:
        copy.start()
    return copies


def inner_kernel(band, step, place_ref, own_ref, one_ref, two_ref,
                 hidden_ref, pre_ref, kept_ref, pair_ref, x_same_ref, x_cross_ref, y_same_ref, y_cross_ref,
                 source_ref, cot_ref, one_held, two_held, stack_ref, first_ref, slope_ref, turned_ref, sems):
    x, y, core = place_ref[0], place_ref[1], place_ref[2]
    cells, channels = first_ref.shape
    copies = fetched(
        ((own_ref.at[:, 0], source_ref), (one_ref, one_held), (own_ref.at[:, 1], cot_ref), (two_ref, two_held)), sems
    )
    half, rows = channels // 2, 32
    deep = half // 4

    def turn(at, field):
        turned = field.T
        for h in range(2):
            for z in range(4):
                begin = (2 * z + h) * deep if at < 2 else h * half + z * deep
                turned_ref[at * 2 + h, z * deep : (z + 1) * deep, :] = turned[begin : begin + deep]

    copies[0].wait()
    source = source_ref[...].reshape(cells, channels)
    write_stack(source, stack_ref, band, step)
    copies[1].wait()
    first_ref[...] = convolved(stack_ref, one_held, band, cells)
    turn(0, source)

    def activate(at, carry):
        span = pl.ds(pl.multiple_of(at * rows, rows), rows)
        first = first_ref[span, :]
        cdf = 0.5 * (1.0 + lax.erf(first * (0.5**0.5)))
        density = jnp.exp(-0.5 * first * first) * ((2.0 * jnp.pi) ** -0.5)
        hidden_ref[span, :] = (first * cdf).astype(BF16)
        slope_ref[span, :] = cdf + first * density
        return carry

    lax.fori_loop(0, cells // rows, activate, 0)
    turn(1, hidden_ref[...])
    copies[2].wait()
    cot = cot_ref[...].reshape(cells, channels)
    write_stack(cot, stack_ref, band, step)
    turn(3, cot)
    copies[3].wait()
    pre_ref[...] = (slope_ref[...] * convolved_back(stack_ref, two_held, band, cells)).astype(BF16)
    turn(2, pre_ref[...])

    def left(of, h):
        return turned_ref[of * 2 + h]

    def right(of, h):
        return turned_ref[4 + of * 2 + h]

    other = 1 - core
    kept_ref[0], kept_ref[1] = left(core, y), right(core, x)
    pair_ref[0], pair_ref[1] = left(other, y), right(other, x)
    x_same_ref[0], x_same_ref[1] = left(core, y), right(core, 1 - x)
    x_cross_ref[0], x_cross_ref[1] = left(other, y), right(other, 1 - x)
    y_same_ref[0], y_same_ref[1] = left(core, 1 - y), right(core, x)
    y_cross_ref[0], y_cross_ref[1] = left(other, 1 - y), right(other, x)


def outer_kernel(band, step, own_ref, hidden_ref, pre_ref, one_ref, two_ref, out_ref,
                 own_held, hidden_held, pre_held, one_held, two_held, stack_ref, sems):
    cells, channels = hidden_ref.shape
    shape = (out_ref.shape[0],) + out_ref.shape[2:]
    copies = fetched(
        ((hidden_ref, hidden_held), (two_ref, two_held), (own_ref, own_held), (pre_ref, pre_held), (one_ref, one_held)),
        sems,
    )
    copies[0].wait()
    write_stack(hidden_held[...], stack_ref, band, step)
    copies[1].wait()
    second = convolved(stack_ref, two_held, band, cells)
    copies[2].wait()
    source = own_held[:, 0].reshape(cells, channels)
    out_ref[:, 0] = (source.astype(F32) + second).astype(BF16).reshape(shape)
    copies[3].wait()
    write_stack(pre_held[...], stack_ref, band, step)
    copies[4].wait()
    back = convolved_back(stack_ref, one_held, band, cells)
    cot = own_held[:, 1].reshape(cells, channels)
    out_ref[:, 1] = (cot.astype(F32) + back).astype(BF16).reshape(shape)


def units(deep):
    count = deep // 16
    for unit in range(9 * count):
        yield unit // count, (unit % count) * 16, (unit // 4) * 16, unit % 4


def grads_kernel(band, step, *refs):
    pieces, (send_ref, turned_ref, moved_ref, sums_ref) = refs[:-4], refs[-4:]
    kept_ref, pair_ref, x_same_ref, x_cross_ref, y_same_ref, y_cross_ref = pieces[:6]
    x_far_same, x_far_cross, y_far_same, y_far_cross = pieces[6:]
    lefts = [ref.at[0] for ref in pieces[:6]] + [x_far_same, x_far_cross]
    rights = [ref.at[1] for ref in pieces[:6]] + [y_far_same, y_far_cross]
    half, cells = x_far_same.shape
    place = lax.broadcasted_iota(jnp.int32, (half, cells), 1) % band
    for at, (left_ref, right_ref) in enumerate(zip(lefts, rights)):
        columns = slice(at * cells, (at + 1) * cells)
        field = left_ref[...]
        wide = field.astype(F32)
        turned_ref[0:half, columns] = jnp.where(place >= step, pltpu.roll(wide, step, 1), 0.0).astype(BF16)
        turned_ref[half : 2 * half, columns] = field
        turned_ref[2 * half :, columns] = jnp.where(
            place < band - step, pltpu.roll(wide, cells - step, 1), 0.0
        ).astype(BF16)
        grad = right_ref[...]
        wide = grad.astype(F32)
        moved_ref[0, :, columns] = pltpu.roll(wide, cells - band, 1).astype(BF16)
        moved_ref[1, :, columns] = grad
        moved_ref[2, :, columns] = pltpu.roll(wide, band, 1).astype(BF16)
    for b in range(3):
        sums_ref[b] = lax.dot_general(
            turned_ref[...], moved_ref[b], (((1,), (1,)), ((), ())), preferred_element_type=F32
        )
    deep, quarter = half // 4, half // 2
    height = send_ref.shape[1]
    for z in range(4):
        for core in range(2):
            blocks = [[] for _ in range(height // 16)]
            for tap, row, to, _ in units(deep):
                begin = (tap // 3) * half + z * deep + row
                blocks[to // 16].append(
                    sums_ref[tap % 3, begin : begin + 16, core * quarter : (core + 1) * quarter]
                )
            for to, parts in enumerate(blocks):
                while len(parts) < 4:
                    parts.append(jnp.zeros((16, quarter), F32))
                send_ref[z * 2 + core, to * 16 : (to + 1) * 16, :] = jnp.concatenate(parts, axis=1).astype(BF16)


def finish_kernel(scale, parts_ref, one_ref, two_ref):
    deep, quarter = one_ref.shape[2:]
    for core, out_ref in enumerate((one_ref, two_ref)):
        total = parts_ref[core].astype(F32)
        for z in range(1, parts_ref.shape[0] // 2):
            total = total + parts_ref[z * 2 + core].astype(F32)
        total = total * scale
        for tap, row, begin, slot in units(deep):
            out_ref[tap // 3, tap % 3, row : row + 16, :] = total[
                begin : begin + 16, slot * quarter : (slot + 1) * quarter
            ]


def fast_local(inputs, conv1_weight, conv2_weight, cotangent):
    rows, width, channels = inputs.shape
    every, line = ("z", "y", "x", "core"), ("z", "core")
    devices = lax.axis_size(every)
    step = width // devices
    cells = rows * width
    lat = lax.axis_size("x") * lax.axis_size("core")
    lon = devices // lat
    band = rows * lat * step
    half, deep = channels // 2, channels // lon
    height = -(-9 * (deep // 16) // 4) * 16
    scale = (rows * lat * width * lon) ** (-0.5)
    flops = 2 * 9 * cells * channels * channels
    vmem, hbm, smem = (pl.BlockSpec(memory_space=space) for space in (pltpu.VMEM, pl.ANY, pltpu.SMEM))

    def held(*shape, kind=BF16):
        return pltpu.VMEM(shape, kind)

    def shaped(*shape, kind=BF16):
        return jax.ShapeDtypeStruct(shape, kind)

    def kernel(body, specs, arguments, out_shape, scratch_shapes, work, megabytes):
        return pl.pallas_call(
            body,
            out_shape=out_shape,
            in_specs=specs,
            out_specs=jax.tree.map(lambda _: vmem, out_shape),
            scratch_shapes=scratch_shapes,
            compiler_params=pltpu.CompilerParams(vmem_limit_bytes=40 * 2**20),
            cost_estimate=pl.CostEstimate(flops=work, bytes_accessed=megabytes * 2**20, transcendentals=0),
        )(*arguments)

    def passed(piece, x, y, core):
        pairs = [(i, i ^ (4 * y + 2 * x + core)) for i in range(8)]
        return lax.ppermute(piece, ("y", "x", "core"), pairs)

    stack = held(cells + 2 * band, 3 * channels)
    weights = held(*conv1_weight.shape)
    dealt = shaped(devices, 2, rows * step, channels)
    own = kernel(functools.partial(deal_kernel, step), [vmem] * 2, (inputs, cotangent), dealt, [], 10**9, 3)
    own = lax.all_to_all(own, every, 0, 0, tiled=True)
    place = jnp.stack([lax.axis_index("x"), lax.axis_index("y"), lax.axis_index("core")]).astype(jnp.int32)
    piece = shaped(2, half, cells)
    hidden, pre_grad, kept, pair, x_same, x_cross, y_same, y_cross = kernel(
        functools.partial(inner_kernel, band, step),
        [smem] + [hbm] * 3,
        (place, own, conv1_weight, conv2_weight),
        (shaped(cells, channels),) * 2 + (piece,) * 6,
        [
            held(devices, rows * step, channels),
            held(devices, rows * step, channels),
            weights,
            weights,
            stack,
            held(cells, channels, kind=F32),
            held(cells, channels, kind=F32),
            held(8, half, cells),
            pltpu.SemaphoreType.DMA((4,)),
        ],
        2 * flops,
        10,
    )
    y_same, x_same = passed(y_same, 0, 1, 0), passed(x_same, 1, 0, 0)
    y_cross, x_cross = passed(y_cross, 0, 1, 1), passed(x_cross, 1, 0, 1)
    pair = passed(pair, 0, 0, 1)
    far = (
        passed(y_same[0], 1, 0, 0),
        passed(y_cross[0], 1, 0, 0),
        passed(x_same[1], 0, 1, 0),
        passed(x_cross[1], 0, 1, 0),
    )
    fields = kernel(
        functools.partial(outer_kernel, band, step),
        [hbm] * 5,
        (own, hidden, pre_grad, conv1_weight, conv2_weight),
        dealt,
        [
            held(devices, 2, rows * step, channels),
            held(cells, channels),
            held(cells, channels),
            weights,
            weights,
            stack,
            pltpu.SemaphoreType.DMA((5,)),
        ],
        2 * flops,
        9,
    )
    fields = lax.all_to_all(fields, every, 0, 0, tiled=True)
    output, input_grad = kernel(
        functools.partial(gather_kernel, step), [vmem], (fields,), (shaped(*inputs.shape),) * 2, [], 10**9, 3
    )
    terms = kernel(
        functools.partial(grads_kernel, band, step),
        [vmem] * 10,
        (kept, pair, x_same, x_cross, y_same, y_cross) + far,
        shaped(8, height, channels),
        [held(3 * half, 8 * cells), held(3, half, 8 * cells), held(3, 3 * half, half, kind=F32)],
        2 * flops,
        6,
    )
    terms = lax.all_to_all(terms, line, 0, 0, tiled=True)
    grad = shaped(3, 3, deep, half // 2, kind=F32)
    conv1_grad, conv2_grad = kernel(
        functools.partial(finish_kernel, scale), [vmem], (terms,), (grad, grad), [], 10**6, 2
    )
    return (output, input_grad, conv1_grad, conv2_grad)


def is_fast(mesh):
    return dict(mesh.shape) == {"lon": 8, "lat": 4}


def solution(mesh):
    body, lon, lat = local, "lon", "lat"
    if is_fast(mesh):
        lon, lat = ("z", "y"), ("x", "core")
        mesh = jax.sharding.Mesh(mesh.devices.reshape(4, 2, 2, 2), lon + lat)
        body = fast_local
    field, grad = P(lat, lon, None), P(None, None, lon, lat)
    return jax.shard_map(
        body,
        mesh=mesh,
        in_specs=(field, P(), P(), field),
        out_specs=(field, field, grad, grad),
        check_vma=False,
    )
```

```python
import functools

import jax
import jax.numpy as jnp
from jax import lax
from jax.experimental import pallas as pl
from jax.experimental.pallas import tpu as pltpu
from jax.sharding import PartitionSpec as P

F32, BF16 = jnp.float32, jnp.bfloat16


def passed_along(shard, axis, by):
    length = lax.axis_size(axis)
    return lax.ppermute(shard, axis, [(i, (i + by) % length) for i in range(length)])


def padded(shard, sides, width):
    for axis, dim in sides:
        size, length = (lax.axis_size(axis), shard.shape[dim])
        up = [(i, (i + 1) % size) for i in range(size - 1)]
        down = [(j, i) for i, j in up]
        last = lax.slice_in_dim(shard, length - width, length, axis=dim)
        initial = lax.slice_in_dim(shard, 0, width, axis=dim)
        before = lax.ppermute(last, axis, up)
        after = lax.ppermute(initial, axis, down)
        shard = jnp.concatenate([before, shard, after], axis=dim)
    return shard


def extend(field):
    western = passed_along(field, "lon", 1)
    eastern = passed_along(field, "lon", -1)
    widened = jnp.concatenate([western, field, eastern], axis=1)
    return padded(widened, (("lat", 0),), 1)


def windows(padded_field, count_of_rows, lon_width, channels, direction):
    pieces = []
    for lat_step in (-1, 0, 1):
        for longitude_stride in (-1, 0, 1):
            row_start = 1 + direction * lat_step
            column_begin = lon_width + direction * lon_width * longitude_stride
            pieces.append(
                padded_field[
                    row_start : row_start + count_of_rows, column_begin : column_begin + lon_width
                ]
            )
    stacked = jnp.concatenate(pieces, axis=2)
    return stacked.reshape(count_of_rows * lon_width, 9 * channels)


def full_terms(stacked, grad, scale, channels):
    product = lax.dot_general(
        stacked, grad, (((0,), (0,)), ((), ())), preferred_element_type=jnp.float32
    )
    return (product * scale).reshape(9, channels, channels)


def local(inputs, conv1_weight, conv2_weight, cotangent):
    count_of_rows, lon_width, channels = inputs.shape
    cells = count_of_rows * lon_width
    lon_count = lax.axis_size("lon")
    latitude_count = lax.axis_size("lat")
    scale = (count_of_rows * latitude_count * lon_width * lon_count) ** (-0.5)
    forward_one = conv1_weight.reshape(9 * channels, channels)
    forward_two = conv2_weight.reshape(9 * channels, channels)
    turned_one = jnp.swapaxes(conv1_weight, 2, 3).reshape(9 * channels, channels)
    turned_two = jnp.swapaxes(conv2_weight, 2, 3).reshape(9 * channels, channels)
    source_field, cot_field = (inputs, cotangent)

    def stack_of(field, direction):
        return windows(extend(field), count_of_rows, lon_width, channels, direction)

    def as_field(flat):
        return flat.reshape(count_of_rows, lon_width, channels)

    stack_input = stack_of(source_field, 1)
    first = jnp.dot(stack_input, forward_one, preferred_element_type=jnp.float32)
    cdf = 0.5 * (1.0 + jax.scipy.special.erf(first / jnp.sqrt(2.0)))
    hidden = (first * cdf).astype(jnp.bfloat16)
    stack_hidden = stack_of(as_field(hidden), 1)
    second = jnp.dot(stack_hidden, forward_two, preferred_element_type=jnp.float32)
    flat_input = source_field.reshape(cells, channels)
    output = (flat_input.astype(jnp.float32) + second).astype(jnp.bfloat16)
    flat_cot = cot_field.reshape(cells, channels)
    stacked_cotangent = stack_of(cot_field, -1)
    upstream = jnp.dot(stacked_cotangent, turned_two, preferred_element_type=jnp.float32)
    density = jnp.exp(-0.5 * first * first) / jnp.sqrt(2.0 * jnp.pi)
    pre_grad = (upstream * (cdf + first * density)).astype(jnp.bfloat16)
    stack_pre = stack_of(as_field(pre_grad), -1)
    back = jnp.dot(stack_pre, turned_one, preferred_element_type=jnp.float32)
    input_grad = (flat_cot.astype(jnp.float32) + back).astype(jnp.bfloat16)
    output = output.reshape(count_of_rows, lon_width, channels)
    input_grad = input_grad.reshape(count_of_rows, lon_width, channels)
    in_part = channels // lon_count
    out_part = channels // latitude_count
    terms_one = full_terms(stack_input, pre_grad, scale, channels)
    terms_two = full_terms(stack_hidden, flat_cot, scale, channels)
    partly = (
        lax.psum_scatter(terms_one, "lon", scatter_dimension=1, tiled=True),
        lax.psum_scatter(terms_two, "lon", scatter_dimension=1, tiled=True),
    )
    grad_one, grad_two = (
        lax.psum_scatter(partly[0], "lat", scatter_dimension=2, tiled=True),
        lax.psum_scatter(partly[1], "lat", scatter_dimension=2, tiled=True),
    )
    conv1_grad = grad_one.reshape(3, 3, in_part, out_part)
    conv2_grad = grad_two.reshape(3, 3, in_part, out_part)
    return (output, input_grad, conv1_grad, conv2_grad)


def write_stack(field, stack_ref, band, step):
    cells, channels = field.shape
    wide = field.astype(F32)
    place = lax.broadcasted_iota(jnp.int32, (cells, channels), 0) % band
    above = jnp.where(place >= step, pltpu.roll(wide, step, 0), 0.0).astype(BF16)
    below = jnp.where(place < band - step, pltpu.roll(wide, cells - step, 0), 0.0).astype(BF16)
    for at, part in enumerate((above, field, below)):
        columns = slice(at * channels, (at + 1) * channels)
        stack_ref[band : band + cells, columns] = part
        stack_ref[0:band, columns] = part[cells - band :]
        stack_ref[band + cells :, columns] = part[0:band]


def convolved(stack_ref, weight_ref, band, cells):
    total = None
    for b in range(3):
        channels = weight_ref.shape[2]
        tap = weight_ref[:, b].reshape(3 * channels, channels)
        term = jnp.dot(stack_ref[b * band : b * band + cells, :], tap, preferred_element_type=F32)
        total = term if total is None else total + term
    return total


def convolved_back(stack_ref, weight_ref, band, cells):
    total = None
    for b in range(3):
        tap = jnp.concatenate([weight_ref[2 - a, 2 - b] for a in range(3)], axis=1)
        term = lax.dot_general(
            stack_ref[b * band : b * band + cells, :],
            tap,
            (((1,), (1,)), ((), ())),
            preferred_element_type=F32,
        )
        total = term if total is None else total + term
    return total


def one_hot_rows(cells, step, devices, back):
    to = lax.broadcasted_iota(jnp.int32, (cells, cells), 1 if back else 0)
    source = lax.broadcasted_iota(jnp.int32, (cells, cells), 0 if back else 1)
    rows = cells // (devices * step)
    device, row, column = to // (rows * step), (to // step) % rows, to % step
    return (source == (row * devices + device) * step + column).astype(BF16)


def deal_kernel(step, inputs_ref, cot_ref, out_ref, held_ref, sems):
    devices, _, rows, channels = out_ref.shape
    cells = devices * rows
    copies = fetched(((inputs_ref, held_ref.at[0]), (cot_ref, held_ref.at[1])), sems)
    chosen = one_hot_rows(cells, step, devices, False)
    for at, copy in enumerate(copies):
        copy.wait()
        field = held_ref[at].reshape(cells, channels)
        dealt = jnp.dot(chosen, field, preferred_element_type=F32).astype(BF16)
        out_ref[:, at] = dealt.reshape(devices, rows, channels)


def gather_kernel(step, fields_ref, output_ref, grad_ref):
    devices, _, rows, channels = fields_ref.shape
    cells = devices * rows
    chosen = one_hot_rows(cells, step, devices, True)
    for at, ref in enumerate((output_ref, grad_ref)):
        field = fields_ref[:, at].reshape(cells, channels)
        ref[...] = jnp.dot(chosen, field, preferred_element_type=F32).astype(BF16).reshape(ref.shape)


def fetched(pairs, sems):
    copies = [pltpu.make_async_copy(source, to, sems.at[at]) for at, (source, to) in enumerate(pairs)]
    for copy in copies:
        copy.start()
    return copies


def inner_kernel(band, step, place_ref, own_ref, one_ref, two_ref,
                 hidden_ref, pre_ref, kept_ref, pair_ref, x_same_ref, x_cross_ref, y_same_ref, y_cross_ref,
                 two_held, stack_ref, first_ref, slope_ref, turned_ref, sems, out_sems):
    x, y, core = place_ref[0], place_ref[1], place_ref[2]
    other = 1 - core
    cells, channels = first_ref.shape
    fetch = fetched(((two_ref, two_held),), sems)[0]
    half, rows = channels // 2, 32
    deep = half // 4

    def turn(at, field):
        turned = field.T
        for h in range(2):
            for z in range(4):
                begin = (2 * z + h) * deep if at < 2 else h * half + z * deep
                turned_ref[at * 2 + h, z * deep : (z + 1) * deep, :] = turned[begin : begin + deep]

    def sent(side, wanted):
        pairs = [(turned_ref.at[4 * side + of * 2 + h], ref.at[side]) for ref, of, h in wanted]
        return fetched(pairs, out_sems.at[side])

    source = own_ref[:, 0].reshape(cells, channels)
    write_stack(source, stack_ref, band, step)
    first_ref[...] = convolved(stack_ref, one_ref, band, cells)
    turn(0, source)

    def activate(at, carry):
        span = pl.ds(pl.multiple_of(at * rows, rows), rows)
        first = first_ref[span, :]
        cdf = 0.5 * (1.0 + lax.erf(first * (0.5**0.5)))
        density = jnp.exp(-0.5 * first * first) * ((2.0 * jnp.pi) ** -0.5)
        hidden_ref[span, :] = (first * cdf).astype(BF16)
        slope_ref[span, :] = cdf + first * density
        return carry

    lax.fori_loop(0, cells // rows, activate, 0)
    turn(1, hidden_ref[...])
    copies = sent(0, (
        (y_same_ref, core, 1 - y), (y_cross_ref, other, 1 - y), (x_same_ref, core, y),
        (x_cross_ref, other, y), (pair_ref, other, y), (kept_ref, core, y),
    ))
    cot = own_ref[:, 1].reshape(cells, channels)
    write_stack(cot, stack_ref, band, step)
    turn(3, cot)
    fetch.wait()
    pre_ref[...] = (slope_ref[...] * convolved_back(stack_ref, two_held, band, cells)).astype(BF16)
    turn(2, pre_ref[...])
    copies += sent(1, (
        (y_same_ref, core, x), (y_cross_ref, other, x), (x_same_ref, core, 1 - x),
        (x_cross_ref, other, 1 - x), (pair_ref, other, x), (kept_ref, core, x),
    ))
    for copy in copies:
        copy.wait()


def outer_kernel(band, step, own_ref, hidden_ref, pre_ref, one_ref, two_ref, out_ref,
                 one_held, two_held, stack_ref, sems):
    cells, channels = hidden_ref.shape
    shape = (out_ref.shape[0],) + out_ref.shape[2:]
    copies = fetched(((two_ref, two_held), (one_ref, one_held)), sems)
    write_stack(hidden_ref[...], stack_ref, band, step)
    copies[0].wait()
    second = convolved(stack_ref, two_held, band, cells)
    source = own_ref[:, 0].reshape(cells, channels)
    out_ref[:, 0] = (source.astype(F32) + second).astype(BF16).reshape(shape)
    write_stack(pre_ref[...], stack_ref, band, step)
    copies[1].wait()
    back = convolved_back(stack_ref, one_held, band, cells)
    cot = own_ref[:, 1].reshape(cells, channels)
    out_ref[:, 1] = (cot.astype(F32) + back).astype(BF16).reshape(shape)


def units(deep):
    count = deep // 16
    for unit in range(9 * count):
        yield unit // count, (unit % count) * 16, (unit // 4) * 16, unit % 4


def summed(band, step, lefts, rights, turned_ref, moved_ref, b):
    half, cells = lefts[0].shape
    if b == 0:
        place = lax.broadcasted_iota(jnp.int32, (half, cells), 1) % band
        for at, (left_ref, right_ref) in enumerate(zip(lefts, rights)):
            columns = slice(at * cells, (at + 1) * cells)
            field = left_ref[...]
            wide = field.astype(F32)
            turned_ref[0:half, columns] = jnp.where(place >= step, pltpu.roll(wide, step, 1), 0.0).astype(BF16)
            turned_ref[half : 2 * half, columns] = field
            turned_ref[2 * half :, columns] = jnp.where(
                place < band - step, pltpu.roll(wide, cells - step, 1), 0.0
            ).astype(BF16)
            grad = right_ref[...]
            wide = grad.astype(F32)
            moved_ref[0, :, columns] = pltpu.roll(wide, cells - band, 1).astype(BF16)
            moved_ref[1, :, columns] = grad
            moved_ref[2, :, columns] = pltpu.roll(wide, band, 1).astype(BF16)
    return lax.dot_general(turned_ref[...], moved_ref[b], (((1,), (1,)), ((), ())), preferred_element_type=F32)


def near_kernel(band, step, *refs):
    pieces, (sums_ref, turned_ref, moved_ref) = refs[:-3], refs[-3:]
    lefts, rights = ([ref.at[side] for ref in pieces] for side in range(2))
    for b in range(3):
        sums_ref[b] = summed(band, step, lefts, rights, turned_ref, moved_ref, b)


def far_kernel(band, step, near_ref, *refs):
    pieces, (send_ref, turned_ref, moved_ref, sums_ref) = refs[:-4], refs[-4:]
    half, cells = pieces[0].shape
    for b in range(3):
        sums_ref[b] = near_ref[b] + summed(band, step, pieces[:2], pieces[2:], turned_ref, moved_ref, b)
    deep, quarter = half // 4, half // 2
    height = send_ref.shape[1]
    for z in range(4):
        for core in range(2):
            blocks = [[] for _ in range(height // 16)]
            for tap, row, to, _ in units(deep):
                begin = (tap // 3) * half + z * deep + row
                blocks[to // 16].append(
                    sums_ref[tap % 3, begin : begin + 16, core * quarter : (core + 1) * quarter]
                )
            for to, parts in enumerate(blocks):
                while len(parts) < 4:
                    parts.append(jnp.zeros((16, quarter), F32))
                send_ref[z * 2 + core, to * 16 : (to + 1) * 16, :] = jnp.concatenate(parts, axis=1).astype(BF16)


def finish_kernel(scale, parts_ref, one_ref, two_ref):
    deep, quarter = one_ref.shape[2:]
    for core, out_ref in enumerate((one_ref, two_ref)):
        total = parts_ref[core].astype(F32)
        for z in range(1, parts_ref.shape[0] // 2):
            total = total + parts_ref[z * 2 + core].astype(F32)
        total = total * scale
        for tap, row, begin, slot in units(deep):
            out_ref[tap // 3, tap % 3, row : row + 16, :] = total[
                begin : begin + 16, slot * quarter : (slot + 1) * quarter
            ]


def fast_local(inputs, conv1_weight, conv2_weight, cotangent):
    rows, width, channels = inputs.shape
    every, line = ("z", "y", "x", "core"), ("z", "core")
    devices = lax.axis_size(every)
    step = width // devices
    cells = rows * width
    lat = lax.axis_size("x") * lax.axis_size("core")
    lon = devices // lat
    band = rows * lat * step
    half, deep = channels // 2, channels // lon
    height = -(-9 * (deep // 16) // 4) * 16
    scale = (rows * lat * width * lon) ** (-0.5)
    flops = 2 * 9 * cells * channels * channels
    vmem, hbm, smem = (pl.BlockSpec(memory_space=space) for space in (pltpu.VMEM, pltpu.HBM, pltpu.SMEM))

    def held(*shape, kind=BF16):
        return pltpu.VMEM(shape, kind)

    def shaped(*shape, kind=BF16):
        return jax.ShapeDtypeStruct(shape, kind)

    def kernel(body, specs, arguments, out_shape, scratch_shapes, work, megabytes, out_specs=None):
        return pl.pallas_call(
            body,
            out_shape=out_shape,
            in_specs=specs,
            out_specs=out_specs or jax.tree.map(lambda _: vmem, out_shape),
            scratch_shapes=scratch_shapes,
            compiler_params=pltpu.CompilerParams(vmem_limit_bytes=28 * 2**20),
            cost_estimate=pl.CostEstimate(flops=work, bytes_accessed=megabytes * 2**20, transcendentals=0),
        )(*arguments)

    def passed(piece, x, y, core):
        pairs = [(i, i ^ (4 * y + 2 * x + core)) for i in range(8)]
        return lax.ppermute(piece, ("y", "x", "core"), pairs)

    stack = held(cells + 2 * band, 3 * channels)
    weights = held(*conv1_weight.shape)
    dealt = shaped(devices, 2, rows * step, channels)
    own = kernel(
        functools.partial(deal_kernel, step),
        [hbm] * 2,
        (inputs, cotangent),
        dealt,
        [held(2, *inputs.shape), pltpu.SemaphoreType.DMA((2,))],
        10**9,
        3,
    )
    own = lax.all_to_all(own, every, 0, 0, tiled=True)
    place = jnp.stack([lax.axis_index("x"), lax.axis_index("y"), lax.axis_index("core")]).astype(jnp.int32)
    piece = shaped(2, half, cells)
    hidden, pre_grad, kept, pair, x_same, x_cross, y_same, y_cross = kernel(
        functools.partial(inner_kernel, band, step),
        [smem, vmem, vmem, hbm],
        (place, own, conv1_weight, conv2_weight),
        (shaped(cells, channels),) * 2 + (piece,) * 6,
        [
            weights,
            stack,
            held(cells, channels, kind=F32),
            held(cells, channels, kind=F32),
            held(8, half, cells),
            pltpu.SemaphoreType.DMA((1,)),
            pltpu.SemaphoreType.DMA((2, 6)),
        ],
        2 * flops,
        10,
        (vmem,) * 2 + (hbm,) * 6,
    )
    y_same, x_same = passed(y_same, 0, 1, 0), passed(x_same, 1, 0, 0)
    y_cross, x_cross = passed(y_cross, 0, 1, 1), passed(x_cross, 1, 0, 1)
    pair = passed(pair, 0, 0, 1)
    far = (
        passed(y_same[0], 1, 0, 0),
        passed(y_cross[0], 1, 0, 0),
        passed(x_same[1], 0, 1, 0),
        passed(x_cross[1], 0, 1, 0),
    )
    fields = kernel(
        functools.partial(outer_kernel, band, step),
        [vmem] * 3 + [hbm] * 2,
        (own, hidden, pre_grad, conv1_weight, conv2_weight),
        dealt,
        [weights, weights, stack, pltpu.SemaphoreType.DMA((2,))],
        2 * flops,
        9,
    )
    fields = lax.all_to_all(fields, every, 0, 0, tiled=True)
    output, input_grad = kernel(
        functools.partial(gather_kernel, step), [vmem], (fields,), (shaped(*inputs.shape),) * 2, [], 10**9, 3
    )
    sums = shaped(3, 3 * half, half, kind=F32)
    near = kernel(
        functools.partial(near_kernel, band, step),
        [vmem] * 6,
        (kept, pair, x_same, x_cross, y_same, y_cross),
        sums,
        [held(3 * half, 6 * cells), held(3, half, 6 * cells)],
        2 * flops,
        6,
    )
    terms = kernel(
        functools.partial(far_kernel, band, step),
        [vmem] * 5,
        (near,) + far,
        shaped(8, height, channels),
        [held(3 * half, 2 * cells), held(3, half, 2 * cells), held(*sums.shape, kind=F32)],
        flops,
        4,
    )
    terms = lax.all_to_all(terms, line, 0, 0, tiled=True)
    grad = shaped(3, 3, deep, half // 2, kind=F32)
    conv1_grad, conv2_grad = kernel(
        functools.partial(finish_kernel, scale), [vmem], (terms,), (grad, grad), [], 10**6, 2
    )
    return (output, input_grad, conv1_grad, conv2_grad)


def is_fast(mesh):
    return dict(mesh.shape) == {"lon": 8, "lat": 4}


def solution(mesh):
    body, lon, lat = local, "lon", "lat"
    if is_fast(mesh):
        lon, lat = ("z", "y"), ("x", "core")
        mesh = jax.sharding.Mesh(mesh.devices.reshape(4, 2, 2, 2), lon + lat)
        body = fast_local
    field, grad = P(lat, lon, None), P(None, None, lon, lat)
    return jax.shard_map(
        body,
        mesh=mesh,
        in_specs=(field, P(), P(), field),
        out_specs=(field, field, grad, grad),
        check_vma=False,
    )
```

```python
import functools

import jax
import jax.numpy as jnp
from jax import lax
from jax.experimental import pallas as pl
from jax.experimental.pallas import tpu as pltpu
from jax.sharding import PartitionSpec as P

F32, BF16 = jnp.float32, jnp.bfloat16


def passed_along(shard, axis, by):
    length = lax.axis_size(axis)
    return lax.ppermute(shard, axis, [(i, (i + by) % length) for i in range(length)])


def padded(shard, sides, width):
    for axis, dim in sides:
        size, length = (lax.axis_size(axis), shard.shape[dim])
        up = [(i, (i + 1) % size) for i in range(size - 1)]
        down = [(j, i) for i, j in up]
        last = lax.slice_in_dim(shard, length - width, length, axis=dim)
        initial = lax.slice_in_dim(shard, 0, width, axis=dim)
        before = lax.ppermute(last, axis, up)
        after = lax.ppermute(initial, axis, down)
        shard = jnp.concatenate([before, shard, after], axis=dim)
    return shard


def extend(field):
    western = passed_along(field, "lon", 1)
    eastern = passed_along(field, "lon", -1)
    widened = jnp.concatenate([western, field, eastern], axis=1)
    return padded(widened, (("lat", 0),), 1)


def windows(padded_field, count_of_rows, lon_width, channels, direction):
    pieces = []
    for lat_step in (-1, 0, 1):
        for longitude_stride in (-1, 0, 1):
            row_start = 1 + direction * lat_step
            column_begin = lon_width + direction * lon_width * longitude_stride
            pieces.append(
                padded_field[
                    row_start : row_start + count_of_rows, column_begin : column_begin + lon_width
                ]
            )
    stacked = jnp.concatenate(pieces, axis=2)
    return stacked.reshape(count_of_rows * lon_width, 9 * channels)


def full_terms(stacked, grad, scale, channels):
    product = lax.dot_general(
        stacked, grad, (((0,), (0,)), ((), ())), preferred_element_type=jnp.float32
    )
    return (product * scale).reshape(9, channels, channels)


def local(inputs, conv1_weight, conv2_weight, cotangent):
    count_of_rows, lon_width, channels = inputs.shape
    cells = count_of_rows * lon_width
    lon_count = lax.axis_size("lon")
    latitude_count = lax.axis_size("lat")
    scale = (count_of_rows * latitude_count * lon_width * lon_count) ** (-0.5)
    forward_one = conv1_weight.reshape(9 * channels, channels)
    forward_two = conv2_weight.reshape(9 * channels, channels)
    turned_one = jnp.swapaxes(conv1_weight, 2, 3).reshape(9 * channels, channels)
    turned_two = jnp.swapaxes(conv2_weight, 2, 3).reshape(9 * channels, channels)
    source_field, cot_field = (inputs, cotangent)

    def stack_of(field, direction):
        return windows(extend(field), count_of_rows, lon_width, channels, direction)

    def as_field(flat):
        return flat.reshape(count_of_rows, lon_width, channels)

    stack_input = stack_of(source_field, 1)
    first = jnp.dot(stack_input, forward_one, preferred_element_type=jnp.float32)
    cdf = 0.5 * (1.0 + jax.scipy.special.erf(first / jnp.sqrt(2.0)))
    hidden = (first * cdf).astype(jnp.bfloat16)
    stack_hidden = stack_of(as_field(hidden), 1)
    second = jnp.dot(stack_hidden, forward_two, preferred_element_type=jnp.float32)
    flat_input = source_field.reshape(cells, channels)
    output = (flat_input.astype(jnp.float32) + second).astype(jnp.bfloat16)
    flat_cot = cot_field.reshape(cells, channels)
    stacked_cotangent = stack_of(cot_field, -1)
    upstream = jnp.dot(stacked_cotangent, turned_two, preferred_element_type=jnp.float32)
    density = jnp.exp(-0.5 * first * first) / jnp.sqrt(2.0 * jnp.pi)
    pre_grad = (upstream * (cdf + first * density)).astype(jnp.bfloat16)
    stack_pre = stack_of(as_field(pre_grad), -1)
    back = jnp.dot(stack_pre, turned_one, preferred_element_type=jnp.float32)
    input_grad = (flat_cot.astype(jnp.float32) + back).astype(jnp.bfloat16)
    output = output.reshape(count_of_rows, lon_width, channels)
    input_grad = input_grad.reshape(count_of_rows, lon_width, channels)
    in_part = channels // lon_count
    out_part = channels // latitude_count
    terms_one = full_terms(stack_input, pre_grad, scale, channels)
    terms_two = full_terms(stack_hidden, flat_cot, scale, channels)
    partly = (
        lax.psum_scatter(terms_one, "lon", scatter_dimension=1, tiled=True),
        lax.psum_scatter(terms_two, "lon", scatter_dimension=1, tiled=True),
    )
    grad_one, grad_two = (
        lax.psum_scatter(partly[0], "lat", scatter_dimension=2, tiled=True),
        lax.psum_scatter(partly[1], "lat", scatter_dimension=2, tiled=True),
    )
    conv1_grad = grad_one.reshape(3, 3, in_part, out_part)
    conv2_grad = grad_two.reshape(3, 3, in_part, out_part)
    return (output, input_grad, conv1_grad, conv2_grad)


def write_stack(field, stack_ref, band, step):
    cells, channels = field.shape
    wide = field.astype(F32)
    place = lax.broadcasted_iota(jnp.int32, (cells, channels), 0) % band
    above = jnp.where(place >= step, pltpu.roll(wide, step, 0), 0.0).astype(BF16)
    below = jnp.where(place < band - step, pltpu.roll(wide, cells - step, 0), 0.0).astype(BF16)
    for at, part in enumerate((above, field, below)):
        columns = slice(at * channels, (at + 1) * channels)
        stack_ref[band : band + cells, columns] = part
        stack_ref[0:band, columns] = part[cells - band :]
        stack_ref[band + cells :, columns] = part[0:band]


def convolved(stack_ref, weight_ref, band, cells):
    total = None
    for b in range(3):
        channels = weight_ref.shape[2]
        tap = weight_ref[:, b].reshape(3 * channels, channels)
        term = jnp.dot(stack_ref[b * band : b * band + cells, :], tap, preferred_element_type=F32)
        total = term if total is None else total + term
    return total


def convolved_back(stack_ref, weight_ref, band, cells):
    total = None
    for b in range(3):
        tap = jnp.concatenate([weight_ref[2 - a, 2 - b] for a in range(3)], axis=1)
        term = lax.dot_general(
            stack_ref[b * band : b * band + cells, :],
            tap,
            (((1,), (1,)), ((), ())),
            preferred_element_type=F32,
        )
        total = term if total is None else total + term
    return total


def one_hot_rows(cells, step, devices, back):
    to = lax.broadcasted_iota(jnp.int32, (cells, cells), 1 if back else 0)
    source = lax.broadcasted_iota(jnp.int32, (cells, cells), 0 if back else 1)
    rows = cells // (devices * step)
    device, row, column = to // (rows * step), (to // step) % rows, to % step
    return (source == (row * devices + device) * step + column).astype(BF16)


def deal_kernel(step, inputs_ref, cot_ref, out_ref, held_ref, sems):
    devices, _, rows, channels = out_ref.shape
    cells = devices * rows
    copies = fetched(((inputs_ref, held_ref.at[0]), (cot_ref, held_ref.at[1])), sems)
    chosen = one_hot_rows(cells, step, devices, False)
    for at, copy in enumerate(copies):
        copy.wait()
        field = held_ref[at].reshape(cells, channels)
        dealt = jnp.dot(chosen, field, preferred_element_type=F32).astype(BF16)
        out_ref[:, at] = dealt.reshape(devices, rows, channels)


def gather_kernel(step, fields_ref, output_ref, grad_ref):
    devices, _, rows, channels = fields_ref.shape
    cells = devices * rows
    chosen = one_hot_rows(cells, step, devices, True)
    for at, ref in enumerate((output_ref, grad_ref)):
        field = fields_ref[:, at].reshape(cells, channels)
        ref[...] = jnp.dot(chosen, field, preferred_element_type=F32).astype(BF16).reshape(ref.shape)


def fetched(pairs, sems):
    copies = [pltpu.make_async_copy(source, to, sems.at[at]) for at, (source, to) in enumerate(pairs)]
    for copy in copies:
        copy.start()
    return copies


def inner_kernel(band, step, place_ref, own_ref, one_ref, two_ref,
                 hidden_ref, pre_ref, kept_ref, pair_ref, x_same_ref, x_cross_ref, y_same_ref, y_cross_ref,
                 two_held, stack_ref, first_ref, slope_ref, turned_ref, sems, out_sems):
    x, y, core = place_ref[0], place_ref[1], place_ref[2]
    other = 1 - core
    cells, channels = first_ref.shape
    fetch = fetched(((two_ref, two_held),), sems)[0]
    half, rows = channels // 2, 32
    deep = half // 4

    def turn(at, field):
        turned = field.T
        for h in range(2):
            for z in range(4):
                begin = (2 * z + h) * deep if at < 2 else h * half + z * deep
                turned_ref[at * 2 + h, z * deep : (z + 1) * deep, :] = turned[begin : begin + deep]

    def sent(side, wanted):
        pairs = [(turned_ref.at[4 * side + of * 2 + h], ref.at[side]) for ref, of, h in wanted]
        return fetched(pairs, out_sems.at[side])

    source = own_ref[:, 0].reshape(cells, channels)
    write_stack(source, stack_ref, band, step)
    first_ref[...] = convolved(stack_ref, one_ref, band, cells)
    turn(0, source)

    def activate(at, carry):
        span = pl.ds(pl.multiple_of(at * rows, rows), rows)
        first = first_ref[span, :]
        cdf = 0.5 * (1.0 + lax.erf(first * (0.5**0.5)))
        density = jnp.exp(-0.5 * first * first) * ((2.0 * jnp.pi) ** -0.5)
        hidden_ref[span, :] = (first * cdf).astype(BF16)
        slope_ref[span, :] = cdf + first * density
        return carry

    lax.fori_loop(0, cells // rows, activate, 0)
    turn(1, hidden_ref[...])
    copies = sent(0, (
        (y_same_ref, core, 1 - y), (y_cross_ref, other, 1 - y), (x_same_ref, core, y),
        (x_cross_ref, other, y), (pair_ref, other, y), (kept_ref, core, y),
    ))
    cot = own_ref[:, 1].reshape(cells, channels)
    write_stack(cot, stack_ref, band, step)
    turn(3, cot)
    fetch.wait()
    pre_ref[...] = (slope_ref[...] * convolved_back(stack_ref, two_held, band, cells)).astype(BF16)
    turn(2, pre_ref[...])
    copies += sent(1, (
        (y_same_ref, core, x), (y_cross_ref, other, x), (x_same_ref, core, 1 - x),
        (x_cross_ref, other, 1 - x), (pair_ref, other, x), (kept_ref, core, x),
    ))
    for copy in copies:
        copy.wait()


def outer_kernel(band, step, own_ref, hidden_ref, pre_ref, one_ref, two_ref, out_ref,
                 one_held, two_held, stack_ref, sems):
    cells, channels = hidden_ref.shape
    shape = (out_ref.shape[0],) + out_ref.shape[2:]
    copies = fetched(((two_ref, two_held), (one_ref, one_held)), sems)
    write_stack(hidden_ref[...], stack_ref, band, step)
    copies[0].wait()
    second = convolved(stack_ref, two_held, band, cells)
    source = own_ref[:, 0].reshape(cells, channels)
    out_ref[:, 0] = (source.astype(F32) + second).astype(BF16).reshape(shape)
    write_stack(pre_ref[...], stack_ref, band, step)
    copies[1].wait()
    back = convolved_back(stack_ref, one_held, band, cells)
    cot = own_ref[:, 1].reshape(cells, channels)
    out_ref[:, 1] = (cot.astype(F32) + back).astype(BF16).reshape(shape)


def units(deep):
    count = deep // 16
    for unit in range(9 * count):
        yield unit // count, (unit % count) * 16, (unit // 4) * 16, unit % 4


def summed(band, step, lefts, rights, turned_ref, moved_ref, b):
    half, cells = lefts[0].shape
    if b == 0:
        place = lax.broadcasted_iota(jnp.int32, (half, cells), 1) % band
        for at, (left_ref, right_ref) in enumerate(zip(lefts, rights)):
            columns = slice(at * cells, (at + 1) * cells)
            field = left_ref[...]
            wide = field.astype(F32)
            turned_ref[0:half, columns] = jnp.where(place >= step, pltpu.roll(wide, step, 1), 0.0).astype(BF16)
            turned_ref[half : 2 * half, columns] = field
            turned_ref[2 * half :, columns] = jnp.where(
                place < band - step, pltpu.roll(wide, cells - step, 1), 0.0
            ).astype(BF16)
            grad = right_ref[...]
            wide = grad.astype(F32)
            moved_ref[0, :, columns] = pltpu.roll(wide, cells - band, 1).astype(BF16)
            moved_ref[1, :, columns] = grad
            moved_ref[2, :, columns] = pltpu.roll(wide, band, 1).astype(BF16)
    return lax.dot_general(turned_ref[...], moved_ref[b], (((1,), (1,)), ((), ())), preferred_element_type=F32)


def near_kernel(band, step, *refs):
    pieces, (sums_ref, turned_ref, moved_ref) = refs[:-3], refs[-3:]
    lefts, rights = ([ref.at[side] for ref in pieces] for side in range(2))
    for b in range(3):
        sums_ref[b] = summed(band, step, lefts, rights, turned_ref, moved_ref, b)


def far_kernel(band, step, near_ref, *refs):
    pieces, (send_ref, turned_ref, moved_ref, sums_ref) = refs[:-4], refs[-4:]
    half, cells = pieces[0].shape
    for b in range(3):
        sums_ref[b] = near_ref[b] + summed(band, step, pieces[:2], pieces[2:], turned_ref, moved_ref, b)
    deep, quarter = half // 4, half // 2
    height = send_ref.shape[1]
    for z in range(4):
        for core in range(2):
            blocks = [[] for _ in range(height // 16)]
            for tap, row, to, _ in units(deep):
                begin = (tap // 3) * half + z * deep + row
                blocks[to // 16].append(
                    sums_ref[tap % 3, begin : begin + 16, core * quarter : (core + 1) * quarter]
                )
            for to, parts in enumerate(blocks):
                while len(parts) < 4:
                    parts.append(jnp.zeros((16, quarter), F32))
                send_ref[z * 2 + core, to * 16 : (to + 1) * 16, :] = jnp.concatenate(parts, axis=1).astype(BF16)


def finish_kernel(scale, parts_ref, one_ref, two_ref):
    deep, quarter = one_ref.shape[2:]
    for core, out_ref in enumerate((one_ref, two_ref)):
        total = parts_ref[core].astype(F32)
        for z in range(1, parts_ref.shape[0] // 2):
            total = total + parts_ref[z * 2 + core].astype(F32)
        total = total * scale
        for tap, row, begin, slot in units(deep):
            out_ref[tap // 3, tap % 3, row : row + 16, :] = total[
                begin : begin + 16, slot * quarter : (slot + 1) * quarter
            ]


def fast_local(inputs, conv1_weight, conv2_weight, cotangent):
    rows, width, channels = inputs.shape
    every, line = ("z", "y", "x", "core"), ("z", "core")
    devices = lax.axis_size(every)
    step = width // devices
    cells = rows * width
    lat = lax.axis_size("x") * lax.axis_size("core")
    lon = devices // lat
    band = rows * lat * step
    half, deep = channels // 2, channels // lon
    height = -(-9 * (deep // 16) // 4) * 16
    scale = (rows * lat * width * lon) ** (-0.5)
    flops = 2 * 9 * cells * channels * channels
    vmem, hbm, smem = (pl.BlockSpec(memory_space=space) for space in (pltpu.VMEM, pltpu.HBM, pltpu.SMEM))

    def held(*shape, kind=BF16):
        return pltpu.VMEM(shape, kind)

    def shaped(*shape, kind=BF16):
        return jax.ShapeDtypeStruct(shape, kind)

    def kernel(body, specs, arguments, out_shape, scratch_shapes, work, megabytes, out_specs=None):
        return pl.pallas_call(
            body,
            out_shape=out_shape,
            in_specs=specs,
            out_specs=out_specs or jax.tree.map(lambda _: vmem, out_shape),
            scratch_shapes=scratch_shapes,
            compiler_params=pltpu.CompilerParams(vmem_limit_bytes=20 * 2**20),
            cost_estimate=pl.CostEstimate(flops=work, bytes_accessed=megabytes * 2**20, transcendentals=0),
        )(*arguments)

    def passed(piece, x, y, core):
        pairs = [(i, i ^ (4 * y + 2 * x + core)) for i in range(8)]
        return lax.ppermute(piece, ("y", "x", "core"), pairs)

    stack = held(cells + 2 * band, 3 * channels)
    weights = held(*conv1_weight.shape)
    dealt = shaped(devices, 2, rows * step, channels)
    own = kernel(
        functools.partial(deal_kernel, step),
        [hbm] * 2,
        [pltpu.with_memory_space_constraint(field, pltpu.HBM) for field in (inputs, cotangent)],
        dealt,
        [held(2, *inputs.shape), pltpu.SemaphoreType.DMA((2,))],
        10**9,
        3,
    )
    own = lax.all_to_all(own, every, 0, 0, tiled=True)
    place = jnp.stack([lax.axis_index("x"), lax.axis_index("y"), lax.axis_index("core")]).astype(jnp.int32)
    piece = pltpu.HBM((2, half, cells), BF16)
    one_far, two_far = (pltpu.with_memory_space_constraint(w, pltpu.HBM) for w in (conv1_weight, conv2_weight))
    hidden, pre_grad, kept, pair, x_same, x_cross, y_same, y_cross = kernel(
        functools.partial(inner_kernel, band, step),
        [smem, vmem, vmem, hbm],
        (place, own, conv1_weight, two_far),
        (shaped(cells, channels),) * 2 + (piece,) * 6,
        [
            weights,
            stack,
            held(cells, channels, kind=F32),
            held(cells, channels, kind=F32),
            held(8, half, cells),
            pltpu.SemaphoreType.DMA((1,)),
            pltpu.SemaphoreType.DMA((2, 6)),
        ],
        2 * flops,
        10,
        (vmem,) * 2 + (hbm,) * 6,
    )
    y_same, x_same = passed(y_same, 0, 1, 0), passed(x_same, 1, 0, 0)
    y_cross, x_cross = passed(y_cross, 0, 1, 1), passed(x_cross, 1, 0, 1)
    pair = passed(pair, 0, 0, 1)
    far = (
        passed(y_same[0], 1, 0, 0),
        passed(y_cross[0], 1, 0, 0),
        passed(x_same[1], 0, 1, 0),
        passed(x_cross[1], 0, 1, 0),
    )
    fields = kernel(
        functools.partial(outer_kernel, band, step),
        [vmem] * 3 + [hbm] * 2,
        (own, hidden, pre_grad, one_far, two_far),
        dealt,
        [weights, weights, stack, pltpu.SemaphoreType.DMA((2,))],
        2 * flops,
        9,
    )
    fields = lax.all_to_all(fields, every, 0, 0, tiled=True)
    output, input_grad = kernel(
        functools.partial(gather_kernel, step), [vmem], (fields,), (shaped(*inputs.shape),) * 2, [], 10**9, 3
    )
    sums = shaped(3, 3 * half, half, kind=F32)
    near = kernel(
        functools.partial(near_kernel, band, step),
        [vmem] * 6,
        (kept, pair, x_same, x_cross, y_same, y_cross),
        sums,
        [held(3 * half, 6 * cells), held(3, half, 6 * cells)],
        2 * flops,
        6,
    )
    terms = kernel(
        functools.partial(far_kernel, band, step),
        [vmem] * 5,
        (near,) + far,
        shaped(8, height, channels),
        [held(3 * half, 2 * cells), held(3, half, 2 * cells), held(*sums.shape, kind=F32)],
        flops,
        4,
    )
    terms = lax.all_to_all(terms, line, 0, 0, tiled=True)
    grad = shaped(3, 3, deep, half // 2, kind=F32)
    conv1_grad, conv2_grad = kernel(
        functools.partial(finish_kernel, scale), [vmem], (terms,), (grad, grad), [], 10**6, 2
    )
    return (output, input_grad, conv1_grad, conv2_grad)


def is_fast(mesh):
    return dict(mesh.shape) == {"lon": 8, "lat": 4}


def solution(mesh):
    body, lon, lat = local, "lon", "lat"
    if is_fast(mesh):
        lon, lat = ("z", "y"), ("x", "core")
        mesh = jax.sharding.Mesh(mesh.devices.reshape(4, 2, 2, 2), lon + lat)
        body = fast_local
    field, grad = P(lat, lon, None), P(None, None, lon, lat)
    return jax.shard_map(
        body,
        mesh=mesh,
        in_specs=(field, P(), P(), field),
        out_specs=(field, field, grad, grad),
        check_vma=False,
    )
```

```python
import functools

import jax
import jax.numpy as jnp
from jax import lax
from jax.experimental import pallas as pl
from jax.experimental.pallas import tpu as pltpu
from jax.sharding import PartitionSpec as P

F32, BF16 = jnp.float32, jnp.bfloat16


def passed_along(shard, axis, by):
    length = lax.axis_size(axis)
    return lax.ppermute(shard, axis, [(i, (i + by) % length) for i in range(length)])


def padded(shard, sides, width):
    for axis, dim in sides:
        size, length = (lax.axis_size(axis), shard.shape[dim])
        up = [(i, (i + 1) % size) for i in range(size - 1)]
        down = [(j, i) for i, j in up]
        last = lax.slice_in_dim(shard, length - width, length, axis=dim)
        initial = lax.slice_in_dim(shard, 0, width, axis=dim)
        before = lax.ppermute(last, axis, up)
        after = lax.ppermute(initial, axis, down)
        shard = jnp.concatenate([before, shard, after], axis=dim)
    return shard


def extend(field):
    western = passed_along(field, "lon", 1)
    eastern = passed_along(field, "lon", -1)
    widened = jnp.concatenate([western, field, eastern], axis=1)
    return padded(widened, (("lat", 0),), 1)


def windows(padded_field, count_of_rows, lon_width, channels, direction):
    pieces = []
    for lat_step in (-1, 0, 1):
        for longitude_stride in (-1, 0, 1):
            row_start = 1 + direction * lat_step
            column_begin = lon_width + direction * lon_width * longitude_stride
            pieces.append(
                padded_field[
                    row_start : row_start + count_of_rows, column_begin : column_begin + lon_width
                ]
            )
    stacked = jnp.concatenate(pieces, axis=2)
    return stacked.reshape(count_of_rows * lon_width, 9 * channels)


def full_terms(stacked, grad, scale, channels):
    product = lax.dot_general(
        stacked, grad, (((0,), (0,)), ((), ())), preferred_element_type=jnp.float32
    )
    return (product * scale).reshape(9, channels, channels)


def local(inputs, conv1_weight, conv2_weight, cotangent):
    count_of_rows, lon_width, channels = inputs.shape
    cells = count_of_rows * lon_width
    lon_count = lax.axis_size("lon")
    latitude_count = lax.axis_size("lat")
    scale = (count_of_rows * latitude_count * lon_width * lon_count) ** (-0.5)
    forward_one = conv1_weight.reshape(9 * channels, channels)
    forward_two = conv2_weight.reshape(9 * channels, channels)
    turned_one = jnp.swapaxes(conv1_weight, 2, 3).reshape(9 * channels, channels)
    turned_two = jnp.swapaxes(conv2_weight, 2, 3).reshape(9 * channels, channels)
    source_field, cot_field = (inputs, cotangent)

    def stack_of(field, direction):
        return windows(extend(field), count_of_rows, lon_width, channels, direction)

    def as_field(flat):
        return flat.reshape(count_of_rows, lon_width, channels)

    stack_input = stack_of(source_field, 1)
    first = jnp.dot(stack_input, forward_one, preferred_element_type=jnp.float32)
    cdf = 0.5 * (1.0 + jax.scipy.special.erf(first / jnp.sqrt(2.0)))
    hidden = (first * cdf).astype(jnp.bfloat16)
    stack_hidden = stack_of(as_field(hidden), 1)
    second = jnp.dot(stack_hidden, forward_two, preferred_element_type=jnp.float32)
    flat_input = source_field.reshape(cells, channels)
    output = (flat_input.astype(jnp.float32) + second).astype(jnp.bfloat16)
    flat_cot = cot_field.reshape(cells, channels)
    stacked_cotangent = stack_of(cot_field, -1)
    upstream = jnp.dot(stacked_cotangent, turned_two, preferred_element_type=jnp.float32)
    density = jnp.exp(-0.5 * first * first) / jnp.sqrt(2.0 * jnp.pi)
    pre_grad = (upstream * (cdf + first * density)).astype(jnp.bfloat16)
    stack_pre = stack_of(as_field(pre_grad), -1)
    back = jnp.dot(stack_pre, turned_one, preferred_element_type=jnp.float32)
    input_grad = (flat_cot.astype(jnp.float32) + back).astype(jnp.bfloat16)
    output = output.reshape(count_of_rows, lon_width, channels)
    input_grad = input_grad.reshape(count_of_rows, lon_width, channels)
    in_part = channels // lon_count
    out_part = channels // latitude_count
    terms_one = full_terms(stack_input, pre_grad, scale, channels)
    terms_two = full_terms(stack_hidden, flat_cot, scale, channels)
    partly = (
        lax.psum_scatter(terms_one, "lon", scatter_dimension=1, tiled=True),
        lax.psum_scatter(terms_two, "lon", scatter_dimension=1, tiled=True),
    )
    grad_one, grad_two = (
        lax.psum_scatter(partly[0], "lat", scatter_dimension=2, tiled=True),
        lax.psum_scatter(partly[1], "lat", scatter_dimension=2, tiled=True),
    )
    conv1_grad = grad_one.reshape(3, 3, in_part, out_part)
    conv2_grad = grad_two.reshape(3, 3, in_part, out_part)
    return (output, input_grad, conv1_grad, conv2_grad)


def write_stack(field, stack_ref, band, step):
    cells, channels = field.shape
    wide = field.astype(F32)
    place = lax.broadcasted_iota(jnp.int32, (cells, channels), 0) % band
    above = jnp.where(place >= step, pltpu.roll(wide, step, 0), 0.0).astype(BF16)
    below = jnp.where(place < band - step, pltpu.roll(wide, cells - step, 0), 0.0).astype(BF16)
    for at, part in enumerate((above, field, below)):
        columns = slice(at * channels, (at + 1) * channels)
        stack_ref[band : band + cells, columns] = part
        stack_ref[0:band, columns] = part[cells - band :]
        stack_ref[band + cells :, columns] = part[0:band]


def convolved(stack_ref, weight_ref, band, cells):
    total = None
    for b in range(3):
        channels = weight_ref.shape[2]
        tap = weight_ref[:, b].reshape(3 * channels, channels)
        term = jnp.dot(stack_ref[b * band : b * band + cells, :], tap, preferred_element_type=F32)
        total = term if total is None else total + term
    return total


def convolved_back(stack_ref, weight_ref, band, cells):
    total = None
    for b in range(3):
        tap = jnp.concatenate([weight_ref[2 - a, 2 - b] for a in range(3)], axis=1)
        term = lax.dot_general(
            stack_ref[b * band : b * band + cells, :],
            tap,
            (((1,), (1,)), ((), ())),
            preferred_element_type=F32,
        )
        total = term if total is None else total + term
    return total


def one_hot_rows(cells, step, devices, back):
    to = lax.broadcasted_iota(jnp.int32, (cells, cells), 1 if back else 0)
    source = lax.broadcasted_iota(jnp.int32, (cells, cells), 0 if back else 1)
    rows = cells // (devices * step)
    device, row, column = to // (rows * step), (to // step) % rows, to % step
    return (source == (row * devices + device) * step + column).astype(BF16)


def deal_kernel(step, inputs_ref, cot_ref, out_ref, held_ref, sems):
    devices, _, rows, channels = out_ref.shape
    cells = devices * rows
    copies = fetched(((inputs_ref, held_ref.at[0]), (cot_ref, held_ref.at[1])), sems)
    chosen = one_hot_rows(cells, step, devices, False)
    for at, copy in enumerate(copies):
        copy.wait()
        field = held_ref[at].reshape(cells, channels)
        dealt = jnp.dot(chosen, field, preferred_element_type=F32).astype(BF16)
        out_ref[:, at] = dealt.reshape(devices, rows, channels)


def gather_kernel(step, fields_ref, output_ref, grad_ref):
    devices, _, rows, channels = fields_ref.shape
    cells = devices * rows
    chosen = one_hot_rows(cells, step, devices, True)
    for at, ref in enumerate((output_ref, grad_ref)):
        field = fields_ref[:, at].reshape(cells, channels)
        ref[...] = jnp.dot(chosen, field, preferred_element_type=F32).astype(BF16).reshape(ref.shape)


def fetched(pairs, sems):
    copies = [pltpu.make_async_copy(source, to, sems.at[at]) for at, (source, to) in enumerate(pairs)]
    for copy in copies:
        copy.start()
    return copies


def inner_kernel(band, step, place_ref, own_ref, one_ref, two_ref,
                 hidden_ref, pre_ref, kept_ref, pair_ref, x_same_ref, x_cross_ref, y_same_ref, y_cross_ref,
                 two_held, stack_ref, first_ref, slope_ref, turned_ref, sems, out_sems):
    x, y, core = place_ref[0], place_ref[1], place_ref[2]
    other = 1 - core
    cells, channels = first_ref.shape
    fetch = fetched(((two_ref, two_held),), sems)[0]
    half, rows = channels // 2, 32
    deep = half // 4

    def turn(at, field):
        turned = field.T
        for h in range(2):
            for z in range(4):
                begin = (2 * z + h) * deep if at < 2 else h * half + z * deep
                turned_ref[at * 2 + h, z * deep : (z + 1) * deep, :] = turned[begin : begin + deep]

    def sent(side, wanted):
        pairs = [(turned_ref.at[4 * side + of * 2 + h], ref.at[side]) for ref, of, h in wanted]
        return fetched(pairs, out_sems.at[side])

    source = own_ref[:, 0].reshape(cells, channels)
    write_stack(source, stack_ref, band, step)
    first_ref[...] = convolved(stack_ref, one_ref, band, cells)
    turn(0, source)

    def activate(at, carry):
        span = pl.ds(pl.multiple_of(at * rows, rows), rows)
        first = first_ref[span, :]
        cdf = 0.5 * (1.0 + lax.erf(first * (0.5**0.5)))
        density = jnp.exp(-0.5 * first * first) * ((2.0 * jnp.pi) ** -0.5)
        hidden_ref[span, :] = (first * cdf).astype(BF16)
        slope_ref[span, :] = cdf + first * density
        return carry

    lax.fori_loop(0, cells // rows, activate, 0)
    turn(1, hidden_ref[...])
    copies = sent(0, (
        (y_same_ref, core, 1 - y), (y_cross_ref, other, 1 - y), (x_same_ref, core, y),
        (x_cross_ref, other, y), (pair_ref, other, y), (kept_ref, core, y),
    ))
    cot = own_ref[:, 1].reshape(cells, channels)
    write_stack(cot, stack_ref, band, step)
    turn(3, cot)
    fetch.wait()
    pre_ref[...] = (slope_ref[...] * convolved_back(stack_ref, two_held, band, cells)).astype(BF16)
    turn(2, pre_ref[...])
    copies += sent(1, (
        (y_same_ref, core, x), (y_cross_ref, other, x), (x_same_ref, core, 1 - x),
        (x_cross_ref, other, 1 - x), (pair_ref, other, x), (kept_ref, core, x),
    ))
    for copy in copies:
        copy.wait()


def outer_kernel(band, step, own_ref, hidden_ref, pre_ref, one_ref, two_ref, out_ref,
                 one_held, two_held, stack_ref, sems):
    cells, channels = hidden_ref.shape
    shape = (out_ref.shape[0],) + out_ref.shape[2:]
    copies = fetched(((two_ref, two_held), (one_ref, one_held)), sems)
    write_stack(hidden_ref[...], stack_ref, band, step)
    copies[0].wait()
    second = convolved(stack_ref, two_held, band, cells)
    source = own_ref[:, 0].reshape(cells, channels)
    out_ref[:, 0] = (source.astype(F32) + second).astype(BF16).reshape(shape)
    write_stack(pre_ref[...], stack_ref, band, step)
    copies[1].wait()
    back = convolved_back(stack_ref, one_held, band, cells)
    cot = own_ref[:, 1].reshape(cells, channels)
    out_ref[:, 1] = (cot.astype(F32) + back).astype(BF16).reshape(shape)


def units(deep):
    count = deep // 16
    for unit in range(9 * count):
        yield unit // count, (unit % count) * 16, (unit // 4) * 16, unit % 4


def summed(band, step, lefts, rights, turned_ref, moved_ref, b):
    half, cells = lefts[0].shape
    if b == 0:
        place = lax.broadcasted_iota(jnp.int32, (half, cells), 1) % band
        for at, (left_ref, right_ref) in enumerate(zip(lefts, rights)):
            columns = slice(at * cells, (at + 1) * cells)
            field = left_ref[...]
            wide = field.astype(F32)
            turned_ref[0:half, columns] = jnp.where(place >= step, pltpu.roll(wide, step, 1), 0.0).astype(BF16)
            turned_ref[half : 2 * half, columns] = field
            turned_ref[2 * half :, columns] = jnp.where(
                place < band - step, pltpu.roll(wide, cells - step, 1), 0.0
            ).astype(BF16)
            grad = right_ref[...]
            wide = grad.astype(F32)
            moved_ref[0, :, columns] = pltpu.roll(wide, cells - band, 1).astype(BF16)
            moved_ref[1, :, columns] = grad
            moved_ref[2, :, columns] = pltpu.roll(wide, band, 1).astype(BF16)
    return lax.dot_general(turned_ref[...], moved_ref[b], (((1,), (1,)), ((), ())), preferred_element_type=F32)


def near_kernel(band, step, *refs):
    pieces, (sums_ref, turned_ref, moved_ref) = refs[:-3], refs[-3:]
    lefts, rights = ([ref.at[side] for ref in pieces] for side in range(2))
    for b in range(3):
        sums_ref[b] = summed(band, step, lefts, rights, turned_ref, moved_ref, b)


def far_kernel(band, step, place_ref, near_ref, *refs):
    pieces, out_refs, (turned_ref, moved_ref, sums_ref, send_ref, sems) = refs[:4], refs[4:-5], refs[-5:]
    me = place_ref[3] * 2 + place_ref[2]
    half, cells = pieces[0].shape
    for b in range(3):
        sums_ref[b] = near_ref[b] + summed(band, step, pieces[:2], pieces[2:], turned_ref, moved_ref, b)
    deep, quarter = half // 4, half // 2
    height = send_ref.shape[1]
    for z in range(4):
        for core in range(2):
            blocks = [[] for _ in range(height // 16)]
            for tap, row, to, _ in units(deep):
                begin = (tap // 3) * half + z * deep + row
                blocks[to // 16].append(
                    sums_ref[tap % 3, begin : begin + 16, core * quarter : (core + 1) * quarter]
                )
            for to, parts in enumerate(blocks):
                while len(parts) < 4:
                    parts.append(jnp.zeros((16, quarter), F32))
                send_ref[z * 2 + core, to * 16 : (to + 1) * 16, :] = jnp.concatenate(parts, axis=1).astype(BF16)
    pairs = [(send_ref.at[me ^ away], ref) for away, ref in enumerate(out_refs)]
    for copy in fetched(pairs, sems):
        copy.wait()


def finish_kernel(scale, place_ref, *refs):
    parts, (one_ref, two_ref) = refs[:-2], refs[-2:]
    core = place_ref[2]
    deep, quarter = one_ref.shape[2:]
    sums = []
    for other in range(2):
        total = parts[other][...].astype(F32)
        for ref in parts[other + 2 :: 2]:
            total = total + ref[...].astype(F32)
        sums.append(total * scale)
    ours, theirs = sums
    for out_ref, total in (
        (one_ref, jnp.where(core == 0, ours, theirs)),
        (two_ref, jnp.where(core == 0, theirs, ours)),
    ):
        for tap, row, begin, slot in units(deep):
            out_ref[tap // 3, tap % 3, row : row + 16, :] = total[
                begin : begin + 16, slot * quarter : (slot + 1) * quarter
            ]


def fast_local(inputs, conv1_weight, conv2_weight, cotangent):
    rows, width, channels = inputs.shape
    every = ("z", "y", "x", "core")
    devices = lax.axis_size(every)
    step = width // devices
    cells = rows * width
    lat = lax.axis_size("x") * lax.axis_size("core")
    lon = devices // lat
    band = rows * lat * step
    half, deep = channels // 2, channels // lon
    height = -(-9 * (deep // 16) // 4) * 16
    scale = (rows * lat * width * lon) ** (-0.5)
    flops = 2 * 9 * cells * channels * channels
    vmem, hbm, smem = (pl.BlockSpec(memory_space=space) for space in (pltpu.VMEM, pltpu.HBM, pltpu.SMEM))

    def held(*shape, kind=BF16):
        return pltpu.VMEM(shape, kind)

    def shaped(*shape, kind=BF16):
        return jax.ShapeDtypeStruct(shape, kind)

    def kernel(body, specs, arguments, out_shape, scratch_shapes, work, megabytes, out_specs=None):
        return pl.pallas_call(
            body,
            out_shape=out_shape,
            in_specs=specs,
            out_specs=out_specs or jax.tree.map(lambda _: vmem, out_shape),
            scratch_shapes=scratch_shapes,
            compiler_params=pltpu.CompilerParams(vmem_limit_bytes=20 * 2**20),
            cost_estimate=pl.CostEstimate(flops=work, bytes_accessed=megabytes * 2**20, transcendentals=0),
        )(*arguments)

    def passed(piece, x, y, core):
        pairs = [(i, i ^ (4 * y + 2 * x + core)) for i in range(8)]
        return lax.ppermute(piece, ("y", "x", "core"), pairs)

    stack = held(cells + 2 * band, 3 * channels)
    weights = held(*conv1_weight.shape)
    dealt = shaped(devices, 2, rows * step, channels)
    own = kernel(
        functools.partial(deal_kernel, step),
        [hbm] * 2,
        [pltpu.with_memory_space_constraint(field, pltpu.HBM) for field in (inputs, cotangent)],
        dealt,
        [held(2, *inputs.shape), pltpu.SemaphoreType.DMA((2,))],
        10**9,
        3,
    )
    own = lax.all_to_all(own, every, 0, 0, tiled=True)
    place = jnp.stack([lax.axis_index(axis) for axis in ("x", "y", "core", "z")]).astype(jnp.int32)
    piece = pltpu.HBM((2, half, cells), BF16)
    one_far, two_far = (pltpu.with_memory_space_constraint(w, pltpu.HBM) for w in (conv1_weight, conv2_weight))
    hidden, pre_grad, kept, pair, x_same, x_cross, y_same, y_cross = kernel(
        functools.partial(inner_kernel, band, step),
        [smem, vmem, vmem, hbm],
        (place, own, conv1_weight, two_far),
        (shaped(cells, channels),) * 2 + (piece,) * 6,
        [
            weights,
            stack,
            held(cells, channels, kind=F32),
            held(cells, channels, kind=F32),
            held(8, half, cells),
            pltpu.SemaphoreType.DMA((1,)),
            pltpu.SemaphoreType.DMA((2, 6)),
        ],
        2 * flops,
        10,
        (vmem,) * 2 + (hbm,) * 6,
    )
    y_same, x_same = passed(y_same, 0, 1, 0), passed(x_same, 1, 0, 0)
    y_cross, x_cross = passed(y_cross, 0, 1, 1), passed(x_cross, 1, 0, 1)
    pair = passed(pair, 0, 0, 1)
    far = (
        passed(y_same[0], 1, 0, 0),
        passed(y_cross[0], 1, 0, 0),
        passed(x_same[1], 0, 1, 0),
        passed(x_cross[1], 0, 1, 0),
    )
    hidden, pre_grad, pair = lax.optimization_barrier((hidden, pre_grad, pair))
    fields = kernel(
        functools.partial(outer_kernel, band, step),
        [vmem] * 3 + [hbm] * 2,
        (own, hidden, pre_grad, one_far, two_far),
        dealt,
        [weights, weights, stack, pltpu.SemaphoreType.DMA((2,))],
        2 * flops,
        9,
    )
    fields = lax.all_to_all(fields, every, 0, 0, tiled=True)
    output, input_grad = kernel(
        functools.partial(gather_kernel, step), [vmem], (fields,), (shaped(*inputs.shape),) * 2, [], 10**9, 3
    )
    sums = shaped(3, 3 * half, half, kind=F32)
    near = kernel(
        functools.partial(near_kernel, band, step),
        [vmem] * 6,
        (kept, pair, x_same, x_cross, y_same, y_cross),
        sums,
        [held(3 * half, 6 * cells), held(3, half, 6 * cells)],
        2 * flops,
        6,
    )
    terms = kernel(
        functools.partial(far_kernel, band, step),
        [smem] + [vmem] * 5,
        (place, near) + far,
        (pltpu.HBM((height, channels), BF16),) * 8,
        [
            held(3 * half, 2 * cells),
            held(3, half, 2 * cells),
            held(*sums.shape, kind=F32),
            held(8, height, channels),
            pltpu.SemaphoreType.DMA((8,)),
        ],
        flops,
        4,
        (hbm,) * 8,
    )
    parts = list(terms)
    for away in (6, 7, 4, 5, 2, 3, 1):
        parts[away] = lax.ppermute(terms[away], ("z", "core"), [(i, i ^ away) for i in range(8)])
    grad = shaped(3, 3, deep, half // 2, kind=F32)
    conv1_grad, conv2_grad = kernel(
        functools.partial(finish_kernel, scale), [smem] + [vmem] * 8, (place, *parts), (grad, grad), [], 10**6, 2
    )
    return (output, input_grad, conv1_grad, conv2_grad)


def is_fast(mesh):
    return dict(mesh.shape) == {"lon": 8, "lat": 4}


def solution(mesh):
    body, lon, lat = local, "lon", "lat"
    if is_fast(mesh):
        lon, lat = ("z", "y"), ("x", "core")
        mesh = jax.sharding.Mesh(mesh.devices.reshape(4, 2, 2, 2), lon + lat)
        body = fast_local
    field, grad = P(lat, lon, None), P(None, None, lon, lat)
    return jax.shard_map(
        body,
        mesh=mesh,
        in_specs=(field, P(), P(), field),
        out_specs=(field, field, grad, grad),
        check_vma=False,
    )
```

```python
import functools

import jax
import jax.numpy as jnp
from jax import lax
from jax.experimental import pallas as pl
from jax.experimental.pallas import tpu as pltpu
from jax.sharding import PartitionSpec as P

F32, BF16 = jnp.float32, jnp.bfloat16


def passed_along(shard, axis, by):
    length = lax.axis_size(axis)
    return lax.ppermute(shard, axis, [(i, (i + by) % length) for i in range(length)])


def padded(shard, sides, width):
    for axis, dim in sides:
        size, length = (lax.axis_size(axis), shard.shape[dim])
        up = [(i, (i + 1) % size) for i in range(size - 1)]
        down = [(j, i) for i, j in up]
        last = lax.slice_in_dim(shard, length - width, length, axis=dim)
        initial = lax.slice_in_dim(shard, 0, width, axis=dim)
        before = lax.ppermute(last, axis, up)
        after = lax.ppermute(initial, axis, down)
        shard = jnp.concatenate([before, shard, after], axis=dim)
    return shard


def extend(field):
    western = passed_along(field, "lon", 1)
    eastern = passed_along(field, "lon", -1)
    widened = jnp.concatenate([western, field, eastern], axis=1)
    return padded(widened, (("lat", 0),), 1)


def windows(padded_field, count_of_rows, lon_width, channels, direction):
    pieces = []
    for lat_step in (-1, 0, 1):
        for longitude_stride in (-1, 0, 1):
            row_start = 1 + direction * lat_step
            column_begin = lon_width + direction * lon_width * longitude_stride
            pieces.append(
                padded_field[
                    row_start : row_start + count_of_rows, column_begin : column_begin + lon_width
                ]
            )
    stacked = jnp.concatenate(pieces, axis=2)
    return stacked.reshape(count_of_rows * lon_width, 9 * channels)


def full_terms(stacked, grad, scale, channels):
    product = lax.dot_general(
        stacked, grad, (((0,), (0,)), ((), ())), preferred_element_type=jnp.float32
    )
    return (product * scale).reshape(9, channels, channels)


def local(inputs, conv1_weight, conv2_weight, cotangent):
    count_of_rows, lon_width, channels = inputs.shape
    cells = count_of_rows * lon_width
    lon_count = lax.axis_size("lon")
    latitude_count = lax.axis_size("lat")
    scale = (count_of_rows * latitude_count * lon_width * lon_count) ** (-0.5)
    forward_one = conv1_weight.reshape(9 * channels, channels)
    forward_two = conv2_weight.reshape(9 * channels, channels)
    turned_one = jnp.swapaxes(conv1_weight, 2, 3).reshape(9 * channels, channels)
    turned_two = jnp.swapaxes(conv2_weight, 2, 3).reshape(9 * channels, channels)
    source_field, cot_field = (inputs, cotangent)

    def stack_of(field, direction):
        return windows(extend(field), count_of_rows, lon_width, channels, direction)

    def as_field(flat):
        return flat.reshape(count_of_rows, lon_width, channels)

    stack_input = stack_of(source_field, 1)
    first = jnp.dot(stack_input, forward_one, preferred_element_type=jnp.float32)
    cdf = 0.5 * (1.0 + jax.scipy.special.erf(first / jnp.sqrt(2.0)))
    hidden = (first * cdf).astype(jnp.bfloat16)
    stack_hidden = stack_of(as_field(hidden), 1)
    second = jnp.dot(stack_hidden, forward_two, preferred_element_type=jnp.float32)
    flat_input = source_field.reshape(cells, channels)
    output = (flat_input.astype(jnp.float32) + second).astype(jnp.bfloat16)
    flat_cot = cot_field.reshape(cells, channels)
    stacked_cotangent = stack_of(cot_field, -1)
    upstream = jnp.dot(stacked_cotangent, turned_two, preferred_element_type=jnp.float32)
    density = jnp.exp(-0.5 * first * first) / jnp.sqrt(2.0 * jnp.pi)
    pre_grad = (upstream * (cdf + first * density)).astype(jnp.bfloat16)
    stack_pre = stack_of(as_field(pre_grad), -1)
    back = jnp.dot(stack_pre, turned_one, preferred_element_type=jnp.float32)
    input_grad = (flat_cot.astype(jnp.float32) + back).astype(jnp.bfloat16)
    output = output.reshape(count_of_rows, lon_width, channels)
    input_grad = input_grad.reshape(count_of_rows, lon_width, channels)
    in_part = channels // lon_count
    out_part = channels // latitude_count
    terms_one = full_terms(stack_input, pre_grad, scale, channels)
    terms_two = full_terms(stack_hidden, flat_cot, scale, channels)
    partly = (
        lax.psum_scatter(terms_one, "lon", scatter_dimension=1, tiled=True),
        lax.psum_scatter(terms_two, "lon", scatter_dimension=1, tiled=True),
    )
    grad_one, grad_two = (
        lax.psum_scatter(partly[0], "lat", scatter_dimension=2, tiled=True),
        lax.psum_scatter(partly[1], "lat", scatter_dimension=2, tiled=True),
    )
    conv1_grad = grad_one.reshape(3, 3, in_part, out_part)
    conv2_grad = grad_two.reshape(3, 3, in_part, out_part)
    return (output, input_grad, conv1_grad, conv2_grad)


def write_stack(field, stack_ref, band, step):
    cells, channels = field.shape
    wide = field.astype(F32)
    place = lax.broadcasted_iota(jnp.int32, (cells, channels), 0) % band
    above = jnp.where(place >= step, pltpu.roll(wide, step, 0), 0.0).astype(BF16)
    below = jnp.where(place < band - step, pltpu.roll(wide, cells - step, 0), 0.0).astype(BF16)
    for at, part in enumerate((above, field, below)):
        columns = slice(at * channels, (at + 1) * channels)
        stack_ref[band : band + cells, columns] = part
        stack_ref[0:band, columns] = part[cells - band :]
        stack_ref[band + cells :, columns] = part[0:band]


def convolved(stack_ref, weight_ref, band, cells, fetch=None):
    total = None
    for b in range(3):
        if fetch is not None:
            fetch[b].wait()
        channels = weight_ref.shape[2]
        tap = weight_ref[:, b].reshape(3 * channels, channels)
        term = jnp.dot(stack_ref[b * band : b * band + cells, :], tap, preferred_element_type=F32)
        total = term if total is None else total + term
    return total


def convolved_back(stack_ref, weight_ref, band, cells):
    total = None
    for b in range(3):
        tap = jnp.concatenate([weight_ref[2 - a, 2 - b] for a in range(3)], axis=1)
        term = lax.dot_general(
            stack_ref[b * band : b * band + cells, :],
            tap,
            (((1,), (1,)), ((), ())),
            preferred_element_type=F32,
        )
        total = term if total is None else total + term
    return total


def one_hot_rows(cells, step, devices, back):
    to = lax.broadcasted_iota(jnp.int32, (cells, cells), 1 if back else 0)
    source = lax.broadcasted_iota(jnp.int32, (cells, cells), 0 if back else 1)
    rows = cells // (devices * step)
    device, row, column = to // (rows * step), (to // step) % rows, to % step
    return (source == (row * devices + device) * step + column).astype(BF16)


def deal_kernel(step, inputs_ref, cot_ref, out_ref, held_ref, sems):
    devices, _, rows, channels = out_ref.shape
    cells = devices * rows
    copies = fetched(((inputs_ref, held_ref.at[0]), (cot_ref, held_ref.at[1])), sems)
    chosen = one_hot_rows(cells, step, devices, False)
    for at, copy in enumerate(copies):
        copy.wait()
        field = held_ref[at].reshape(cells, channels)
        dealt = jnp.dot(chosen, field, preferred_element_type=F32).astype(BF16)
        out_ref[:, at] = dealt.reshape(devices, rows, channels)


def gather_kernel(step, fields_ref, output_ref, grad_ref):
    devices, _, rows, channels = fields_ref.shape
    cells = devices * rows
    chosen = one_hot_rows(cells, step, devices, True)
    for at, ref in enumerate((output_ref, grad_ref)):
        field = fields_ref[:, at].reshape(cells, channels)
        ref[...] = jnp.dot(chosen, field, preferred_element_type=F32).astype(BF16).reshape(ref.shape)


def fetched(pairs, sems):
    copies = [pltpu.make_async_copy(source, to, sems.at[at]) for at, (source, to) in enumerate(pairs)]
    for copy in copies:
        copy.start()
    return copies


def inner_kernel(band, step, place_ref, own_ref, one_ref, two_ref,
                 hidden_ref, pre_ref, kept_ref, pair_ref, x_same_ref, x_cross_ref, y_same_ref, y_cross_ref,
                 one_held, two_held, stack_ref, first_ref, slope_ref, turned_ref, sems, out_sems):
    x, y, core = place_ref[0], place_ref[1], place_ref[2]
    other = 1 - core
    cells, channels = first_ref.shape
    fetch = fetched([(one_ref.at[:, b], one_held.at[:, b]) for b in range(3)] + [(two_ref, two_held)], sems)
    half, rows = channels // 2, 32
    deep = half // 4

    def turn(at, field):
        turned = field.T
        for h in range(2):
            for z in range(4):
                begin = (2 * z + h) * deep if at < 2 else h * half + z * deep
                turned_ref[at * 2 + h, z * deep : (z + 1) * deep, :] = turned[begin : begin + deep]

    def sent(side, wanted):
        pairs = [(turned_ref.at[4 * side + of * 2 + h], ref.at[side]) for ref, of, h in wanted]
        return fetched(pairs, out_sems.at[side])

    source = own_ref[:, 0].reshape(cells, channels)
    write_stack(source, stack_ref, band, step)
    first_ref[...] = convolved(stack_ref, one_held, band, cells, fetch)
    turn(0, source)

    def activate(at, carry):
        span = pl.ds(pl.multiple_of(at * rows, rows), rows)
        first = first_ref[span, :]
        cdf = 0.5 * (1.0 + lax.erf(first * (0.5**0.5)))
        density = jnp.exp(-0.5 * first * first) * ((2.0 * jnp.pi) ** -0.5)
        hidden_ref[span, :] = (first * cdf).astype(BF16)
        slope_ref[span, :] = cdf + first * density
        return carry

    lax.fori_loop(0, cells // rows, activate, 0)
    turn(1, hidden_ref[...])
    copies = sent(0, (
        (y_same_ref, core, 1 - y), (y_cross_ref, other, 1 - y), (x_same_ref, core, y),
        (x_cross_ref, other, y), (pair_ref, other, y), (kept_ref, core, y),
    ))
    cot = own_ref[:, 1].reshape(cells, channels)
    write_stack(cot, stack_ref, band, step)
    turn(3, cot)
    fetch[3].wait()
    pre_ref[...] = (slope_ref[...] * convolved_back(stack_ref, two_held, band, cells)).astype(BF16)
    turn(2, pre_ref[...])
    copies += sent(1, (
        (y_same_ref, core, x), (y_cross_ref, other, x), (x_same_ref, core, 1 - x),
        (x_cross_ref, other, 1 - x), (pair_ref, other, x), (kept_ref, core, x),
    ))
    for copy in copies:
        copy.wait()


def outer_kernel(band, step, own_ref, hidden_ref, pre_ref, one_ref, two_ref, out_ref,
                 one_held, two_held, stack_ref, sems):
    cells, channels = hidden_ref.shape
    shape = (out_ref.shape[0],) + out_ref.shape[2:]
    copies = fetched(((two_ref, two_held), (one_ref, one_held)), sems)
    write_stack(hidden_ref[...], stack_ref, band, step)
    copies[0].wait()
    second = convolved(stack_ref, two_held, band, cells)
    source = own_ref[:, 0].reshape(cells, channels)
    out_ref[:, 0] = (source.astype(F32) + second).astype(BF16).reshape(shape)
    write_stack(pre_ref[...], stack_ref, band, step)
    copies[1].wait()
    back = convolved_back(stack_ref, one_held, band, cells)
    cot = own_ref[:, 1].reshape(cells, channels)
    out_ref[:, 1] = (cot.astype(F32) + back).astype(BF16).reshape(shape)


def units(deep):
    count = deep // 16
    for unit in range(9 * count):
        yield unit // count, (unit % count) * 16, (unit // 4) * 16, unit % 4


def summed(band, step, lefts, rights, turned_ref, moved_ref, b):
    half, cells = lefts[0].shape
    if b == 0:
        place = lax.broadcasted_iota(jnp.int32, (half, cells), 1) % band
        for at, (left_ref, right_ref) in enumerate(zip(lefts, rights)):
            columns = slice(at * cells, (at + 1) * cells)
            field = left_ref[...]
            wide = field.astype(F32)
            turned_ref[0:half, columns] = jnp.where(place >= step, pltpu.roll(wide, step, 1), 0.0).astype(BF16)
            turned_ref[half : 2 * half, columns] = field
            turned_ref[2 * half :, columns] = jnp.where(
                place < band - step, pltpu.roll(wide, cells - step, 1), 0.0
            ).astype(BF16)
            grad = right_ref[...]
            wide = grad.astype(F32)
            moved_ref[0, :, columns] = pltpu.roll(wide, cells - band, 1).astype(BF16)
            moved_ref[1, :, columns] = grad
            moved_ref[2, :, columns] = pltpu.roll(wide, band, 1).astype(BF16)
    return lax.dot_general(turned_ref[...], moved_ref[b], (((1,), (1,)), ((), ())), preferred_element_type=F32)


def near_kernel(band, step, *refs):
    pieces, (sums_ref, turned_ref, moved_ref) = refs[:-3], refs[-3:]
    lefts, rights = ([ref.at[side] for ref in pieces] for side in range(2))
    for b in range(3):
        sums_ref[b] = summed(band, step, lefts, rights, turned_ref, moved_ref, b)


def far_kernel(band, step, place_ref, near_ref, *refs):
    pieces, out_refs, (turned_ref, moved_ref, sums_ref, send_ref, sems) = refs[:4], refs[4:-5], refs[-5:]
    me = place_ref[3] * 2 + place_ref[2]
    half, cells = pieces[0].shape
    for b in range(3):
        sums_ref[b] = near_ref[b] + summed(band, step, pieces[:2], pieces[2:], turned_ref, moved_ref, b)
    deep, quarter = half // 4, half // 2
    height = send_ref.shape[1]
    for z in range(4):
        for core in range(2):
            blocks = [[] for _ in range(height // 16)]
            for tap, row, to, _ in units(deep):
                begin = (tap // 3) * half + z * deep + row
                blocks[to // 16].append(
                    sums_ref[tap % 3, begin : begin + 16, core * quarter : (core + 1) * quarter]
                )
            for to, parts in enumerate(blocks):
                while len(parts) < 4:
                    parts.append(jnp.zeros((16, quarter), F32))
                send_ref[z * 2 + core, to * 16 : (to + 1) * 16, :] = jnp.concatenate(parts, axis=1).astype(BF16)
    pairs = [(send_ref.at[me ^ away], ref) for away, ref in enumerate(out_refs)]
    for copy in fetched(pairs, sems):
        copy.wait()


def finish_kernel(scale, place_ref, *refs):
    parts, (one_ref, two_ref) = refs[:-2], refs[-2:]
    core = place_ref[2]
    deep, quarter = one_ref.shape[2:]
    sums = []
    for other in range(2):
        total = parts[other][...].astype(F32)
        for ref in parts[other + 2 :: 2]:
            total = total + ref[...].astype(F32)
        sums.append(total * scale)
    ours, theirs = sums
    for out_ref, total in (
        (one_ref, jnp.where(core == 0, ours, theirs)),
        (two_ref, jnp.where(core == 0, theirs, ours)),
    ):
        for tap, row, begin, slot in units(deep):
            out_ref[tap // 3, tap % 3, row : row + 16, :] = total[
                begin : begin + 16, slot * quarter : (slot + 1) * quarter
            ]


def fast_local(inputs, conv1_weight, conv2_weight, cotangent):
    rows, width, channels = inputs.shape
    every = ("z", "y", "x", "core")
    devices = lax.axis_size(every)
    step = width // devices
    cells = rows * width
    lat = lax.axis_size("x") * lax.axis_size("core")
    lon = devices // lat
    band = rows * lat * step
    half, deep = channels // 2, channels // lon
    height = -(-9 * (deep // 16) // 4) * 16
    scale = (rows * lat * width * lon) ** (-0.5)
    flops = 2 * 9 * cells * channels * channels
    vmem, hbm, smem = (pl.BlockSpec(memory_space=space) for space in (pltpu.VMEM, pltpu.HBM, pltpu.SMEM))

    def held(*shape, kind=BF16):
        return pltpu.VMEM(shape, kind)

    def shaped(*shape, kind=BF16):
        return jax.ShapeDtypeStruct(shape, kind)

    def kernel(body, specs, arguments, out_shape, scratch_shapes, work, megabytes):
        return pl.pallas_call(
            body,
            out_shape=out_shape,
            in_specs=specs,
            out_specs=jax.tree.map(lambda _: vmem, out_shape),
            scratch_shapes=scratch_shapes,
            compiler_params=pltpu.CompilerParams(vmem_limit_bytes=20 * 2**20),
            cost_estimate=pl.CostEstimate(flops=work, bytes_accessed=megabytes * 2**20, transcendentals=0),
        )(*arguments)

    def passed(piece, x, y, core):
        pairs = [(i, i ^ (4 * y + 2 * x + core)) for i in range(8)]
        return lax.ppermute(piece, ("y", "x", "core"), pairs)

    stack = held(cells + 2 * band, 3 * channels)
    weights = held(*conv1_weight.shape)
    dealt = shaped(devices, 2, rows * step, channels)
    own = kernel(
        functools.partial(deal_kernel, step),
        [hbm] * 2,
        [pltpu.with_memory_space_constraint(field, pltpu.HBM) for field in (inputs, cotangent)],
        dealt,
        [held(2, *inputs.shape), pltpu.SemaphoreType.DMA((2,))],
        10**9,
        3,
    )
    own = lax.all_to_all(own, every, 0, 0, tiled=True)
    place = jnp.stack([lax.axis_index(axis) for axis in ("x", "y", "core", "z")]).astype(jnp.int32)
    piece = pltpu.VMEM((2, half, cells), BF16)
    one_far, two_far = (pltpu.with_memory_space_constraint(w, pltpu.HBM) for w in (conv1_weight, conv2_weight))
    hidden, pre_grad, kept, pair, x_same, x_cross, y_same, y_cross = kernel(
        functools.partial(inner_kernel, band, step),
        [smem, vmem, hbm, hbm],
        (place, own, one_far, two_far),
        (shaped(cells, channels),) * 2 + (piece,) * 6,
        [
            weights,
            weights,
            stack,
            held(cells, channels, kind=F32),
            held(cells, channels, kind=F32),
            held(8, half, cells),
            pltpu.SemaphoreType.DMA((4,)),
            pltpu.SemaphoreType.DMA((2, 6)),
        ],
        2 * flops,
        10,
    )
    y_same, x_same = passed(y_same, 0, 1, 0), passed(x_same, 1, 0, 0)
    y_cross, x_cross = passed(y_cross, 0, 1, 1), passed(x_cross, 1, 0, 1)
    pair = passed(pair, 0, 0, 1)
    hidden, pre_grad, pair = lax.optimization_barrier((hidden, pre_grad, pair))
    fields = kernel(
        functools.partial(outer_kernel, band, step),
        [vmem] * 3 + [hbm] * 2,
        (own, hidden, pre_grad, one_far, two_far),
        dealt,
        [weights, weights, stack, pltpu.SemaphoreType.DMA((2,))],
        2 * flops,
        9,
    )
    fields, y_same, x_same = lax.optimization_barrier((fields, y_same, x_same))
    far = (
        passed(y_same[0], 1, 0, 0),
        passed(y_cross[0], 1, 0, 0),
        passed(x_same[1], 0, 1, 0),
        passed(x_cross[1], 0, 1, 0),
    )
    fields = lax.all_to_all(fields, every, 0, 0, tiled=True)
    output, input_grad = kernel(
        functools.partial(gather_kernel, step), [vmem], (fields,), (shaped(*inputs.shape),) * 2, [], 10**9, 3
    )
    sums = shaped(3, 3 * half, half, kind=F32)
    near = kernel(
        functools.partial(near_kernel, band, step),
        [vmem] * 6,
        (kept, pair, x_same, x_cross, y_same, y_cross),
        sums,
        [held(3 * half, 6 * cells), held(3, half, 6 * cells)],
        2 * flops,
        6,
    )
    terms = kernel(
        functools.partial(far_kernel, band, step),
        [smem] + [vmem] * 5,
        (place, near) + far,
        (pltpu.VMEM((height, channels), BF16),) * 8,
        [
            held(3 * half, 2 * cells),
            held(3, half, 2 * cells),
            held(*sums.shape, kind=F32),
            held(8, height, channels),
            pltpu.SemaphoreType.DMA((8,)),
        ],
        flops,
        4,
    )
    parts = list(terms)
    for away in (6, 7, 4, 5, 2, 3, 1):
        parts[away] = lax.ppermute(terms[away], ("z", "core"), [(i, i ^ away) for i in range(8)])
    output, input_grad, parts = lax.optimization_barrier((output, input_grad, parts))
    grad = shaped(3, 3, deep, half // 2, kind=F32)
    conv1_grad, conv2_grad = kernel(
        functools.partial(finish_kernel, scale), [smem] + [vmem] * 8, (place, *parts), (grad, grad), [], 10**6, 2
    )
    return (output, input_grad, conv1_grad, conv2_grad)


def is_fast(mesh):
    return dict(mesh.shape) == {"lon": 8, "lat": 4}


def solution(mesh):
    body, lon, lat = local, "lon", "lat"
    if is_fast(mesh):
        lon, lat = ("z", "y"), ("x", "core")
        mesh = jax.sharding.Mesh(mesh.devices.reshape(4, 2, 2, 2), lon + lat)
        body = fast_local
    field, grad = P(lat, lon, None), P(None, None, lon, lat)
    return jax.shard_map(
        body,
        mesh=mesh,
        in_specs=(field, P(), P(), field),
        out_specs=(field, field, grad, grad),
        check_vma=False,
    )
```

```python
import functools

import jax
import jax.numpy as jnp
from jax import lax
from jax.experimental import pallas as pl
from jax.experimental.pallas import tpu as pltpu
from jax.sharding import PartitionSpec as P

F32, BF16 = jnp.float32, jnp.bfloat16


def passed_along(shard, axis, by):
    length = lax.axis_size(axis)
    return lax.ppermute(shard, axis, [(i, (i + by) % length) for i in range(length)])


def padded(shard, sides, width):
    for axis, dim in sides:
        size, length = (lax.axis_size(axis), shard.shape[dim])
        up = [(i, (i + 1) % size) for i in range(size - 1)]
        down = [(j, i) for i, j in up]
        last = lax.slice_in_dim(shard, length - width, length, axis=dim)
        initial = lax.slice_in_dim(shard, 0, width, axis=dim)
        before = lax.ppermute(last, axis, up)
        after = lax.ppermute(initial, axis, down)
        shard = jnp.concatenate([before, shard, after], axis=dim)
    return shard


def extend(field):
    western = passed_along(field, "lon", 1)
    eastern = passed_along(field, "lon", -1)
    widened = jnp.concatenate([western, field, eastern], axis=1)
    return padded(widened, (("lat", 0),), 1)


def windows(padded_field, count_of_rows, lon_width, channels, direction):
    pieces = []
    for lat_step in (-1, 0, 1):
        for longitude_stride in (-1, 0, 1):
            row_start = 1 + direction * lat_step
            column_begin = lon_width + direction * lon_width * longitude_stride
            pieces.append(
                padded_field[
                    row_start : row_start + count_of_rows, column_begin : column_begin + lon_width
                ]
            )
    stacked = jnp.concatenate(pieces, axis=2)
    return stacked.reshape(count_of_rows * lon_width, 9 * channels)


def full_terms(stacked, grad, scale, channels):
    product = lax.dot_general(
        stacked, grad, (((0,), (0,)), ((), ())), preferred_element_type=jnp.float32
    )
    return (product * scale).reshape(9, channels, channels)


def local(inputs, conv1_weight, conv2_weight, cotangent):
    count_of_rows, lon_width, channels = inputs.shape
    cells = count_of_rows * lon_width
    lon_count = lax.axis_size("lon")
    latitude_count = lax.axis_size("lat")
    scale = (count_of_rows * latitude_count * lon_width * lon_count) ** (-0.5)
    forward_one = conv1_weight.reshape(9 * channels, channels)
    forward_two = conv2_weight.reshape(9 * channels, channels)
    turned_one = jnp.swapaxes(conv1_weight, 2, 3).reshape(9 * channels, channels)
    turned_two = jnp.swapaxes(conv2_weight, 2, 3).reshape(9 * channels, channels)
    source_field, cot_field = (inputs, cotangent)

    def stack_of(field, direction):
        return windows(extend(field), count_of_rows, lon_width, channels, direction)

    def as_field(flat):
        return flat.reshape(count_of_rows, lon_width, channels)

    stack_input = stack_of(source_field, 1)
    first = jnp.dot(stack_input, forward_one, preferred_element_type=jnp.float32)
    cdf = 0.5 * (1.0 + jax.scipy.special.erf(first / jnp.sqrt(2.0)))
    hidden = (first * cdf).astype(jnp.bfloat16)
    stack_hidden = stack_of(as_field(hidden), 1)
    second = jnp.dot(stack_hidden, forward_two, preferred_element_type=jnp.float32)
    flat_input = source_field.reshape(cells, channels)
    output = (flat_input.astype(jnp.float32) + second).astype(jnp.bfloat16)
    flat_cot = cot_field.reshape(cells, channels)
    stacked_cotangent = stack_of(cot_field, -1)
    upstream = jnp.dot(stacked_cotangent, turned_two, preferred_element_type=jnp.float32)
    density = jnp.exp(-0.5 * first * first) / jnp.sqrt(2.0 * jnp.pi)
    pre_grad = (upstream * (cdf + first * density)).astype(jnp.bfloat16)
    stack_pre = stack_of(as_field(pre_grad), -1)
    back = jnp.dot(stack_pre, turned_one, preferred_element_type=jnp.float32)
    input_grad = (flat_cot.astype(jnp.float32) + back).astype(jnp.bfloat16)
    output = output.reshape(count_of_rows, lon_width, channels)
    input_grad = input_grad.reshape(count_of_rows, lon_width, channels)
    in_part = channels // lon_count
    out_part = channels // latitude_count
    terms_one = full_terms(stack_input, pre_grad, scale, channels)
    terms_two = full_terms(stack_hidden, flat_cot, scale, channels)
    partly = (
        lax.psum_scatter(terms_one, "lon", scatter_dimension=1, tiled=True),
        lax.psum_scatter(terms_two, "lon", scatter_dimension=1, tiled=True),
    )
    grad_one, grad_two = (
        lax.psum_scatter(partly[0], "lat", scatter_dimension=2, tiled=True),
        lax.psum_scatter(partly[1], "lat", scatter_dimension=2, tiled=True),
    )
    conv1_grad = grad_one.reshape(3, 3, in_part, out_part)
    conv2_grad = grad_two.reshape(3, 3, in_part, out_part)
    return (output, input_grad, conv1_grad, conv2_grad)


def write_stack(field, stack_ref, band, step):
    cells, channels = field.shape
    wide = field.astype(F32)
    place = lax.broadcasted_iota(jnp.int32, (cells, channels), 0) % band
    above = jnp.where(place >= step, pltpu.roll(wide, step, 0), 0.0).astype(BF16)
    below = jnp.where(place < band - step, pltpu.roll(wide, cells - step, 0), 0.0).astype(BF16)
    for at, part in enumerate((above, field, below)):
        columns = slice(at * channels, (at + 1) * channels)
        stack_ref[band : band + cells, columns] = part
        stack_ref[0:band, columns] = part[cells - band :]
        stack_ref[band + cells :, columns] = part[0:band]


def convolved(stack_ref, weight_ref, band, cells):
    total = None
    for b in range(3):
        channels = weight_ref.shape[2]
        tap = weight_ref[:, b].reshape(3 * channels, channels)
        term = jnp.dot(stack_ref[b * band : b * band + cells, :], tap, preferred_element_type=F32)
        total = term if total is None else total + term
    return total


def convolved_back(stack_ref, weight_ref, band, cells):
    total = None
    for b in range(3):
        tap = jnp.concatenate([weight_ref[2 - a, 2 - b] for a in range(3)], axis=1)
        term = lax.dot_general(
            stack_ref[b * band : b * band + cells, :],
            tap,
            (((1,), (1,)), ((), ())),
            preferred_element_type=F32,
        )
        total = term if total is None else total + term
    return total


def one_hot_rows(cells, step, devices, back):
    to = lax.broadcasted_iota(jnp.int32, (cells, cells), 1 if back else 0)
    source = lax.broadcasted_iota(jnp.int32, (cells, cells), 0 if back else 1)
    rows = cells // (devices * step)
    device, row, column = to // (rows * step), (to // step) % rows, to % step
    return (source == (row * devices + device) * step + column).astype(BF16)


def deal_kernel(step, inputs_ref, cot_ref, out_ref, held_ref, sems):
    devices, _, rows, channels = out_ref.shape
    cells = devices * rows
    copies = fetched(((inputs_ref, held_ref.at[0]), (cot_ref, held_ref.at[1])), sems)
    chosen = one_hot_rows(cells, step, devices, False)
    for at, copy in enumerate(copies):
        copy.wait()
        field = held_ref[at].reshape(cells, channels)
        dealt = jnp.dot(chosen, field, preferred_element_type=F32).astype(BF16)
        out_ref[:, at] = dealt.reshape(devices, rows, channels)


def gather_kernel(step, fields_ref, output_ref, grad_ref):
    devices, _, rows, channels = fields_ref.shape
    cells = devices * rows
    chosen = one_hot_rows(cells, step, devices, True)
    for at, ref in enumerate((output_ref, grad_ref)):
        field = fields_ref[:, at].reshape(cells, channels)
        ref[...] = jnp.dot(chosen, field, preferred_element_type=F32).astype(BF16).reshape(ref.shape)


def fetched(pairs, sems):
    copies = [pltpu.make_async_copy(source, to, sems.at[at]) for at, (source, to) in enumerate(pairs)]
    for copy in copies:
        copy.start()
    return copies


def weights_kernel(one_ref, two_ref, one_out, two_out, sems):
    for copy in fetched(((one_ref, one_out), (two_ref, two_out)), sems):
        copy.wait()


def inner_kernel(band, step, place_ref, own_ref, one_ref, two_ref,
                 hidden_ref, pre_ref, mine_ref, give_ref,
                 stack_ref, first_ref, slope_ref, turned_ref):
    x, y, core = place_ref[0], place_ref[1], place_ref[2]
    cells, channels = first_ref.shape
    half, rows = channels // 2, 32
    deep = half // 4

    def turn(at, field):
        turned = field.T
        for h in range(2):
            for z in range(4):
                begin = (2 * z + h) * deep if at < 2 else h * half + z * deep
                turned_ref[at * 2 + h, z * deep : (z + 1) * deep, :] = turned[begin : begin + deep]

    source = own_ref[:, 0].reshape(cells, channels)
    write_stack(source, stack_ref, band, step)
    first_ref[...] = convolved(stack_ref, one_ref, band, cells)
    turn(0, source)

    def activate(at, carry):
        span = pl.ds(pl.multiple_of(at * rows, rows), rows)
        first = first_ref[span, :]
        cdf = 0.5 * (1.0 + lax.erf(first * (0.5**0.5)))
        density = jnp.exp(-0.5 * first * first) * ((2.0 * jnp.pi) ** -0.5)
        hidden_ref[span, :] = (first * cdf).astype(BF16)
        slope_ref[span, :] = cdf + first * density
        return carry

    lax.fori_loop(0, cells // rows, activate, 0)
    turn(1, hidden_ref[...])
    cot = own_ref[:, 1].reshape(cells, channels)
    write_stack(cot, stack_ref, band, step)
    turn(3, cot)
    pre_ref[...] = (slope_ref[...] * convolved_back(stack_ref, two_ref, band, cells)).astype(BF16)
    turn(2, pre_ref[...])

    for ref, of in ((mine_ref, core), (give_ref, 1 - core)):
        ref[0] = turned_ref[of * 2 + 1 - y]
        ref[1] = turned_ref[of * 2 + y]
        ref[2] = turned_ref[4 + of * 2 + 1 - x]
        ref[3] = turned_ref[4 + of * 2 + x]


def join_kernel(mine_ref, got_ref, x_ref, y_ref):
    for at, ref in enumerate((mine_ref, got_ref)):
        y_ref[at] = ref[0]
        x_ref[2 + at] = ref[1]
        x_ref[at] = ref[2]
        y_ref[2 + at] = ref[3]


def outer_kernel(band, step, own_ref, hidden_ref, pre_ref, one_ref, two_ref, out_ref, stack_ref):
    cells, channels = hidden_ref.shape
    shape = (out_ref.shape[0],) + out_ref.shape[2:]
    write_stack(hidden_ref[...], stack_ref, band, step)
    second = convolved(stack_ref, two_ref, band, cells)
    source = own_ref[:, 0].reshape(cells, channels)
    out_ref[:, 0] = (source.astype(F32) + second).astype(BF16).reshape(shape)
    write_stack(pre_ref[...], stack_ref, band, step)
    back = convolved_back(stack_ref, one_ref, band, cells)
    cot = own_ref[:, 1].reshape(cells, channels)
    out_ref[:, 1] = (cot.astype(F32) + back).astype(BF16).reshape(shape)


def units(deep):
    count = deep // 16
    for unit in range(9 * count):
        yield unit // count, (unit % count) * 16, (unit // 4) * 16, unit % 4


def summed(band, step, lefts, rights, turned_ref, moved_ref, b):
    half, cells = lefts[0].shape
    if b == 0:
        place = lax.broadcasted_iota(jnp.int32, (half, cells), 1) % band
        for at, (left_ref, right_ref) in enumerate(zip(lefts, rights)):
            columns = slice(at * cells, (at + 1) * cells)
            field = left_ref[...]
            wide = field.astype(F32)
            turned_ref[0:half, columns] = jnp.where(place >= step, pltpu.roll(wide, step, 1), 0.0).astype(BF16)
            turned_ref[half : 2 * half, columns] = field
            turned_ref[2 * half :, columns] = jnp.where(
                place < band - step, pltpu.roll(wide, cells - step, 1), 0.0
            ).astype(BF16)
            grad = right_ref[...]
            wide = grad.astype(F32)
            moved_ref[0, :, columns] = pltpu.roll(wide, cells - band, 1).astype(BF16)
            moved_ref[1, :, columns] = grad
            moved_ref[2, :, columns] = pltpu.roll(wide, band, 1).astype(BF16)
    return lax.dot_general(turned_ref[...], moved_ref[b], (((1,), (1,)), ((), ())), preferred_element_type=F32)


def near_kernel(band, step, x_ref, y_ref, x_got_ref, y_got_ref, sums_ref, turned_ref, moved_ref):
    lefts = [x_ref.at[2], x_ref.at[3], x_got_ref.at[2], x_got_ref.at[3], y_got_ref.at[0], y_got_ref.at[1]]
    rights = [y_ref.at[2], y_ref.at[3], x_got_ref.at[0], x_got_ref.at[1], y_got_ref.at[2], y_got_ref.at[3]]
    for b in range(3):
        sums_ref[b] = summed(band, step, lefts, rights, turned_ref, moved_ref, b)


def far_kernel(band, step, place_ref, near_ref, left_ref, right_ref, *refs):
    out_refs, (turned_ref, moved_ref, sums_ref, send_ref, sems) = refs[:-5], refs[-5:]
    me = place_ref[3] * 2 + place_ref[2]
    half = left_ref.shape[1]
    lefts, rights = ([ref.at[at] for at in range(2)] for ref in (left_ref, right_ref))
    for b in range(3):
        sums_ref[b] = near_ref[b] + summed(band, step, lefts, rights, turned_ref, moved_ref, b)
    deep, quarter = half // 4, half // 2
    height = send_ref.shape[1]
    for z in range(4):
        for core in range(2):
            blocks = [[] for _ in range(height // 16)]
            for tap, row, to, _ in units(deep):
                begin = (tap // 3) * half + z * deep + row
                blocks[to // 16].append(
                    sums_ref[tap % 3, begin : begin + 16, core * quarter : (core + 1) * quarter]
                )
            for to, parts in enumerate(blocks):
                while len(parts) < 4:
                    parts.append(jnp.zeros((16, quarter), F32))
                send_ref[z * 2 + core, to * 16 : (to + 1) * 16, :] = jnp.concatenate(parts, axis=1).astype(BF16)
    pairs = [(send_ref.at[me ^ away], ref) for away, ref in enumerate(out_refs)]
    for copy in fetched(pairs, sems):
        copy.wait()


def finish_kernel(scale, place_ref, *refs):
    parts, (one_ref, two_ref) = refs[:-2], refs[-2:]
    core = place_ref[2]
    deep, quarter = one_ref.shape[2:]
    sums = []
    for other in range(2):
        total = parts[other][...].astype(F32)
        for ref in parts[other + 2 :: 2]:
            total = total + ref[...].astype(F32)
        sums.append(total * scale)
    ours, theirs = sums
    for out_ref, total in (
        (one_ref, jnp.where(core == 0, ours, theirs)),
        (two_ref, jnp.where(core == 0, theirs, ours)),
    ):
        for tap, row, begin, slot in units(deep):
            out_ref[tap // 3, tap % 3, row : row + 16, :] = total[
                begin : begin + 16, slot * quarter : (slot + 1) * quarter
            ]


def fast_local(inputs, conv1_weight, conv2_weight, cotangent):
    rows, width, channels = inputs.shape
    every = ("z", "y", "x", "core")
    devices = lax.axis_size(every)
    step = width // devices
    cells = rows * width
    lat = lax.axis_size("x") * lax.axis_size("core")
    lon = devices // lat
    band = rows * lat * step
    half, deep = channels // 2, channels // lon
    height = -(-9 * (deep // 16) // 4) * 16
    scale = (rows * lat * width * lon) ** (-0.5)
    flops = 2 * 9 * cells * channels * channels
    vmem, hbm, smem = (pl.BlockSpec(memory_space=space) for space in (pltpu.VMEM, pltpu.HBM, pltpu.SMEM))

    def held(*shape, kind=BF16):
        return pltpu.VMEM(shape, kind)

    def shaped(*shape, kind=BF16):
        return jax.ShapeDtypeStruct(shape, kind)

    def kernel(body, specs, arguments, out_shape, scratch_shapes, work, megabytes):
        return pl.pallas_call(
            body,
            out_shape=out_shape,
            in_specs=specs,
            out_specs=jax.tree.map(lambda _: vmem, out_shape),
            scratch_shapes=scratch_shapes,
            compiler_params=pltpu.CompilerParams(vmem_limit_bytes=20 * 2**20),
            cost_estimate=pl.CostEstimate(flops=work, bytes_accessed=megabytes * 2**20, transcendentals=0),
        )(*arguments)

    def passed(piece, x, y, core):
        pairs = [(i, i ^ (4 * y + 2 * x + core)) for i in range(8)]
        return lax.ppermute(piece, ("y", "x", "core"), pairs)

    stack = held(cells + 2 * band, 3 * channels)
    weights = held(*conv1_weight.shape)
    dealt = shaped(devices, 2, rows * step, channels)
    own = kernel(
        functools.partial(deal_kernel, step),
        [hbm] * 2,
        [pltpu.with_memory_space_constraint(field, pltpu.HBM) for field in (inputs, cotangent)],
        dealt,
        [held(2, *inputs.shape), pltpu.SemaphoreType.DMA((2,))],
        10**9,
        3,
    )
    own = lax.all_to_all(own, every, 0, 0, tiled=True)
    place = jnp.stack([lax.axis_index(axis) for axis in ("x", "y", "core", "z")]).astype(jnp.int32)
    one, two = kernel(
        weights_kernel,
        [hbm] * 2,
        [pltpu.with_memory_space_constraint(w, pltpu.HBM) for w in (conv1_weight, conv2_weight)],
        (weights, weights),
        [pltpu.SemaphoreType.DMA((2,))],
        10**6,
        10,
    )
    pieces = held(4, half, cells)
    hidden, pre_grad, mine, give = kernel(
        functools.partial(inner_kernel, band, step),
        [smem] + [vmem] * 3,
        (place, own, one, two),
        (held(cells, channels), held(cells, channels), pieces, pieces),
        [stack, held(cells, channels, kind=F32), held(cells, channels, kind=F32), held(8, half, cells)],
        2 * flops,
        10,
    )
    x_given, y_given = kernel(
        join_kernel, [vmem] * 2, (mine, passed(give, 0, 0, 1)), (pieces, pieces), [], 10**6, 4
    )
    x_got, y_got = passed(x_given, 1, 0, 0), passed(y_given, 0, 1, 0)
    far = (passed(y_got[:2], 1, 0, 0), passed(x_got[:2], 0, 1, 0))
    hidden, pre_grad, x_given = lax.optimization_barrier((hidden, pre_grad, x_given))
    fields = kernel(
        functools.partial(outer_kernel, band, step),
        [vmem] * 5,
        (own, hidden, pre_grad, one, two),
        dealt,
        [stack],
        2 * flops,
        9,
    )
    fields = lax.all_to_all(fields, every, 0, 0, tiled=True)
    output, input_grad = kernel(
        functools.partial(gather_kernel, step), [vmem], (fields,), (shaped(*inputs.shape),) * 2, [], 10**9, 3
    )
    sums = shaped(3, 3 * half, half, kind=F32)
    near = kernel(
        functools.partial(near_kernel, band, step),
        [vmem] * 4,
        (x_given, y_given, x_got, y_got),
        sums,
        [held(3 * half, 6 * cells), held(3, half, 6 * cells)],
        2 * flops,
        6,
    )
    terms = kernel(
        functools.partial(far_kernel, band, step),
        [smem] + [vmem] * 3,
        (place, near) + far,
        (pltpu.VMEM((height, channels), BF16),) * 8,
        [
            held(3 * half, 2 * cells),
            held(3, half, 2 * cells),
            held(*sums.shape, kind=F32),
            held(8, height, channels),
            pltpu.SemaphoreType.DMA((8,)),
        ],
        flops,
        4,
    )
    parts = list(terms)
    for away in (6, 7, 4, 5, 2, 3, 1):
        parts[away] = lax.ppermute(terms[away], ("z", "core"), [(i, i ^ away) for i in range(8)])
    output, input_grad, parts = lax.optimization_barrier((output, input_grad, parts))
    grad = shaped(3, 3, deep, half // 2, kind=F32)
    conv1_grad, conv2_grad = kernel(
        functools.partial(finish_kernel, scale), [smem] + [vmem] * 8, (place, *parts), (grad, grad), [], 10**6, 2
    )
    return (output, input_grad, conv1_grad, conv2_grad)


def is_fast(mesh):
    return dict(mesh.shape) == {"lon": 8, "lat": 4}


def solution(mesh):
    body, lon, lat = local, "lon", "lat"
    if is_fast(mesh):
        lon, lat = ("z", "y"), ("x", "core")
        mesh = jax.sharding.Mesh(mesh.devices.reshape(4, 2, 2, 2), lon + lat)
        body = fast_local
    field, grad = P(lat, lon, None), P(None, None, lon, lat)
    return jax.shard_map(
        body,
        mesh=mesh,
        in_specs=(field, P(), P(), field),
        out_specs=(field, field, grad, grad),
        check_vma=False,
    )
```

```python
import functools

import jax
import jax.numpy as jnp
from jax import lax
from jax.experimental import pallas as pl
from jax.experimental.pallas import tpu as pltpu
from jax.sharding import PartitionSpec as P

F32, BF16 = jnp.float32, jnp.bfloat16


def passed_along(shard, axis, by):
    length = lax.axis_size(axis)
    return lax.ppermute(shard, axis, [(i, (i + by) % length) for i in range(length)])


def padded(shard, sides, width):
    for axis, dim in sides:
        size, length = (lax.axis_size(axis), shard.shape[dim])
        up = [(i, (i + 1) % size) for i in range(size - 1)]
        down = [(j, i) for i, j in up]
        last = lax.slice_in_dim(shard, length - width, length, axis=dim)
        initial = lax.slice_in_dim(shard, 0, width, axis=dim)
        before = lax.ppermute(last, axis, up)
        after = lax.ppermute(initial, axis, down)
        shard = jnp.concatenate([before, shard, after], axis=dim)
    return shard


def extend(field):
    western = passed_along(field, "lon", 1)
    eastern = passed_along(field, "lon", -1)
    widened = jnp.concatenate([western, field, eastern], axis=1)
    return padded(widened, (("lat", 0),), 1)


def windows(padded_field, count_of_rows, lon_width, channels, direction):
    pieces = []
    for lat_step in (-1, 0, 1):
        for longitude_stride in (-1, 0, 1):
            row_start = 1 + direction * lat_step
            column_begin = lon_width + direction * lon_width * longitude_stride
            pieces.append(
                padded_field[
                    row_start : row_start + count_of_rows, column_begin : column_begin + lon_width
                ]
            )
    stacked = jnp.concatenate(pieces, axis=2)
    return stacked.reshape(count_of_rows * lon_width, 9 * channels)


def full_terms(stacked, grad, scale, channels):
    product = lax.dot_general(
        stacked, grad, (((0,), (0,)), ((), ())), preferred_element_type=jnp.float32
    )
    return (product * scale).reshape(9, channels, channels)


def local(inputs, conv1_weight, conv2_weight, cotangent):
    count_of_rows, lon_width, channels = inputs.shape
    cells = count_of_rows * lon_width
    lon_count = lax.axis_size("lon")
    latitude_count = lax.axis_size("lat")
    scale = (count_of_rows * latitude_count * lon_width * lon_count) ** (-0.5)
    forward_one = conv1_weight.reshape(9 * channels, channels)
    forward_two = conv2_weight.reshape(9 * channels, channels)
    turned_one = jnp.swapaxes(conv1_weight, 2, 3).reshape(9 * channels, channels)
    turned_two = jnp.swapaxes(conv2_weight, 2, 3).reshape(9 * channels, channels)
    source_field, cot_field = (inputs, cotangent)

    def stack_of(field, direction):
        return windows(extend(field), count_of_rows, lon_width, channels, direction)

    def as_field(flat):
        return flat.reshape(count_of_rows, lon_width, channels)

    stack_input = stack_of(source_field, 1)
    first = jnp.dot(stack_input, forward_one, preferred_element_type=jnp.float32)
    cdf = 0.5 * (1.0 + jax.scipy.special.erf(first / jnp.sqrt(2.0)))
    hidden = (first * cdf).astype(jnp.bfloat16)
    stack_hidden = stack_of(as_field(hidden), 1)
    second = jnp.dot(stack_hidden, forward_two, preferred_element_type=jnp.float32)
    flat_input = source_field.reshape(cells, channels)
    output = (flat_input.astype(jnp.float32) + second).astype(jnp.bfloat16)
    flat_cot = cot_field.reshape(cells, channels)
    stacked_cotangent = stack_of(cot_field, -1)
    upstream = jnp.dot(stacked_cotangent, turned_two, preferred_element_type=jnp.float32)
    density = jnp.exp(-0.5 * first * first) / jnp.sqrt(2.0 * jnp.pi)
    pre_grad = (upstream * (cdf + first * density)).astype(jnp.bfloat16)
    stack_pre = stack_of(as_field(pre_grad), -1)
    back = jnp.dot(stack_pre, turned_one, preferred_element_type=jnp.float32)
    input_grad = (flat_cot.astype(jnp.float32) + back).astype(jnp.bfloat16)
    output = output.reshape(count_of_rows, lon_width, channels)
    input_grad = input_grad.reshape(count_of_rows, lon_width, channels)
    in_part = channels // lon_count
    out_part = channels // latitude_count
    terms_one = full_terms(stack_input, pre_grad, scale, channels)
    terms_two = full_terms(stack_hidden, flat_cot, scale, channels)
    partly = (
        lax.psum_scatter(terms_one, "lon", scatter_dimension=1, tiled=True),
        lax.psum_scatter(terms_two, "lon", scatter_dimension=1, tiled=True),
    )
    grad_one, grad_two = (
        lax.psum_scatter(partly[0], "lat", scatter_dimension=2, tiled=True),
        lax.psum_scatter(partly[1], "lat", scatter_dimension=2, tiled=True),
    )
    conv1_grad = grad_one.reshape(3, 3, in_part, out_part)
    conv2_grad = grad_two.reshape(3, 3, in_part, out_part)
    return (output, input_grad, conv1_grad, conv2_grad)


def write_stack(field, stack_ref, band, step):
    cells, channels = field.shape
    wide = field.astype(F32)
    place = lax.broadcasted_iota(jnp.int32, (cells, channels), 0) % band
    above = jnp.where(place >= step, pltpu.roll(wide, step, 0), 0.0).astype(BF16)
    below = jnp.where(place < band - step, pltpu.roll(wide, cells - step, 0), 0.0).astype(BF16)
    for at, part in enumerate((above, field, below)):
        columns = slice(at * channels, (at + 1) * channels)
        stack_ref[band : band + cells, columns] = part
        stack_ref[0:band, columns] = part[cells - band :]
        stack_ref[band + cells :, columns] = part[0:band]


def convolved(stack_ref, weight_ref, band, cells, copies):
    total = None
    for b in range(3):
        copies[b].wait()
        channels = weight_ref.shape[2]
        tap = weight_ref[:, b].reshape(3 * channels, channels)
        term = jnp.dot(stack_ref[b * band : b * band + cells, :], tap, preferred_element_type=F32)
        total = term if total is None else total + term
    return total


def convolved_back(stack_ref, weight_ref, band, cells, copies):
    total = None
    for b in range(3):
        copies[b].wait()
        tap = jnp.concatenate([weight_ref[2 - a, 2 - b] for a in range(3)], axis=1)
        term = lax.dot_general(
            stack_ref[b * band : b * band + cells, :],
            tap,
            (((1,), (1,)), ((), ())),
            preferred_element_type=F32,
        )
        total = term if total is None else total + term
    return total


def one_hot_rows(cells, step, devices, back):
    to = lax.broadcasted_iota(jnp.int32, (cells, cells), 1 if back else 0)
    source = lax.broadcasted_iota(jnp.int32, (cells, cells), 0 if back else 1)
    rows = cells // (devices * step)
    device, row, column = to // (rows * step), (to // step) % rows, to % step
    return (source == (row * devices + device) * step + column).astype(BF16)


def deal_kernel(step, inputs_ref, cot_ref, out_ref, held_ref, sems):
    devices, _, rows, channels = out_ref.shape
    cells = devices * rows
    copies = fetched(((inputs_ref, held_ref.at[0]), (cot_ref, held_ref.at[1])), sems)
    chosen = one_hot_rows(cells, step, devices, False)
    for at, copy in enumerate(copies):
        copy.wait()
        field = held_ref[at].reshape(cells, channels)
        dealt = jnp.dot(chosen, field, preferred_element_type=F32).astype(BF16)
        out_ref[:, at] = dealt.reshape(devices, rows, channels)


def gather_kernel(step, fields_ref, output_ref, grad_ref):
    devices, _, rows, channels = fields_ref.shape
    cells = devices * rows
    chosen = one_hot_rows(cells, step, devices, True)
    for at, ref in enumerate((output_ref, grad_ref)):
        field = fields_ref[:, at].reshape(cells, channels)
        ref[...] = jnp.dot(chosen, field, preferred_element_type=F32).astype(BF16).reshape(ref.shape)


def fetched(pairs, sems):
    copies = [pltpu.make_async_copy(source, to, sems.at[at]) for at, (source, to) in enumerate(pairs)]
    for copy in copies:
        copy.start()
    return copies


def by_tap(weight_ref, held_ref, sems, order):
    return fetched([(weight_ref.at[:, b], held_ref.at[:, b]) for b in order], sems)


def inner_kernel(band, step, place_ref, own_ref, one_ref, two_ref,
                 hidden_ref, pre_ref, mine_ref, give_ref,
                 one_held, two_held, stack_ref, first_ref, slope_ref, turned_ref, sems):
    x, y, core = place_ref[0], place_ref[1], place_ref[2]
    cells, channels = first_ref.shape
    first_weight = by_tap(one_ref, one_held, sems.at[0], range(3))
    half, rows = channels // 2, 32
    deep = half // 4

    def turn(at, field):
        turned = field.T
        for h in range(2):
            for z in range(4):
                begin = (2 * z + h) * deep if at < 2 else h * half + z * deep
                turned_ref[at * 2 + h, z * deep : (z + 1) * deep, :] = turned[begin : begin + deep]

    source = own_ref[:, 0].reshape(cells, channels)
    write_stack(source, stack_ref, band, step)
    first_ref[...] = convolved(stack_ref, one_held, band, cells, first_weight)
    second_weight = by_tap(two_ref, two_held, sems.at[1], (2, 1, 0))
    turn(0, source)

    def activate(at, carry):
        span = pl.ds(pl.multiple_of(at * rows, rows), rows)
        first = first_ref[span, :]
        cdf = 0.5 * (1.0 + lax.erf(first * (0.5**0.5)))
        density = jnp.exp(-0.5 * first * first) * ((2.0 * jnp.pi) ** -0.5)
        hidden_ref[span, :] = (first * cdf).astype(BF16)
        slope_ref[span, :] = cdf + first * density
        return carry

    lax.fori_loop(0, cells // rows, activate, 0)
    turn(1, hidden_ref[...])
    cot = own_ref[:, 1].reshape(cells, channels)
    write_stack(cot, stack_ref, band, step)
    turn(3, cot)
    pre_ref[...] = (slope_ref[...] * convolved_back(stack_ref, two_held, band, cells, second_weight)).astype(BF16)
    turn(2, pre_ref[...])

    for ref, of in ((mine_ref, core), (give_ref, 1 - core)):
        ref[0] = turned_ref[of * 2 + 1 - y]
        ref[1] = turned_ref[of * 2 + y]
        ref[2] = turned_ref[4 + of * 2 + 1 - x]
        ref[3] = turned_ref[4 + of * 2 + x]


def join_kernel(mine_ref, got_ref, x_ref, y_ref):
    for at, ref in enumerate((mine_ref, got_ref)):
        y_ref[at] = ref[0]
        x_ref[2 + at] = ref[1]
        x_ref[at] = ref[2]
        y_ref[2 + at] = ref[3]


def outer_kernel(band, step, own_ref, hidden_ref, pre_ref, one_ref, two_ref, out_ref,
                 one_held, two_held, stack_ref, sems):
    cells, channels = hidden_ref.shape
    shape = (out_ref.shape[0],) + out_ref.shape[2:]
    second_weight = by_tap(two_ref, two_held, sems.at[1], range(3))
    write_stack(hidden_ref[...], stack_ref, band, step)
    second = convolved(stack_ref, two_held, band, cells, second_weight)
    first_weight = by_tap(one_ref, one_held, sems.at[0], (2, 1, 0))
    source = own_ref[:, 0].reshape(cells, channels)
    out_ref[:, 0] = (source.astype(F32) + second).astype(BF16).reshape(shape)
    write_stack(pre_ref[...], stack_ref, band, step)
    back = convolved_back(stack_ref, one_held, band, cells, first_weight)
    cot = own_ref[:, 1].reshape(cells, channels)
    out_ref[:, 1] = (cot.astype(F32) + back).astype(BF16).reshape(shape)


def units(deep):
    count = deep // 16
    for unit in range(9 * count):
        yield unit // count, (unit % count) * 16, (unit // 4) * 16, unit % 4


def summed(band, step, lefts, rights, turned_ref, moved_ref, b):
    half, cells = lefts[0].shape
    if b == 0:
        place = lax.broadcasted_iota(jnp.int32, (half, cells), 1) % band
        for at, (left_ref, right_ref) in enumerate(zip(lefts, rights)):
            columns = slice(at * cells, (at + 1) * cells)
            field = left_ref[...]
            wide = field.astype(F32)
            turned_ref[0:half, columns] = jnp.where(place >= step, pltpu.roll(wide, step, 1), 0.0).astype(BF16)
            turned_ref[half : 2 * half, columns] = field
            turned_ref[2 * half :, columns] = jnp.where(
                place < band - step, pltpu.roll(wide, cells - step, 1), 0.0
            ).astype(BF16)
            grad = right_ref[...]
            wide = grad.astype(F32)
            moved_ref[0, :, columns] = pltpu.roll(wide, cells - band, 1).astype(BF16)
            moved_ref[1, :, columns] = grad
            moved_ref[2, :, columns] = pltpu.roll(wide, band, 1).astype(BF16)
    return lax.dot_general(turned_ref[...], moved_ref[b], (((1,), (1,)), ((), ())), preferred_element_type=F32)


def near_kernel(band, step, x_ref, y_ref, x_got_ref, y_got_ref, sums_ref, turned_ref, moved_ref):
    lefts = [x_ref.at[2], x_ref.at[3], x_got_ref.at[2], x_got_ref.at[3], y_got_ref.at[0], y_got_ref.at[1]]
    rights = [y_ref.at[2], y_ref.at[3], x_got_ref.at[0], x_got_ref.at[1], y_got_ref.at[2], y_got_ref.at[3]]
    for b in range(3):
        sums_ref[b] = summed(band, step, lefts, rights, turned_ref, moved_ref, b)


def far_kernel(band, step, place_ref, near_ref, left_ref, right_ref, *refs):
    out_refs, (turned_ref, moved_ref, sums_ref, send_ref, sems) = refs[:-5], refs[-5:]
    me = place_ref[3] * 2 + place_ref[2]
    half = left_ref.shape[1]
    lefts, rights = ([ref.at[at] for at in range(2)] for ref in (left_ref, right_ref))
    for b in range(3):
        sums_ref[b] = near_ref[b] + summed(band, step, lefts, rights, turned_ref, moved_ref, b)
    deep, quarter = half // 4, half // 2
    height = send_ref.shape[1]
    for z in range(4):
        for core in range(2):
            blocks = [[] for _ in range(height // 16)]
            for tap, row, to, _ in units(deep):
                begin = (tap // 3) * half + z * deep + row
                blocks[to // 16].append(
                    sums_ref[tap % 3, begin : begin + 16, core * quarter : (core + 1) * quarter]
                )
            for to, parts in enumerate(blocks):
                while len(parts) < 4:
                    parts.append(jnp.zeros((16, quarter), F32))
                send_ref[z * 2 + core, to * 16 : (to + 1) * 16, :] = jnp.concatenate(parts, axis=1).astype(BF16)
    pairs = [(send_ref.at[me ^ away], ref) for away, ref in enumerate(out_refs)]
    for copy in fetched(pairs, sems):
        copy.wait()


def finish_kernel(scale, place_ref, *refs):
    parts, (one_ref, two_ref) = refs[:-2], refs[-2:]
    core = place_ref[2]
    deep, quarter = one_ref.shape[2:]
    sums = []
    for other in range(2):
        total = parts[other][...].astype(F32)
        for ref in parts[other + 2 :: 2]:
            total = total + ref[...].astype(F32)
        sums.append(total * scale)
    ours, theirs = sums
    for out_ref, total in (
        (one_ref, jnp.where(core == 0, ours, theirs)),
        (two_ref, jnp.where(core == 0, theirs, ours)),
    ):
        for tap, row, begin, slot in units(deep):
            out_ref[tap // 3, tap % 3, row : row + 16, :] = total[
                begin : begin + 16, slot * quarter : (slot + 1) * quarter
            ]


def fast_local(inputs, conv1_weight, conv2_weight, cotangent):
    rows, width, channels = inputs.shape
    every = ("z", "y", "x", "core")
    devices = lax.axis_size(every)
    step = width // devices
    cells = rows * width
    lat = lax.axis_size("x") * lax.axis_size("core")
    lon = devices // lat
    band = rows * lat * step
    half, deep = channels // 2, channels // lon
    height = -(-9 * (deep // 16) // 4) * 16
    scale = (rows * lat * width * lon) ** (-0.5)
    flops = 2 * 9 * cells * channels * channels
    vmem, hbm, smem = (pl.BlockSpec(memory_space=space) for space in (pltpu.VMEM, pltpu.HBM, pltpu.SMEM))

    def held(*shape, kind=BF16):
        return pltpu.VMEM(shape, kind)

    def shaped(*shape, kind=BF16):
        return jax.ShapeDtypeStruct(shape, kind)

    def kernel(body, specs, arguments, out_shape, scratch_shapes, work, megabytes):
        return pl.pallas_call(
            body,
            out_shape=out_shape,
            in_specs=specs,
            out_specs=jax.tree.map(lambda _: vmem, out_shape),
            scratch_shapes=scratch_shapes,
            compiler_params=pltpu.CompilerParams(vmem_limit_bytes=20 * 2**20),
            cost_estimate=pl.CostEstimate(flops=work, bytes_accessed=megabytes * 2**20, transcendentals=0),
        )(*arguments)

    def passed(piece, x, y, core):
        pairs = [(i, i ^ (4 * y + 2 * x + core)) for i in range(8)]
        return lax.ppermute(piece, ("y", "x", "core"), pairs)

    stack = held(cells + 2 * band, 3 * channels)
    weights = held(*conv1_weight.shape)
    dealt = shaped(devices, 2, rows * step, channels)
    own = kernel(
        functools.partial(deal_kernel, step),
        [hbm] * 2,
        [pltpu.with_memory_space_constraint(field, pltpu.HBM) for field in (inputs, cotangent)],
        dealt,
        [held(2, *inputs.shape), pltpu.SemaphoreType.DMA((2,))],
        10**9,
        3,
    )
    own = lax.all_to_all(own, every, 0, 0, tiled=True)
    place = jnp.stack([lax.axis_index(axis) for axis in ("x", "y", "core", "z")]).astype(jnp.int32)
    one, two = (pltpu.with_memory_space_constraint(w, pltpu.HBM) for w in (conv1_weight, conv2_weight))
    taps = pltpu.SemaphoreType.DMA((2, 3))
    pieces = held(4, half, cells)
    hidden, pre_grad, mine, give = kernel(
        functools.partial(inner_kernel, band, step),
        [smem, vmem, hbm, hbm],
        (place, own, one, two),
        (held(cells, channels), held(cells, channels), pieces, pieces),
        [
            weights,
            weights,
            stack,
            held(cells, channels, kind=F32),
            held(cells, channels, kind=F32),
            held(8, half, cells),
            taps,
        ],
        2 * flops,
        10,
    )
    x_given, y_given = kernel(
        join_kernel, [vmem] * 2, (mine, passed(give, 0, 0, 1)), (pieces, pieces), [], 10**6, 4
    )
    x_got, y_got = passed(x_given, 1, 0, 0), passed(y_given, 0, 1, 0)
    hidden, pre_grad, x_given = lax.optimization_barrier((hidden, pre_grad, x_given))
    fields = kernel(
        functools.partial(outer_kernel, band, step),
        [vmem] * 3 + [hbm] * 2,
        (own, hidden, pre_grad, one, two),
        dealt,
        [weights, weights, stack, taps],
        2 * flops,
        9,
    )
    fields, x_got, y_got = lax.optimization_barrier((fields, x_got, y_got))
    far = (passed(y_got[:2], 1, 0, 0), passed(x_got[:2], 0, 1, 0))
    fields = lax.all_to_all(fields, every, 0, 0, tiled=True)
    output, input_grad = kernel(
        functools.partial(gather_kernel, step), [vmem], (fields,), (shaped(*inputs.shape),) * 2, [], 10**9, 3
    )
    sums = shaped(3, 3 * half, half, kind=F32)
    near = kernel(
        functools.partial(near_kernel, band, step),
        [vmem] * 4,
        (x_given, y_given, x_got, y_got),
        sums,
        [held(3 * half, 6 * cells), held(3, half, 6 * cells)],
        5 * flops,
        6,
    )
    terms = kernel(
        functools.partial(far_kernel, band, step),
        [smem] + [vmem] * 3,
        (place, near) + far,
        (pltpu.VMEM((height, channels), BF16),) * 8,
        [
            held(3 * half, 2 * cells),
            held(3, half, 2 * cells),
            held(*sums.shape, kind=F32),
            held(8, height, channels),
            pltpu.SemaphoreType.DMA((8,)),
        ],
        5 * flops,
        4,
    )
    parts = list(terms)
    for away in (6, 7, 4, 5, 2, 3, 1):
        parts[away] = lax.ppermute(terms[away], ("z", "core"), [(i, i ^ away) for i in range(8)])
    output, input_grad, parts = lax.optimization_barrier((output, input_grad, parts))
    grad = shaped(3, 3, deep, half // 2, kind=F32)
    conv1_grad, conv2_grad = kernel(
        functools.partial(finish_kernel, scale), [smem] + [vmem] * 8, (place, *parts), (grad, grad), [], 10**6, 2
    )
    return (output, input_grad, conv1_grad, conv2_grad)


def is_fast(mesh):
    return dict(mesh.shape) == {"lon": 8, "lat": 4}


def solution(mesh):
    body, lon, lat = local, "lon", "lat"
    if is_fast(mesh):
        lon, lat = ("z", "y"), ("x", "core")
        mesh = jax.sharding.Mesh(mesh.devices.reshape(4, 2, 2, 2), lon + lat)
        body = fast_local
    field, grad = P(lat, lon, None), P(None, None, lon, lat)
    return jax.shard_map(
        body,
        mesh=mesh,
        in_specs=(field, P(), P(), field),
        out_specs=(field, field, grad, grad),
        check_vma=False,
    )
```

```python
import functools

import jax
import jax.numpy as jnp
from jax import lax
from jax.experimental import pallas as pl
from jax.experimental.pallas import tpu as pltpu
from jax.sharding import PartitionSpec as P

F32, BF16 = jnp.float32, jnp.bfloat16


def passed_along(shard, axis, by):
    length = lax.axis_size(axis)
    return lax.ppermute(shard, axis, [(i, (i + by) % length) for i in range(length)])


def padded(shard, sides, width):
    for axis, dim in sides:
        size, length = (lax.axis_size(axis), shard.shape[dim])
        up = [(i, (i + 1) % size) for i in range(size - 1)]
        down = [(j, i) for i, j in up]
        last = lax.slice_in_dim(shard, length - width, length, axis=dim)
        initial = lax.slice_in_dim(shard, 0, width, axis=dim)
        before = lax.ppermute(last, axis, up)
        after = lax.ppermute(initial, axis, down)
        shard = jnp.concatenate([before, shard, after], axis=dim)
    return shard


def extend(field):
    western = passed_along(field, "lon", 1)
    eastern = passed_along(field, "lon", -1)
    widened = jnp.concatenate([western, field, eastern], axis=1)
    return padded(widened, (("lat", 0),), 1)


def windows(padded_field, count_of_rows, lon_width, channels, direction):
    pieces = []
    for lat_step in (-1, 0, 1):
        for longitude_stride in (-1, 0, 1):
            row_start = 1 + direction * lat_step
            column_begin = lon_width + direction * lon_width * longitude_stride
            pieces.append(
                padded_field[
                    row_start : row_start + count_of_rows, column_begin : column_begin + lon_width
                ]
            )
    stacked = jnp.concatenate(pieces, axis=2)
    return stacked.reshape(count_of_rows * lon_width, 9 * channels)


def full_terms(stacked, grad, scale, channels):
    product = lax.dot_general(
        stacked, grad, (((0,), (0,)), ((), ())), preferred_element_type=jnp.float32
    )
    return (product * scale).reshape(9, channels, channels)


def local(inputs, conv1_weight, conv2_weight, cotangent):
    count_of_rows, lon_width, channels = inputs.shape
    cells = count_of_rows * lon_width
    lon_count = lax.axis_size("lon")
    latitude_count = lax.axis_size("lat")
    scale = (count_of_rows * latitude_count * lon_width * lon_count) ** (-0.5)
    forward_one = conv1_weight.reshape(9 * channels, channels)
    forward_two = conv2_weight.reshape(9 * channels, channels)
    turned_one = jnp.swapaxes(conv1_weight, 2, 3).reshape(9 * channels, channels)
    turned_two = jnp.swapaxes(conv2_weight, 2, 3).reshape(9 * channels, channels)
    source_field, cot_field = (inputs, cotangent)

    def stack_of(field, direction):
        return windows(extend(field), count_of_rows, lon_width, channels, direction)

    def as_field(flat):
        return flat.reshape(count_of_rows, lon_width, channels)

    stack_input = stack_of(source_field, 1)
    first = jnp.dot(stack_input, forward_one, preferred_element_type=jnp.float32)
    cdf = 0.5 * (1.0 + jax.scipy.special.erf(first / jnp.sqrt(2.0)))
    hidden = (first * cdf).astype(jnp.bfloat16)
    stack_hidden = stack_of(as_field(hidden), 1)
    second = jnp.dot(stack_hidden, forward_two, preferred_element_type=jnp.float32)
    flat_input = source_field.reshape(cells, channels)
    output = (flat_input.astype(jnp.float32) + second).astype(jnp.bfloat16)
    flat_cot = cot_field.reshape(cells, channels)
    stacked_cotangent = stack_of(cot_field, -1)
    upstream = jnp.dot(stacked_cotangent, turned_two, preferred_element_type=jnp.float32)
    density = jnp.exp(-0.5 * first * first) / jnp.sqrt(2.0 * jnp.pi)
    pre_grad = (upstream * (cdf + first * density)).astype(jnp.bfloat16)
    stack_pre = stack_of(as_field(pre_grad), -1)
    back = jnp.dot(stack_pre, turned_one, preferred_element_type=jnp.float32)
    input_grad = (flat_cot.astype(jnp.float32) + back).astype(jnp.bfloat16)
    output = output.reshape(count_of_rows, lon_width, channels)
    input_grad = input_grad.reshape(count_of_rows, lon_width, channels)
    in_part = channels // lon_count
    out_part = channels // latitude_count
    terms_one = full_terms(stack_input, pre_grad, scale, channels)
    terms_two = full_terms(stack_hidden, flat_cot, scale, channels)
    partly = (
        lax.psum_scatter(terms_one, "lon", scatter_dimension=1, tiled=True),
        lax.psum_scatter(terms_two, "lon", scatter_dimension=1, tiled=True),
    )
    grad_one, grad_two = (
        lax.psum_scatter(partly[0], "lat", scatter_dimension=2, tiled=True),
        lax.psum_scatter(partly[1], "lat", scatter_dimension=2, tiled=True),
    )
    conv1_grad = grad_one.reshape(3, 3, in_part, out_part)
    conv2_grad = grad_two.reshape(3, 3, in_part, out_part)
    return (output, input_grad, conv1_grad, conv2_grad)


def write_stack(field, stack_ref, band, step):
    cells, channels = field.shape
    wide = field.astype(F32)
    place = lax.broadcasted_iota(jnp.int32, (cells, channels), 0) % band
    above = jnp.where(place >= step, pltpu.roll(wide, step, 0), 0.0).astype(BF16)
    below = jnp.where(place < band - step, pltpu.roll(wide, cells - step, 0), 0.0).astype(BF16)
    for at, part in enumerate((above, field, below)):
        columns = slice(at * channels, (at + 1) * channels)
        stack_ref[band : band + cells, columns] = part
        stack_ref[0:band, columns] = part[cells - band :]
        stack_ref[band + cells :, columns] = part[0:band]


def convolved(stack_ref, weight_ref, band, cells):
    total = None
    for b in range(3):
        channels = weight_ref.shape[2]
        tap = weight_ref[:, b].reshape(3 * channels, channels)
        term = jnp.dot(stack_ref[b * band : b * band + cells, :], tap, preferred_element_type=F32)
        total = term if total is None else total + term
    return total


def convolved_back(stack_ref, weight_ref, band, cells):
    total = None
    for b in range(3):
        tap = jnp.concatenate([weight_ref[2 - a, 2 - b] for a in range(3)], axis=1)
        term = lax.dot_general(
            stack_ref[b * band : b * band + cells, :],
            tap,
            (((1,), (1,)), ((), ())),
            preferred_element_type=F32,
        )
        total = term if total is None else total + term
    return total


def one_hot_rows(cells, step, devices, back):
    to = lax.broadcasted_iota(jnp.int32, (cells, cells), 1 if back else 0)
    source = lax.broadcasted_iota(jnp.int32, (cells, cells), 0 if back else 1)
    rows = cells // (devices * step)
    device, row, column = to // (rows * step), (to // step) % rows, to % step
    return (source == (row * devices + device) * step + column).astype(BF16)


def deal_kernel(step, inputs_ref, cot_ref, out_ref, held_ref, sems):
    devices, _, rows, channels = out_ref.shape
    cells = devices * rows
    copies = fetched(((inputs_ref, held_ref.at[0]), (cot_ref, held_ref.at[1])), sems)
    chosen = one_hot_rows(cells, step, devices, False)
    for at, copy in enumerate(copies):
        copy.wait()
        field = held_ref[at].reshape(cells, channels)
        dealt = jnp.dot(chosen, field, preferred_element_type=F32).astype(BF16)
        out_ref[:, at] = dealt.reshape(devices, rows, channels)


def gather_kernel(step, fields_ref, output_ref, grad_ref):
    devices, _, rows, channels = fields_ref.shape
    cells = devices * rows
    chosen = one_hot_rows(cells, step, devices, True)
    for at, ref in enumerate((output_ref, grad_ref)):
        field = fields_ref[:, at].reshape(cells, channels)
        ref[...] = jnp.dot(chosen, field, preferred_element_type=F32).astype(BF16).reshape(ref.shape)


def fetched(pairs, sems):
    copies = [pltpu.make_async_copy(source, to, sems.at[at]) for at, (source, to) in enumerate(pairs)]
    for copy in copies:
        copy.start()
    return copies


def inner_kernel(band, step, place_ref, own_ref, one_ref, two_ref,
                 hidden_ref, pre_ref, mine_ref, give_ref,
                 one_held, two_held, stack_ref, cot_stack_ref, first_ref, up_ref, slope_ref, turned_ref, sems):
    x, y, core = place_ref[0], place_ref[1], place_ref[2]
    cells, channels = first_ref.shape
    fetch = fetched(((one_ref, one_held),), sems.at[0])
    half, rows = channels // 2, 32
    deep = half // 4

    def turn(at, field):
        turned = field.T
        for h in range(2):
            for z in range(4):
                begin = (2 * z + h) * deep if at < 2 else h * half + z * deep
                turned_ref[at * 2 + h, z * deep : (z + 1) * deep, :] = turned[begin : begin + deep]

    source = own_ref[:, 0].reshape(cells, channels)
    write_stack(source, stack_ref, band, step)
    fetch[0].wait()
    later = fetched(((two_ref, two_held),), sems.at[1])[0]
    first_ref[...] = convolved(stack_ref, one_held, band, cells)
    cot = own_ref[:, 1].reshape(cells, channels)
    write_stack(cot, cot_stack_ref, band, step)
    turn(0, source)
    turn(3, cot)
    later.wait()
    up_ref[...] = convolved_back(cot_stack_ref, two_held, band, cells)
    for begin in range(0, cells, rows):
        span = slice(begin, begin + rows)
        first = first_ref[span, :]
        cdf = 0.5 * (1.0 + lax.erf(first * (0.5**0.5)))
        density = jnp.exp(-0.5 * first * first) * ((2.0 * jnp.pi) ** -0.5)
        hidden_ref[span, :] = (first * cdf).astype(BF16)
        slope_ref[span, :] = cdf + first * density
    turn(1, hidden_ref[...])
    pre_ref[...] = (slope_ref[...] * up_ref[...]).astype(BF16)
    turn(2, pre_ref[...])

    for ref, of in ((mine_ref, core), (give_ref, 1 - core)):
        ref[0] = turned_ref[of * 2 + 1 - y]
        ref[1] = turned_ref[of * 2 + y]
        ref[2] = turned_ref[4 + of * 2 + 1 - x]
        ref[3] = turned_ref[4 + of * 2 + x]


def join_kernel(mine_ref, got_ref, x_ref, y_ref):
    for at, ref in enumerate((mine_ref, got_ref)):
        y_ref[at] = ref[0]
        x_ref[2 + at] = ref[1]
        x_ref[at] = ref[2]
        y_ref[2 + at] = ref[3]


def outer_kernel(band, step, own_ref, hidden_ref, pre_ref, one_ref, two_ref, out_ref,
                 one_held, two_held, stack_ref, sems):
    cells, channels = hidden_ref.shape
    shape = (out_ref.shape[0],) + out_ref.shape[2:]
    fetch = fetched(((two_ref, two_held),), sems.at[1])[0]
    later = fetched(((one_ref, one_held),), sems.at[0])[0]
    write_stack(hidden_ref[...], stack_ref, band, step)
    fetch.wait()
    second = convolved(stack_ref, two_held, band, cells)
    source = own_ref[:, 0].reshape(cells, channels)
    out_ref[:, 0] = (source.astype(F32) + second).astype(BF16).reshape(shape)
    write_stack(pre_ref[...], stack_ref, band, step)
    later.wait()
    back = convolved_back(stack_ref, one_held, band, cells)
    cot = own_ref[:, 1].reshape(cells, channels)
    out_ref[:, 1] = (cot.astype(F32) + back).astype(BF16).reshape(shape)


def units(deep):
    count = deep // 16
    for unit in range(9 * count):
        yield unit // count, (unit % count) * 16, (unit // 4) * 16, unit % 4


def summed(band, step, lefts, rights, turned_ref, moved_ref, b):
    half, cells = lefts[0].shape
    if b == 0:
        place = lax.broadcasted_iota(jnp.int32, (half, cells), 1) % band
        for at, (left_ref, right_ref) in enumerate(zip(lefts, rights)):
            columns = slice(at * cells, (at + 1) * cells)
            field = left_ref[...]
            wide = field.astype(F32)
            turned_ref[0:half, columns] = jnp.where(place >= step, pltpu.roll(wide, step, 1), 0.0).astype(BF16)
            turned_ref[half : 2 * half, columns] = field
            turned_ref[2 * half :, columns] = jnp.where(
                place < band - step, pltpu.roll(wide, cells - step, 1), 0.0
            ).astype(BF16)
            grad = right_ref[...]
            wide = grad.astype(F32)
            moved_ref[0, :, columns] = pltpu.roll(wide, cells - band, 1).astype(BF16)
            moved_ref[1, :, columns] = grad
            moved_ref[2, :, columns] = pltpu.roll(wide, band, 1).astype(BF16)
    return lax.dot_general(turned_ref[...], moved_ref[b], (((1,), (1,)), ((), ())), preferred_element_type=F32)


def near_kernel(band, step, x_ref, y_ref, x_got_ref, y_got_ref, sums_ref, turned_ref, moved_ref):
    lefts = [x_ref.at[2], x_ref.at[3], x_got_ref.at[2], x_got_ref.at[3], y_got_ref.at[0], y_got_ref.at[1]]
    rights = [y_ref.at[2], y_ref.at[3], x_got_ref.at[0], x_got_ref.at[1], y_got_ref.at[2], y_got_ref.at[3]]
    for b in range(3):
        sums_ref[b] = summed(band, step, lefts, rights, turned_ref, moved_ref, b)


def far_kernel(band, step, place_ref, near_ref, left_ref, right_ref, *refs):
    out_refs, (turned_ref, moved_ref, sums_ref, send_ref, sems) = refs[:-5], refs[-5:]
    me = place_ref[3] * 2 + place_ref[2]
    half = left_ref.shape[1]
    lefts, rights = ([ref.at[at] for at in range(2)] for ref in (left_ref, right_ref))
    for b in range(3):
        sums_ref[b] = near_ref[b] + summed(band, step, lefts, rights, turned_ref, moved_ref, b)
    deep, quarter = half // 4, half // 2
    height = send_ref.shape[1]
    for z in range(4):
        for core in range(2):
            blocks = [[] for _ in range(height // 16)]
            for tap, row, to, _ in units(deep):
                begin = (tap // 3) * half + z * deep + row
                blocks[to // 16].append(
                    sums_ref[tap % 3, begin : begin + 16, core * quarter : (core + 1) * quarter]
                )
            for to, parts in enumerate(blocks):
                while len(parts) < 4:
                    parts.append(jnp.zeros((16, quarter), F32))
                send_ref[z * 2 + core, to * 16 : (to + 1) * 16, :] = jnp.concatenate(parts, axis=1).astype(BF16)
    pairs = [(send_ref.at[me ^ away], ref) for away, ref in enumerate(out_refs)]
    for copy in fetched(pairs, sems):
        copy.wait()


def finish_kernel(scale, place_ref, *refs):
    parts, (one_ref, two_ref) = refs[:-2], refs[-2:]
    core = place_ref[2]
    deep, quarter = one_ref.shape[2:]
    sums = []
    for other in range(2):
        total = parts[other][...].astype(F32)
        for ref in parts[other + 2 :: 2]:
            total = total + ref[...].astype(F32)
        sums.append(total * scale)
    ours, theirs = sums
    for out_ref, total in (
        (one_ref, jnp.where(core == 0, ours, theirs)),
        (two_ref, jnp.where(core == 0, theirs, ours)),
    ):
        for tap, row, begin, slot in units(deep):
            out_ref[tap // 3, tap % 3, row : row + 16, :] = total[
                begin : begin + 16, slot * quarter : (slot + 1) * quarter
            ]


def fast_local(inputs, conv1_weight, conv2_weight, cotangent):
    rows, width, channels = inputs.shape
    every = ("z", "y", "x", "core")
    devices = lax.axis_size(every)
    step = width // devices
    cells = rows * width
    lat = lax.axis_size("x") * lax.axis_size("core")
    lon = devices // lat
    band = rows * lat * step
    half, deep = channels // 2, channels // lon
    height = -(-9 * (deep // 16) // 4) * 16
    scale = (rows * lat * width * lon) ** (-0.5)
    flops = 2 * 9 * cells * channels * channels
    vmem, hbm, smem = (pl.BlockSpec(memory_space=space) for space in (pltpu.VMEM, pltpu.HBM, pltpu.SMEM))

    def held(*shape, kind=BF16):
        return pltpu.VMEM(shape, kind)

    def shaped(*shape, kind=BF16):
        return jax.ShapeDtypeStruct(shape, kind)

    def kernel(body, specs, arguments, out_shape, scratch_shapes, work, megabytes):
        return pl.pallas_call(
            body,
            out_shape=out_shape,
            in_specs=specs,
            out_specs=jax.tree.map(lambda _: vmem, out_shape),
            scratch_shapes=scratch_shapes,
            compiler_params=pltpu.CompilerParams(vmem_limit_bytes=20 * 2**20),
            cost_estimate=pl.CostEstimate(flops=work, bytes_accessed=megabytes * 2**20, transcendentals=0),
        )(*arguments)

    def passed(piece, x, y, core):
        pairs = [(i, i ^ (4 * y + 2 * x + core)) for i in range(8)]
        return lax.ppermute(piece, ("y", "x", "core"), pairs)

    stack = held(cells + 2 * band, 3 * channels)
    weights = held(*conv1_weight.shape)
    dealt = shaped(devices, 2, rows * step, channels)
    own = kernel(
        functools.partial(deal_kernel, step),
        [hbm] * 2,
        [pltpu.with_memory_space_constraint(field, pltpu.HBM) for field in (inputs, cotangent)],
        dealt,
        [held(2, *inputs.shape), pltpu.SemaphoreType.DMA((2,))],
        10**9,
        3,
    )
    own = lax.all_to_all(own, every, 0, 0, tiled=True)
    place = jnp.stack([lax.axis_index(axis) for axis in ("x", "y", "core", "z")]).astype(jnp.int32)
    one, two = (pltpu.with_memory_space_constraint(w, pltpu.HBM) for w in (conv1_weight, conv2_weight))
    taps = pltpu.SemaphoreType.DMA((2, 1))
    pieces = held(4, half, cells)
    hidden, pre_grad, mine, give = kernel(
        functools.partial(inner_kernel, band, step),
        [smem, vmem, hbm, hbm],
        (place, own, one, two),
        (held(cells, channels), held(cells, channels), pieces, pieces),
        [
            weights,
            weights,
            stack,
            stack,
            held(cells, channels, kind=F32),
            held(cells, channels, kind=F32),
            held(cells, channels, kind=F32),
            held(8, half, cells),
            taps,
        ],
        2 * flops,
        10,
    )
    x_given, y_given = kernel(
        join_kernel, [vmem] * 2, (mine, passed(give, 0, 0, 1)), (pieces, pieces), [], 10**6, 4
    )
    x_got, y_got = passed(x_given, 1, 0, 0), passed(y_given, 0, 1, 0)
    hidden, pre_grad, x_given = lax.optimization_barrier((hidden, pre_grad, x_given))
    fields = kernel(
        functools.partial(outer_kernel, band, step),
        [vmem] * 3 + [hbm] * 2,
        (own, hidden, pre_grad, one, two),
        dealt,
        [weights, weights, stack, taps],
        2 * flops,
        9,
    )
    fields, x_got, y_got = lax.optimization_barrier((fields, x_got, y_got))
    far = (passed(y_got[:2], 1, 0, 0), passed(x_got[:2], 0, 1, 0))
    fields = lax.all_to_all(fields, every, 0, 0, tiled=True)
    output, input_grad = kernel(
        functools.partial(gather_kernel, step), [vmem], (fields,), (shaped(*inputs.shape),) * 2, [], 10**9, 3
    )
    sums = shaped(3, 3 * half, half, kind=F32)
    near = kernel(
        functools.partial(near_kernel, band, step),
        [vmem] * 4,
        (x_given, y_given, x_got, y_got),
        sums,
        [held(3 * half, 6 * cells), held(3, half, 6 * cells)],
        3 * flops,
        6,
    )
    terms = kernel(
        functools.partial(far_kernel, band, step),
        [smem] + [vmem] * 3,
        (place, near) + far,
        (pltpu.VMEM((height, channels), BF16),) * 8,
        [
            held(3 * half, 2 * cells),
            held(3, half, 2 * cells),
            held(*sums.shape, kind=F32),
            held(8, height, channels),
            pltpu.SemaphoreType.DMA((8,)),
        ],
        3 * flops,
        4,
    )
    parts = list(terms)
    for away in (6, 7, 4, 5, 2, 3, 1):
        parts[away] = lax.ppermute(terms[away], ("z", "core"), [(i, i ^ away) for i in range(8)])
    output, input_grad, parts = lax.optimization_barrier((output, input_grad, parts))
    grad = shaped(3, 3, deep, half // 2, kind=F32)
    conv1_grad, conv2_grad = kernel(
        functools.partial(finish_kernel, scale), [smem] + [vmem] * 8, (place, *parts), (grad, grad), [], 10**6, 2
    )
    return (output, input_grad, conv1_grad, conv2_grad)


def is_fast(mesh):
    return dict(mesh.shape) == {"lon": 8, "lat": 4}


def solution(mesh):
    body, lon, lat = local, "lon", "lat"
    if is_fast(mesh):
        lon, lat = ("z", "y"), ("x", "core")
        mesh = jax.sharding.Mesh(mesh.devices.reshape(4, 2, 2, 2), lon + lat)
        body = fast_local
    field, grad = P(lat, lon, None), P(None, None, lon, lat)
    return jax.shard_map(
        body,
        mesh=mesh,
        in_specs=(field, P(), P(), field),
        out_specs=(field, field, grad, grad),
        check_vma=False,
    )
```

```python
import functools

import jax
import jax.numpy as jnp
from jax import lax
from jax.experimental import pallas as pl
from jax.experimental.pallas import tpu as pltpu
from jax.sharding import PartitionSpec as P

F32, BF16 = jnp.float32, jnp.bfloat16


def passed_along(shard, axis, by):
    length = lax.axis_size(axis)
    return lax.ppermute(shard, axis, [(i, (i + by) % length) for i in range(length)])


def padded(shard, sides, width):
    for axis, dim in sides:
        size, length = (lax.axis_size(axis), shard.shape[dim])
        up = [(i, (i + 1) % size) for i in range(size - 1)]
        down = [(j, i) for i, j in up]
        last = lax.slice_in_dim(shard, length - width, length, axis=dim)
        initial = lax.slice_in_dim(shard, 0, width, axis=dim)
        before = lax.ppermute(last, axis, up)
        after = lax.ppermute(initial, axis, down)
        shard = jnp.concatenate([before, shard, after], axis=dim)
    return shard


def extend(field):
    western = passed_along(field, "lon", 1)
    eastern = passed_along(field, "lon", -1)
    widened = jnp.concatenate([western, field, eastern], axis=1)
    return padded(widened, (("lat", 0),), 1)


def windows(padded_field, count_of_rows, lon_width, channels, direction):
    pieces = []
    for lat_step in (-1, 0, 1):
        for longitude_stride in (-1, 0, 1):
            row_start = 1 + direction * lat_step
            column_begin = lon_width + direction * lon_width * longitude_stride
            pieces.append(
                padded_field[
                    row_start : row_start + count_of_rows, column_begin : column_begin + lon_width
                ]
            )
    stacked = jnp.concatenate(pieces, axis=2)
    return stacked.reshape(count_of_rows * lon_width, 9 * channels)


def full_terms(stacked, grad, scale, channels):
    product = lax.dot_general(
        stacked, grad, (((0,), (0,)), ((), ())), preferred_element_type=jnp.float32
    )
    return (product * scale).reshape(9, channels, channels)


def local(inputs, conv1_weight, conv2_weight, cotangent):
    count_of_rows, lon_width, channels = inputs.shape
    cells = count_of_rows * lon_width
    lon_count = lax.axis_size("lon")
    latitude_count = lax.axis_size("lat")
    scale = (count_of_rows * latitude_count * lon_width * lon_count) ** (-0.5)
    forward_one = conv1_weight.reshape(9 * channels, channels)
    forward_two = conv2_weight.reshape(9 * channels, channels)
    turned_one = jnp.swapaxes(conv1_weight, 2, 3).reshape(9 * channels, channels)
    turned_two = jnp.swapaxes(conv2_weight, 2, 3).reshape(9 * channels, channels)
    source_field, cot_field = (inputs, cotangent)

    def stack_of(field, direction):
        return windows(extend(field), count_of_rows, lon_width, channels, direction)

    def as_field(flat):
        return flat.reshape(count_of_rows, lon_width, channels)

    stack_input = stack_of(source_field, 1)
    first = jnp.dot(stack_input, forward_one, preferred_element_type=jnp.float32)
    cdf = 0.5 * (1.0 + jax.scipy.special.erf(first / jnp.sqrt(2.0)))
    hidden = (first * cdf).astype(jnp.bfloat16)
    stack_hidden = stack_of(as_field(hidden), 1)
    second = jnp.dot(stack_hidden, forward_two, preferred_element_type=jnp.float32)
    flat_input = source_field.reshape(cells, channels)
    output = (flat_input.astype(jnp.float32) + second).astype(jnp.bfloat16)
    flat_cot = cot_field.reshape(cells, channels)
    stacked_cotangent = stack_of(cot_field, -1)
    upstream = jnp.dot(stacked_cotangent, turned_two, preferred_element_type=jnp.float32)
    density = jnp.exp(-0.5 * first * first) / jnp.sqrt(2.0 * jnp.pi)
    pre_grad = (upstream * (cdf + first * density)).astype(jnp.bfloat16)
    stack_pre = stack_of(as_field(pre_grad), -1)
    back = jnp.dot(stack_pre, turned_one, preferred_element_type=jnp.float32)
    input_grad = (flat_cot.astype(jnp.float32) + back).astype(jnp.bfloat16)
    output = output.reshape(count_of_rows, lon_width, channels)
    input_grad = input_grad.reshape(count_of_rows, lon_width, channels)
    in_part = channels // lon_count
    out_part = channels // latitude_count
    terms_one = full_terms(stack_input, pre_grad, scale, channels)
    terms_two = full_terms(stack_hidden, flat_cot, scale, channels)
    partly = (
        lax.psum_scatter(terms_one, "lon", scatter_dimension=1, tiled=True),
        lax.psum_scatter(terms_two, "lon", scatter_dimension=1, tiled=True),
    )
    grad_one, grad_two = (
        lax.psum_scatter(partly[0], "lat", scatter_dimension=2, tiled=True),
        lax.psum_scatter(partly[1], "lat", scatter_dimension=2, tiled=True),
    )
    conv1_grad = grad_one.reshape(3, 3, in_part, out_part)
    conv2_grad = grad_two.reshape(3, 3, in_part, out_part)
    return (output, input_grad, conv1_grad, conv2_grad)


def write_stack(field, stack_ref, band, step):
    cells, channels = field.shape
    wide = field.astype(F32)
    place = lax.broadcasted_iota(jnp.int32, (cells, channels), 0) % band
    above = jnp.where(place >= step, pltpu.roll(wide, step, 0), 0.0).astype(BF16)
    below = jnp.where(place < band - step, pltpu.roll(wide, cells - step, 0), 0.0).astype(BF16)
    for at, part in enumerate((above, field, below)):
        columns = slice(at * channels, (at + 1) * channels)
        stack_ref[band : band + cells, columns] = part
        stack_ref[0:band, columns] = part[cells - band :]
        stack_ref[band + cells :, columns] = part[0:band]


def convolved(stack_ref, weight_ref, band, cells, copies):
    total = None
    for b in range(3):
        copies[b].wait()
        channels = weight_ref.shape[2]
        tap = weight_ref[:, b].reshape(3 * channels, channels)
        term = jnp.dot(stack_ref[b * band : b * band + cells, :], tap, preferred_element_type=F32)
        total = term if total is None else total + term
    return total


def convolved_back(stack_ref, weight_ref, band, cells, copies):
    total = None
    for b in range(3):
        copies[b].wait()
        tap = jnp.concatenate([weight_ref[2 - a, 2 - b] for a in range(3)], axis=1)
        term = lax.dot_general(
            stack_ref[b * band : b * band + cells, :],
            tap,
            (((1,), (1,)), ((), ())),
            preferred_element_type=F32,
        )
        total = term if total is None else total + term
    return total


def one_hot_rows(cells, step, devices, back):
    to = lax.broadcasted_iota(jnp.int32, (cells, cells), 1 if back else 0)
    source = lax.broadcasted_iota(jnp.int32, (cells, cells), 0 if back else 1)
    rows = cells // (devices * step)
    device, row, column = to // (rows * step), (to // step) % rows, to % step
    return (source == (row * devices + device) * step + column).astype(BF16)


def deal_kernel(step, inputs_ref, cot_ref, out_ref, held_ref, sems):
    devices, _, rows, channels = out_ref.shape
    cells = devices * rows
    copies = fetched(((inputs_ref, held_ref.at[0]), (cot_ref, held_ref.at[1])), sems)
    chosen = one_hot_rows(cells, step, devices, False)
    for at, copy in enumerate(copies):
        copy.wait()
        field = held_ref[at].reshape(cells, channels)
        dealt = jnp.dot(chosen, field, preferred_element_type=F32).astype(BF16)
        out_ref[:, at] = dealt.reshape(devices, rows, channels)


def gather_kernel(step, fields_ref, output_ref, grad_ref):
    devices, _, rows, channels = fields_ref.shape
    cells = devices * rows
    chosen = one_hot_rows(cells, step, devices, True)
    for at, ref in enumerate((output_ref, grad_ref)):
        field = fields_ref[:, at].reshape(cells, channels)
        ref[...] = jnp.dot(chosen, field, preferred_element_type=F32).astype(BF16).reshape(ref.shape)


def fetched(pairs, sems):
    copies = [pltpu.make_async_copy(source, to, sems.at[at]) for at, (source, to) in enumerate(pairs)]
    for copy in copies:
        copy.start()
    return copies


def by_tap(weight_ref, held_ref, sems, order):
    return fetched([(weight_ref.at[:, b], held_ref.at[:, b]) for b in order], sems)


def inner_kernel(band, step, place_ref, own_ref, one_ref, two_ref,
                 hidden_ref, pre_ref, mine_ref, give_ref,
                 one_held, two_held, stack_ref, first_ref, slope_ref, turned_ref, sems):
    x, y, core = place_ref[0], place_ref[1], place_ref[2]
    cells, channels = first_ref.shape
    first_weight = by_tap(one_ref, one_held, sems.at[0], range(3))
    half, rows = channels // 2, 32
    deep = half // 4

    def turn(at, field):
        turned = field.T
        for h in range(2):
            for z in range(4):
                begin = (2 * z + h) * deep if at < 2 else h * half + z * deep
                turned_ref[at * 2 + h, z * deep : (z + 1) * deep, :] = turned[begin : begin + deep]

    source = own_ref[:, 0].reshape(cells, channels)
    write_stack(source, stack_ref, band, step)
    first_ref[...] = convolved(stack_ref, one_held, band, cells, first_weight)
    second_weight = by_tap(two_ref, two_held, sems.at[1], (2, 1, 0))
    turn(0, source)

    def activate(at, carry):
        span = pl.ds(pl.multiple_of(at * rows, rows), rows)
        first = first_ref[span, :]
        cdf = 0.5 * (1.0 + lax.erf(first * (0.5**0.5)))
        density = jnp.exp(-0.5 * first * first) * ((2.0 * jnp.pi) ** -0.5)
        hidden_ref[span, :] = (first * cdf).astype(BF16)
        slope_ref[span, :] = cdf + first * density
        return carry

    lax.fori_loop(0, cells // rows, activate, 0)
    turn(1, hidden_ref[...])
    cot = own_ref[:, 1].reshape(cells, channels)
    write_stack(cot, stack_ref, band, step)
    turn(3, cot)
    pre_ref[...] = (slope_ref[...] * convolved_back(stack_ref, two_held, band, cells, second_weight)).astype(BF16)
    turn(2, pre_ref[...])

    for ref, of in ((mine_ref, core), (give_ref, 1 - core)):
        ref[0] = turned_ref[of * 2 + 1 - y]
        ref[1] = turned_ref[of * 2 + y]
        ref[2] = turned_ref[4 + of * 2 + 1 - x]
        ref[3] = turned_ref[4 + of * 2 + x]


def join_kernel(mine_ref, got_ref, x_ref, y_ref):
    for at, ref in enumerate((mine_ref, got_ref)):
        y_ref[at] = ref[0]
        x_ref[2 + at] = ref[1]
        x_ref[at] = ref[2]
        y_ref[2 + at] = ref[3]


def outer_kernel(band, step, own_ref, hidden_ref, pre_ref, one_ref, two_ref, out_ref,
                 one_held, two_held, stack_ref, sems):
    cells, channels = hidden_ref.shape
    shape = (out_ref.shape[0],) + out_ref.shape[2:]
    second_weight = by_tap(two_ref, two_held, sems.at[1], range(3))
    write_stack(hidden_ref[...], stack_ref, band, step)
    second = convolved(stack_ref, two_held, band, cells, second_weight)
    first_weight = by_tap(one_ref, one_held, sems.at[0], (2, 1, 0))
    source = own_ref[:, 0].reshape(cells, channels)
    out_ref[:, 0] = (source.astype(F32) + second).astype(BF16).reshape(shape)
    write_stack(pre_ref[...], stack_ref, band, step)
    back = convolved_back(stack_ref, one_held, band, cells, first_weight)
    cot = own_ref[:, 1].reshape(cells, channels)
    out_ref[:, 1] = (cot.astype(F32) + back).astype(BF16).reshape(shape)


def units(deep):
    count = deep // 16
    for unit in range(9 * count):
        yield unit // count, (unit % count) * 16, (unit // 4) * 16, unit % 4


def summed(band, step, lefts, rights, turned_ref, moved_ref, b):
    half, cells = lefts[0].shape
    if b == 0:
        place = lax.broadcasted_iota(jnp.int32, (half, cells), 1) % band
        for at, (left_ref, right_ref) in enumerate(zip(lefts, rights)):
            columns = slice(at * cells, (at + 1) * cells)
            field = left_ref[...]
            wide = field.astype(F32)
            turned_ref[0:half, columns] = jnp.where(place >= step, pltpu.roll(wide, step, 1), 0.0).astype(BF16)
            turned_ref[half : 2 * half, columns] = field
            turned_ref[2 * half :, columns] = jnp.where(
                place < band - step, pltpu.roll(wide, cells - step, 1), 0.0
            ).astype(BF16)
            grad = right_ref[...]
            wide = grad.astype(F32)
            moved_ref[0, :, columns] = pltpu.roll(wide, cells - band, 1).astype(BF16)
            moved_ref[1, :, columns] = grad
            moved_ref[2, :, columns] = pltpu.roll(wide, band, 1).astype(BF16)
    return lax.dot_general(turned_ref[...], moved_ref[b], (((1,), (1,)), ((), ())), preferred_element_type=F32)


def near_kernel(band, step, x_ref, y_ref, x_got_ref, y_got_ref, sums_ref, turned_ref, moved_ref):
    lefts = [x_ref.at[2], x_ref.at[3], x_got_ref.at[2], x_got_ref.at[3], y_got_ref.at[0], y_got_ref.at[1]]
    rights = [y_ref.at[2], y_ref.at[3], x_got_ref.at[0], x_got_ref.at[1], y_got_ref.at[2], y_got_ref.at[3]]
    for b in range(3):
        sums_ref[b] = summed(band, step, lefts, rights, turned_ref, moved_ref, b)


def far_kernel(band, step, place_ref, near_ref, left_ref, right_ref, *refs):
    out_refs, (turned_ref, moved_ref, sums_ref, send_ref, sems) = refs[:-5], refs[-5:]
    me = place_ref[3] * 2 + place_ref[2]
    half = left_ref.shape[1]
    lefts, rights = ([ref.at[at] for at in range(2)] for ref in (left_ref, right_ref))
    for b in range(3):
        sums_ref[b] = near_ref[b] + summed(band, step, lefts, rights, turned_ref, moved_ref, b)
    deep, quarter = half // 4, half // 2
    height = send_ref.shape[1]
    for z in range(4):
        for core in range(2):
            blocks = [[] for _ in range(height // 16)]
            for tap, row, to, _ in units(deep):
                begin = (tap // 3) * half + z * deep + row
                blocks[to // 16].append(
                    sums_ref[tap % 3, begin : begin + 16, core * quarter : (core + 1) * quarter]
                )
            for to, parts in enumerate(blocks):
                while len(parts) < 4:
                    parts.append(jnp.zeros((16, quarter), F32))
                send_ref[z * 2 + core, to * 16 : (to + 1) * 16, :] = jnp.concatenate(parts, axis=1).astype(BF16)
    pairs = [(send_ref.at[me ^ away], ref) for away, ref in enumerate(out_refs)]
    for copy in fetched(pairs, sems):
        copy.wait()


def finish_kernel(scale, place_ref, *refs):
    parts, (one_ref, two_ref) = refs[:-2], refs[-2:]
    core = place_ref[2]
    deep, quarter = one_ref.shape[2:]
    sums = []
    for other in range(2):
        total = parts[other][...].astype(F32)
        for ref in parts[other + 2 :: 2]:
            total = total + ref[...].astype(F32)
        sums.append(total * scale)
    ours, theirs = sums
    for out_ref, total in (
        (one_ref, jnp.where(core == 0, ours, theirs)),
        (two_ref, jnp.where(core == 0, theirs, ours)),
    ):
        for tap, row, begin, slot in units(deep):
            out_ref[tap // 3, tap % 3, row : row + 16, :] = total[
                begin : begin + 16, slot * quarter : (slot + 1) * quarter
            ]


def fast_local(inputs, conv1_weight, conv2_weight, cotangent):
    rows, width, channels = inputs.shape
    every = ("z", "y", "x", "core")
    devices = lax.axis_size(every)
    step = width // devices
    cells = rows * width
    lat = lax.axis_size("x") * lax.axis_size("core")
    lon = devices // lat
    band = rows * lat * step
    half, deep = channels // 2, channels // lon
    height = -(-9 * (deep // 16) // 4) * 16
    scale = (rows * lat * width * lon) ** (-0.5)
    flops = 2 * 9 * cells * channels * channels
    vmem, hbm, smem = (pl.BlockSpec(memory_space=space) for space in (pltpu.VMEM, pltpu.HBM, pltpu.SMEM))

    def held(*shape, kind=BF16):
        return pltpu.VMEM(shape, kind)

    def shaped(*shape, kind=BF16):
        return jax.ShapeDtypeStruct(shape, kind)

    def kernel(body, specs, arguments, out_shape, scratch_shapes, work, megabytes):
        return pl.pallas_call(
            body,
            out_shape=out_shape,
            in_specs=specs,
            out_specs=jax.tree.map(lambda _: vmem, out_shape),
            scratch_shapes=scratch_shapes,
            compiler_params=pltpu.CompilerParams(vmem_limit_bytes=20 * 2**20),
            cost_estimate=pl.CostEstimate(flops=work, bytes_accessed=megabytes * 2**20, transcendentals=0),
        )(*arguments)

    def passed(piece, x, y, core):
        pairs = [(i, i ^ (4 * y + 2 * x + core)) for i in range(8)]
        return lax.ppermute(piece, ("y", "x", "core"), pairs)

    stack = held(cells + 2 * band, 3 * channels)
    weights = held(*conv1_weight.shape)
    dealt = shaped(devices, 2, rows * step, channels)
    own = kernel(
        functools.partial(deal_kernel, step),
        [hbm] * 2,
        [pltpu.with_memory_space_constraint(field, pltpu.HBM) for field in (inputs, cotangent)],
        dealt,
        [held(2, *inputs.shape), pltpu.SemaphoreType.DMA((2,))],
        10**9,
        3,
    )
    own = lax.all_to_all(own, every, 0, 0, tiled=True)
    place = jnp.stack([lax.axis_index(axis) for axis in ("x", "y", "core", "z")]).astype(jnp.int32)
    one, two = (pltpu.with_memory_space_constraint(w, pltpu.HBM) for w in (conv1_weight, conv2_weight))
    taps = pltpu.SemaphoreType.DMA((2, 3))
    pieces = held(4, half, cells)
    hidden, pre_grad, mine, give = kernel(
        functools.partial(inner_kernel, band, step),
        [smem, vmem, hbm, hbm],
        (place, own, one, two),
        (held(cells, channels), held(cells, channels), pieces, pieces),
        [
            weights,
            weights,
            stack,
            held(cells, channels, kind=F32),
            held(cells, channels, kind=F32),
            held(8, half, cells),
            taps,
        ],
        2 * flops,
        10,
    )
    x_given, y_given = kernel(
        join_kernel, [vmem] * 2, (mine, passed(give, 0, 0, 1)), (pieces, pieces), [], 10**6, 4
    )
    x_got, y_got = passed(x_given, 1, 0, 0), passed(y_given, 0, 1, 0)
    hidden, pre_grad, x_given = lax.optimization_barrier((hidden, pre_grad, x_given))
    fields = kernel(
        functools.partial(outer_kernel, band, step),
        [vmem] * 3 + [hbm] * 2,
        (own, hidden, pre_grad, one, two),
        dealt,
        [weights, weights, stack, taps],
        2 * flops,
        9,
    )
    _, x_got, y_got = lax.optimization_barrier((fields, x_got, y_got))
    far = (passed(y_got[:2], 1, 0, 0), passed(x_got[:2], 0, 1, 0))
    fields = lax.all_to_all(fields, every, 0, 0, tiled=True)
    output, input_grad = kernel(
        functools.partial(gather_kernel, step), [vmem], (fields,), (shaped(*inputs.shape),) * 2, [], 10**9, 3
    )
    sums = shaped(3, 3 * half, half, kind=F32)
    near = kernel(
        functools.partial(near_kernel, band, step),
        [vmem] * 4,
        (x_given, y_given, x_got, y_got),
        sums,
        [held(3 * half, 6 * cells), held(3, half, 6 * cells)],
        3 * flops,
        6,
    )
    terms = kernel(
        functools.partial(far_kernel, band, step),
        [smem] + [vmem] * 3,
        (place, near) + far,
        (pltpu.VMEM((height, channels), BF16),) * 8,
        [
            held(3 * half, 2 * cells),
            held(3, half, 2 * cells),
            held(*sums.shape, kind=F32),
            held(8, height, channels),
            pltpu.SemaphoreType.DMA((8,)),
        ],
        3 * flops,
        4,
    )
    parts = list(terms)
    for away in (6, 7, 4, 5, 2, 3, 1):
        parts[away] = lax.ppermute(terms[away], ("z", "core"), [(i, i ^ away) for i in range(8)])
    output, input_grad, parts = lax.optimization_barrier((output, input_grad, parts))
    grad = shaped(3, 3, deep, half // 2, kind=F32)
    conv1_grad, conv2_grad = kernel(
        functools.partial(finish_kernel, scale), [smem] + [vmem] * 8, (place, *parts), (grad, grad), [], 10**6, 2
    )
    return (output, input_grad, conv1_grad, conv2_grad)


def is_fast(mesh):
    return dict(mesh.shape) == {"lon": 8, "lat": 4}


def solution(mesh):
    body, lon, lat = local, "lon", "lat"
    if is_fast(mesh):
        lon, lat = ("z", "y"), ("x", "core")
        mesh = jax.sharding.Mesh(mesh.devices.reshape(4, 2, 2, 2), lon + lat)
        body = fast_local
    field, grad = P(lat, lon, None), P(None, None, lon, lat)
    return jax.shard_map(
        body,
        mesh=mesh,
        in_specs=(field, P(), P(), field),
        out_specs=(field, field, grad, grad),
        check_vma=False,
    )
```

```python
import functools

import jax
import jax.numpy as jnp
from jax import lax
from jax.experimental import pallas as pl
from jax.experimental.pallas import tpu as pltpu
from jax.sharding import PartitionSpec as P

F32, BF16 = jnp.float32, jnp.bfloat16


def passed_along(shard, axis, by):
    length = lax.axis_size(axis)
    return lax.ppermute(shard, axis, [(i, (i + by) % length) for i in range(length)])


def padded(shard, sides, width):
    for axis, dim in sides:
        size, length = (lax.axis_size(axis), shard.shape[dim])
        up = [(i, (i + 1) % size) for i in range(size - 1)]
        down = [(j, i) for i, j in up]
        last = lax.slice_in_dim(shard, length - width, length, axis=dim)
        initial = lax.slice_in_dim(shard, 0, width, axis=dim)
        before = lax.ppermute(last, axis, up)
        after = lax.ppermute(initial, axis, down)
        shard = jnp.concatenate([before, shard, after], axis=dim)
    return shard


def extend(field):
    western = passed_along(field, "lon", 1)
    eastern = passed_along(field, "lon", -1)
    widened = jnp.concatenate([western, field, eastern], axis=1)
    return padded(widened, (("lat", 0),), 1)


def windows(padded_field, count_of_rows, lon_width, channels, direction):
    pieces = []
    for lat_step in (-1, 0, 1):
        for longitude_stride in (-1, 0, 1):
            row_start = 1 + direction * lat_step
            column_begin = lon_width + direction * lon_width * longitude_stride
            pieces.append(
                padded_field[
                    row_start : row_start + count_of_rows, column_begin : column_begin + lon_width
                ]
            )
    stacked = jnp.concatenate(pieces, axis=2)
    return stacked.reshape(count_of_rows * lon_width, 9 * channels)


def full_terms(stacked, grad, scale, channels):
    product = lax.dot_general(
        stacked, grad, (((0,), (0,)), ((), ())), preferred_element_type=jnp.float32
    )
    return (product * scale).reshape(9, channels, channels)


def local(inputs, conv1_weight, conv2_weight, cotangent):
    count_of_rows, lon_width, channels = inputs.shape
    cells = count_of_rows * lon_width
    lon_count = lax.axis_size("lon")
    latitude_count = lax.axis_size("lat")
    scale = (count_of_rows * latitude_count * lon_width * lon_count) ** (-0.5)
    forward_one = conv1_weight.reshape(9 * channels, channels)
    forward_two = conv2_weight.reshape(9 * channels, channels)
    turned_one = jnp.swapaxes(conv1_weight, 2, 3).reshape(9 * channels, channels)
    turned_two = jnp.swapaxes(conv2_weight, 2, 3).reshape(9 * channels, channels)
    source_field, cot_field = (inputs, cotangent)

    def stack_of(field, direction):
        return windows(extend(field), count_of_rows, lon_width, channels, direction)

    def as_field(flat):
        return flat.reshape(count_of_rows, lon_width, channels)

    stack_input = stack_of(source_field, 1)
    first = jnp.dot(stack_input, forward_one, preferred_element_type=jnp.float32)
    cdf = 0.5 * (1.0 + jax.scipy.special.erf(first / jnp.sqrt(2.0)))
    hidden = (first * cdf).astype(jnp.bfloat16)
    stack_hidden = stack_of(as_field(hidden), 1)
    second = jnp.dot(stack_hidden, forward_two, preferred_element_type=jnp.float32)
    flat_input = source_field.reshape(cells, channels)
    output = (flat_input.astype(jnp.float32) + second).astype(jnp.bfloat16)
    flat_cot = cot_field.reshape(cells, channels)
    stacked_cotangent = stack_of(cot_field, -1)
    upstream = jnp.dot(stacked_cotangent, turned_two, preferred_element_type=jnp.float32)
    density = jnp.exp(-0.5 * first * first) / jnp.sqrt(2.0 * jnp.pi)
    pre_grad = (upstream * (cdf + first * density)).astype(jnp.bfloat16)
    stack_pre = stack_of(as_field(pre_grad), -1)
    back = jnp.dot(stack_pre, turned_one, preferred_element_type=jnp.float32)
    input_grad = (flat_cot.astype(jnp.float32) + back).astype(jnp.bfloat16)
    output = output.reshape(count_of_rows, lon_width, channels)
    input_grad = input_grad.reshape(count_of_rows, lon_width, channels)
    in_part = channels // lon_count
    out_part = channels // latitude_count
    terms_one = full_terms(stack_input, pre_grad, scale, channels)
    terms_two = full_terms(stack_hidden, flat_cot, scale, channels)
    partly = (
        lax.psum_scatter(terms_one, "lon", scatter_dimension=1, tiled=True),
        lax.psum_scatter(terms_two, "lon", scatter_dimension=1, tiled=True),
    )
    grad_one, grad_two = (
        lax.psum_scatter(partly[0], "lat", scatter_dimension=2, tiled=True),
        lax.psum_scatter(partly[1], "lat", scatter_dimension=2, tiled=True),
    )
    conv1_grad = grad_one.reshape(3, 3, in_part, out_part)
    conv2_grad = grad_two.reshape(3, 3, in_part, out_part)
    return (output, input_grad, conv1_grad, conv2_grad)


def write_stack(field, stack_ref, band, step):
    cells, channels = field.shape
    wide = field.astype(F32)
    place = lax.broadcasted_iota(jnp.int32, (cells, channels), 0) % band
    above = jnp.where(place >= step, pltpu.roll(wide, step, 0), 0.0).astype(BF16)
    below = jnp.where(place < band - step, pltpu.roll(wide, cells - step, 0), 0.0).astype(BF16)
    for at, part in enumerate((above, field, below)):
        columns = slice(at * channels, (at + 1) * channels)
        stack_ref[band : band + cells, columns] = part
        stack_ref[0:band, columns] = part[cells - band :]
        stack_ref[band + cells :, columns] = part[0:band]


def convolved(stack_ref, weight_ref, band, cells, copies):
    total = None
    for b in range(3):
        copies[b].wait()
        channels = weight_ref.shape[2]
        tap = weight_ref[:, b].reshape(3 * channels, channels)
        term = jnp.dot(stack_ref[b * band : b * band + cells, :], tap, preferred_element_type=F32)
        total = term if total is None else total + term
    return total


def convolved_back(stack_ref, weight_ref, band, cells, copies):
    total = None
    for b in range(3):
        copies[b].wait()
        tap = jnp.concatenate([weight_ref[2 - a, 2 - b] for a in range(3)], axis=1)
        term = lax.dot_general(
            stack_ref[b * band : b * band + cells, :],
            tap,
            (((1,), (1,)), ((), ())),
            preferred_element_type=F32,
        )
        total = term if total is None else total + term
    return total


def one_hot_rows(cells, step, devices, back):
    to = lax.broadcasted_iota(jnp.int32, (cells, cells), 1 if back else 0)
    source = lax.broadcasted_iota(jnp.int32, (cells, cells), 0 if back else 1)
    rows = cells // (devices * step)
    device, row, column = to // (rows * step), (to // step) % rows, to % step
    return (source == (row * devices + device) * step + column).astype(BF16)


def deal_kernel(step, inputs_ref, cot_ref, out_ref, held_ref, sems):
    devices, _, rows, channels = out_ref.shape
    cells = devices * rows
    copies = fetched(((inputs_ref, held_ref.at[0]), (cot_ref, held_ref.at[1])), sems)
    chosen = one_hot_rows(cells, step, devices, False)
    for at, copy in enumerate(copies):
        copy.wait()
        field = held_ref[at].reshape(cells, channels)
        dealt = jnp.dot(chosen, field, preferred_element_type=F32).astype(BF16)
        out_ref[:, at] = dealt.reshape(devices, rows, channels)


def gather_kernel(step, fields_ref, output_ref, grad_ref):
    devices, _, rows, channels = fields_ref.shape
    cells = devices * rows
    chosen = one_hot_rows(cells, step, devices, True)
    for at, ref in enumerate((output_ref, grad_ref)):
        field = fields_ref[:, at].reshape(cells, channels)
        ref[...] = jnp.dot(chosen, field, preferred_element_type=F32).astype(BF16).reshape(ref.shape)


def fetched(pairs, sems):
    copies = [pltpu.make_async_copy(source, to, sems.at[at]) for at, (source, to) in enumerate(pairs)]
    for copy in copies:
        copy.start()
    return copies


def by_tap(weight_ref, held_ref, sems, order):
    return fetched([(weight_ref.at[:, b], held_ref.at[:, b]) for b in order], sems)


def inner_kernel(band, step, place_ref, own_ref, one_ref, two_ref,
                 hidden_ref, pre_ref, mine_ref, give_ref,
                 one_held, two_held, stack_ref, first_ref, slope_ref, turned_ref, sems):
    x, y, core = place_ref[0], place_ref[1], place_ref[2]
    cells, channels = first_ref.shape
    first_weight = by_tap(one_ref, one_held, sems.at[0], range(3))
    half, rows = channels // 2, 32
    deep = half // 4

    def turn(at, field):
        turned = field.T
        for h in range(2):
            for z in range(4):
                begin = (2 * z + h) * deep if at < 2 else h * half + z * deep
                turned_ref[at * 2 + h, z * deep : (z + 1) * deep, :] = turned[begin : begin + deep]

    source = own_ref[:, 0].reshape(cells, channels)
    write_stack(source, stack_ref, band, step)
    first_ref[...] = convolved(stack_ref, one_held, band, cells, first_weight)
    second_weight = by_tap(two_ref, two_held, sems.at[1], (2, 1, 0))
    turn(0, source)

    def activate(at, carry):
        span = pl.ds(pl.multiple_of(at * rows, rows), rows)
        first = first_ref[span, :]
        cdf = 0.5 * (1.0 + lax.erf(first * (0.5**0.5)))
        density = jnp.exp(-0.5 * first * first) * ((2.0 * jnp.pi) ** -0.5)
        hidden_ref[span, :] = (first * cdf).astype(BF16)
        slope_ref[span, :] = cdf + first * density
        return carry

    lax.fori_loop(0, cells // rows, activate, 0)
    turn(1, hidden_ref[...])
    cot = own_ref[:, 1].reshape(cells, channels)
    write_stack(cot, stack_ref, band, step)
    turn(3, cot)
    pre_ref[...] = (slope_ref[...] * convolved_back(stack_ref, two_held, band, cells, second_weight)).astype(BF16)
    turn(2, pre_ref[...])

    for ref, of, side in ((mine_ref, core, jnp.where(core == 0, x, y)), (give_ref, 1 - core, jnp.where(core == 0, y, x))):
        ref[0] = turned_ref[6 * of]
        ref[1] = turned_ref[6 * of + 1]
        ref[2] = turned_ref[4 - 2 * of + 1 - side]
        ref[3] = turned_ref[4 - 2 * of + side]


def outer_kernel(band, step, own_ref, hidden_ref, pre_ref, one_ref, two_ref, out_ref,
                 one_held, two_held, stack_ref, sems):
    cells, channels = hidden_ref.shape
    shape = (out_ref.shape[0],) + out_ref.shape[2:]
    second_weight = by_tap(two_ref, two_held, sems.at[1], range(3))
    write_stack(hidden_ref[...], stack_ref, band, step)
    second = convolved(stack_ref, two_held, band, cells, second_weight)
    first_weight = by_tap(one_ref, one_held, sems.at[0], (2, 1, 0))
    source = own_ref[:, 0].reshape(cells, channels)
    out_ref[:, 0] = (source.astype(F32) + second).astype(BF16).reshape(shape)
    write_stack(pre_ref[...], stack_ref, band, step)
    back = convolved_back(stack_ref, one_held, band, cells, first_weight)
    cot = own_ref[:, 1].reshape(cells, channels)
    out_ref[:, 1] = (cot.astype(F32) + back).astype(BF16).reshape(shape)


def units(deep):
    count = deep // 16
    for unit in range(9 * count):
        yield unit // count, (unit % count) * 16, (unit // 4) * 16, unit % 4


def grads_kernel(band, step, place_ref, mine_ref, got_ref, far_ref, far_pair_ref, keep_ref, give_ref, whole_ref, moved_ref):
    x, y, core = place_ref[0], place_ref[1], place_ref[2]
    half, cells = mine_ref.shape[1:]
    place = lax.broadcasted_iota(jnp.int32, (half, cells), 1) % band
    for at, (ref, moving) in enumerate(((mine_ref, 3), (got_ref, 3), (far_ref, 2), (far_pair_ref, 2))):
        columns = slice(at * cells, (at + 1) * cells)
        whole_ref[0, :, columns] = ref[0]
        whole_ref[1, :, columns] = ref[1]
        wide = ref[moving].astype(F32)
        for a in range(-1, 2):
            for b in range(-1, 2):
                shift = (-(b * band + a * step)) % cells
                part = pltpu.roll(wide, shift, 1) if shift else wide
                if a > 0:
                    part = jnp.where(place < band - step, part, 0.0)
                if a < 0:
                    part = jnp.where(place >= step, part, 0.0)
                tap = (a + 1) * 3 + b + 1
                moved_ref[jnp.where(core == 0, 8 - tap, tap), :, columns] = part.astype(BF16)
    moved = moved_ref[...].reshape(9 * half, 4 * cells)
    stays = jnp.where(core == 0, y, x)
    for ref, which in ((give_ref, 1 - stays), (keep_ref, stays)):
        whole = whole_ref[which]

        @pl.when(core == 0)
        def _():
            ref[...] = lax.dot_general(
                whole, moved, (((1,), (1,)), ((), ())), preferred_element_type=F32
            ).astype(ref.dtype)

        @pl.when(core == 1)
        def _():
            terms = lax.dot_general(moved, whole, (((1,), (1,)), ((), ())), preferred_element_type=F32)
            for tap in range(9):
                rows = slice(tap * half, (tap + 1) * half)
                ref[:, rows] = terms[rows].astype(ref.dtype)


def pack_kernel(place_ref, keep_ref, got_ref, *refs):
    out_refs, (sums_ref, send_ref, sems) = refs[:-3], refs[-3:]
    me = place_ref[3] * 2 + place_ref[2]
    half = keep_ref.shape[0]
    sums_ref[...] = keep_ref[...] + got_ref[...].astype(F32)
    deep, quarter = half // 4, half // 2
    height = send_ref.shape[1]
    for z in range(4):
        for core in range(2):
            blocks = [[] for _ in range(height // 16)]
            for tap, row, to, _ in units(deep):
                begin, first = z * deep + row, tap * half + core * quarter
                blocks[to // 16].append(sums_ref[begin : begin + 16, first : first + quarter])
            for to, parts in enumerate(blocks):
                while len(parts) < 4:
                    parts.append(jnp.zeros((16, quarter), F32))
                send_ref[z * 2 + core, to * 16 : (to + 1) * 16, :] = jnp.concatenate(parts, axis=1).astype(BF16)
    pairs = [(send_ref.at[me ^ away], ref) for away, ref in enumerate(out_refs)]
    for copy in fetched(pairs, sems):
        copy.wait()


def finish_kernel(scale, place_ref, *refs):
    parts, (one_ref, two_ref) = refs[:-2], refs[-2:]
    core = place_ref[2]
    deep, quarter = one_ref.shape[2:]
    sums = []
    for other in range(2):
        total = parts[other][...].astype(F32)
        for ref in parts[other + 2 :: 2]:
            total = total + ref[...].astype(F32)
        sums.append(total * scale)
    ours, theirs = sums
    for out_ref, total in (
        (one_ref, jnp.where(core == 0, ours, theirs)),
        (two_ref, jnp.where(core == 0, theirs, ours)),
    ):
        for tap, row, begin, slot in units(deep):
            out_ref[tap // 3, tap % 3, row : row + 16, :] = total[
                begin : begin + 16, slot * quarter : (slot + 1) * quarter
            ]


def fast_local(inputs, conv1_weight, conv2_weight, cotangent):
    rows, width, channels = inputs.shape
    every = ("z", "y", "x", "core")
    devices = lax.axis_size(every)
    step = width // devices
    cells = rows * width
    lat = lax.axis_size("x") * lax.axis_size("core")
    lon = devices // lat
    band = rows * lat * step
    half, deep = channels // 2, channels // lon
    height = -(-9 * (deep // 16) // 4) * 16
    scale = (rows * lat * width * lon) ** (-0.5)
    flops = 2 * 9 * cells * channels * channels
    vmem, hbm, smem = (pl.BlockSpec(memory_space=space) for space in (pltpu.VMEM, pltpu.HBM, pltpu.SMEM))

    def held(*shape, kind=BF16):
        return pltpu.VMEM(shape, kind)

    def shaped(*shape, kind=BF16):
        return jax.ShapeDtypeStruct(shape, kind)

    def kernel(body, specs, arguments, out_shape, scratch_shapes, work, megabytes):
        return pl.pallas_call(
            body,
            out_shape=out_shape,
            in_specs=specs,
            out_specs=jax.tree.map(lambda _: vmem, out_shape),
            scratch_shapes=scratch_shapes,
            compiler_params=pltpu.CompilerParams(vmem_limit_bytes=32 * 2**20),
            cost_estimate=pl.CostEstimate(flops=work, bytes_accessed=megabytes * 2**20, transcendentals=0),
        )(*arguments)

    def passed(piece, x, y, core):
        pairs = [(i, i ^ (4 * (i % 2 == y) + 2 * (i % 2 == x) + core)) for i in range(8)]
        return lax.ppermute(piece, ("y", "x", "core"), pairs)

    stack = held(cells + 2 * band, 3 * channels)
    weights = held(*conv1_weight.shape)
    dealt = shaped(devices, 2, rows * step, channels)
    own = kernel(
        functools.partial(deal_kernel, step),
        [hbm] * 2,
        [pltpu.with_memory_space_constraint(field, pltpu.HBM) for field in (inputs, cotangent)],
        dealt,
        [held(2, *inputs.shape), pltpu.SemaphoreType.DMA((2,))],
        10**9,
        3,
    )
    own = lax.all_to_all(own, every, 0, 0, tiled=True)
    place = jnp.stack([lax.axis_index(axis) for axis in ("x", "y", "core", "z")]).astype(jnp.int32)
    one, two = (pltpu.with_memory_space_constraint(w, pltpu.HBM) for w in (conv1_weight, conv2_weight))
    taps = pltpu.SemaphoreType.DMA((2, 3))
    pieces = held(4, half, cells)
    hidden, pre_grad, mine, give = kernel(
        functools.partial(inner_kernel, band, step),
        [smem, vmem, hbm, hbm],
        (place, own, one, two),
        (held(cells, channels), held(cells, channels), pieces, pieces),
        [
            weights,
            weights,
            stack,
            held(cells, channels, kind=F32),
            held(cells, channels, kind=F32),
            held(8, half, cells),
            taps,
        ],
        2 * flops,
        10,
    )
    got = passed(give, None, None, 1)
    far, far_pair = passed(mine[:3], 0, 1, 0), passed(got[:3], 0, 1, 0)
    hidden, pre_grad, got = lax.optimization_barrier((hidden, pre_grad, got))
    fields = kernel(
        functools.partial(outer_kernel, band, step),
        [vmem] * 3 + [hbm] * 2,
        (own, hidden, pre_grad, one, two),
        dealt,
        [weights, weights, stack, taps],
        2 * flops,
        9,
    )
    _, far, far_pair = lax.optimization_barrier((fields, far, far_pair))
    fields = lax.all_to_all(fields, every, 0, 0, tiled=True)
    output, input_grad = kernel(
        functools.partial(gather_kernel, step), [vmem], (fields,), (shaped(*inputs.shape),) * 2, [], 10**9, 3
    )
    keep, give = kernel(
        functools.partial(grads_kernel, band, step),
        [smem] + [vmem] * 4,
        (place, mine, got, far, far_pair),
        (held(half, 9 * half, kind=F32), held(half, 9 * half)),
        [held(2, half, 4 * cells), held(9, half, 4 * cells)],
        4 * flops,
        6,
    )
    terms = kernel(
        pack_kernel,
        [smem] + [vmem] * 2,
        (place, keep, passed(give, 1, 0, 0)),
        (held(height, channels),) * 8,
        [held(half, 9 * half, kind=F32), held(8, height, channels), pltpu.SemaphoreType.DMA((8,))],
        2 * flops,
        4,
    )
    parts = list(terms)
    for away in (6, 7, 4, 5, 2, 3, 1):
        parts[away] = lax.ppermute(terms[away], ("z", "core"), [(i, i ^ away) for i in range(8)])
    output, input_grad, parts = lax.optimization_barrier((output, input_grad, parts))
    grad = shaped(3, 3, deep, half // 2, kind=F32)
    conv1_grad, conv2_grad = kernel(
        functools.partial(finish_kernel, scale), [smem] + [vmem] * 8, (place, *parts), (grad, grad), [], 10**6, 2
    )
    return (output, input_grad, conv1_grad, conv2_grad)


def is_fast(mesh):
    return dict(mesh.shape) == {"lon": 8, "lat": 4}


def solution(mesh):
    body, lon, lat = local, "lon", "lat"
    if is_fast(mesh):
        lon, lat = ("z", "y"), ("x", "core")
        mesh = jax.sharding.Mesh(mesh.devices.reshape(4, 2, 2, 2), lon + lat)
        body = fast_local
    field, grad = P(lat, lon, None), P(None, None, lon, lat)
    return jax.shard_map(
        body,
        mesh=mesh,
        in_specs=(field, P(), P(), field),
        out_specs=(field, field, grad, grad),
        check_vma=False,
    )
```

```python
import functools

import jax
import jax.numpy as jnp
from jax import lax
from jax.experimental import pallas as pl
from jax.experimental.pallas import tpu as pltpu
from jax.sharding import PartitionSpec as P

F32, BF16 = jnp.float32, jnp.bfloat16


def passed_along(shard, axis, by):
    length = lax.axis_size(axis)
    return lax.ppermute(shard, axis, [(i, (i + by) % length) for i in range(length)])


def padded(shard, sides, width):
    for axis, dim in sides:
        size, length = (lax.axis_size(axis), shard.shape[dim])
        up = [(i, (i + 1) % size) for i in range(size - 1)]
        down = [(j, i) for i, j in up]
        last = lax.slice_in_dim(shard, length - width, length, axis=dim)
        initial = lax.slice_in_dim(shard, 0, width, axis=dim)
        before = lax.ppermute(last, axis, up)
        after = lax.ppermute(initial, axis, down)
        shard = jnp.concatenate([before, shard, after], axis=dim)
    return shard


def extend(field):
    western = passed_along(field, "lon", 1)
    eastern = passed_along(field, "lon", -1)
    widened = jnp.concatenate([western, field, eastern], axis=1)
    return padded(widened, (("lat", 0),), 1)


def windows(padded_field, count_of_rows, lon_width, channels, direction):
    pieces = []
    for lat_step in (-1, 0, 1):
        for longitude_stride in (-1, 0, 1):
            row_start = 1 + direction * lat_step
            column_begin = lon_width + direction * lon_width * longitude_stride
            pieces.append(
                padded_field[
                    row_start : row_start + count_of_rows, column_begin : column_begin + lon_width
                ]
            )
    stacked = jnp.concatenate(pieces, axis=2)
    return stacked.reshape(count_of_rows * lon_width, 9 * channels)


def full_terms(stacked, grad, scale, channels):
    product = lax.dot_general(
        stacked, grad, (((0,), (0,)), ((), ())), preferred_element_type=jnp.float32
    )
    return (product * scale).reshape(9, channels, channels)


def local(inputs, conv1_weight, conv2_weight, cotangent):
    count_of_rows, lon_width, channels = inputs.shape
    cells = count_of_rows * lon_width
    lon_count = lax.axis_size("lon")
    latitude_count = lax.axis_size("lat")
    scale = (count_of_rows * latitude_count * lon_width * lon_count) ** (-0.5)
    forward_one = conv1_weight.reshape(9 * channels, channels)
    forward_two = conv2_weight.reshape(9 * channels, channels)
    turned_one = jnp.swapaxes(conv1_weight, 2, 3).reshape(9 * channels, channels)
    turned_two = jnp.swapaxes(conv2_weight, 2, 3).reshape(9 * channels, channels)
    source_field, cot_field = (inputs, cotangent)

    def stack_of(field, direction):
        return windows(extend(field), count_of_rows, lon_width, channels, direction)

    def as_field(flat):
        return flat.reshape(count_of_rows, lon_width, channels)

    stack_input = stack_of(source_field, 1)
    first = jnp.dot(stack_input, forward_one, preferred_element_type=jnp.float32)
    cdf = 0.5 * (1.0 + jax.scipy.special.erf(first / jnp.sqrt(2.0)))
    hidden = (first * cdf).astype(jnp.bfloat16)
    stack_hidden = stack_of(as_field(hidden), 1)
    second = jnp.dot(stack_hidden, forward_two, preferred_element_type=jnp.float32)
    flat_input = source_field.reshape(cells, channels)
    output = (flat_input.astype(jnp.float32) + second).astype(jnp.bfloat16)
    flat_cot = cot_field.reshape(cells, channels)
    stacked_cotangent = stack_of(cot_field, -1)
    upstream = jnp.dot(stacked_cotangent, turned_two, preferred_element_type=jnp.float32)
    density = jnp.exp(-0.5 * first * first) / jnp.sqrt(2.0 * jnp.pi)
    pre_grad = (upstream * (cdf + first * density)).astype(jnp.bfloat16)
    stack_pre = stack_of(as_field(pre_grad), -1)
    back = jnp.dot(stack_pre, turned_one, preferred_element_type=jnp.float32)
    input_grad = (flat_cot.astype(jnp.float32) + back).astype(jnp.bfloat16)
    output = output.reshape(count_of_rows, lon_width, channels)
    input_grad = input_grad.reshape(count_of_rows, lon_width, channels)
    in_part = channels // lon_count
    out_part = channels // latitude_count
    terms_one = full_terms(stack_input, pre_grad, scale, channels)
    terms_two = full_terms(stack_hidden, flat_cot, scale, channels)
    partly = (
        lax.psum_scatter(terms_one, "lon", scatter_dimension=1, tiled=True),
        lax.psum_scatter(terms_two, "lon", scatter_dimension=1, tiled=True),
    )
    grad_one, grad_two = (
        lax.psum_scatter(partly[0], "lat", scatter_dimension=2, tiled=True),
        lax.psum_scatter(partly[1], "lat", scatter_dimension=2, tiled=True),
    )
    conv1_grad = grad_one.reshape(3, 3, in_part, out_part)
    conv2_grad = grad_two.reshape(3, 3, in_part, out_part)
    return (output, input_grad, conv1_grad, conv2_grad)


def write_stack(field, stack_ref, band, step):
    cells, channels = field.shape
    wide = field.astype(F32)
    place = lax.broadcasted_iota(jnp.int32, (cells, channels), 0) % band
    above = jnp.where(place >= step, pltpu.roll(wide, step, 0), 0.0).astype(BF16)
    below = jnp.where(place < band - step, pltpu.roll(wide, cells - step, 0), 0.0).astype(BF16)
    for at, part in enumerate((above, field, below)):
        columns = slice(at * channels, (at + 1) * channels)
        stack_ref[band : band + cells, columns] = part
        stack_ref[0:band, columns] = part[cells - band :]
        stack_ref[band + cells :, columns] = part[0:band]


def convolved(stack_ref, weight_ref, band, cells, copies=None):
    total = None
    for b in range(3):
        if copies:
            copies[b].wait()
        channels = weight_ref.shape[2]
        tap = weight_ref[:, b].reshape(3 * channels, channels)
        term = jnp.dot(stack_ref[b * band : b * band + cells, :], tap, preferred_element_type=F32)
        total = term if total is None else total + term
    return total


def convolved_back(stack_ref, weight_ref, band, cells, copies=None):
    total = None
    for b in range(3):
        if copies:
            copies[b].wait()
        tap = jnp.concatenate([weight_ref[2 - a, 2 - b] for a in range(3)], axis=1)
        term = lax.dot_general(
            stack_ref[b * band : b * band + cells, :],
            tap,
            (((1,), (1,)), ((), ())),
            preferred_element_type=F32,
        )
        total = term if total is None else total + term
    return total


def one_hot_rows(cells, step, devices, back):
    to = lax.broadcasted_iota(jnp.int32, (cells, cells), 1 if back else 0)
    source = lax.broadcasted_iota(jnp.int32, (cells, cells), 0 if back else 1)
    rows = cells // (devices * step)
    device, row, column = to // (rows * step), (to // step) % rows, to % step
    return (source == (row * devices + device) * step + column).astype(BF16)


def deal_kernel(step, inputs_ref, cot_ref, out_ref, held_ref, sems):
    devices, _, rows, channels = out_ref.shape
    cells = devices * rows
    copies = fetched(((inputs_ref, held_ref.at[0]), (cot_ref, held_ref.at[1])), sems)
    chosen = one_hot_rows(cells, step, devices, False)
    for at, copy in enumerate(copies):
        copy.wait()
        field = held_ref[at].reshape(cells, channels)
        dealt = jnp.dot(chosen, field, preferred_element_type=F32).astype(BF16)
        out_ref[:, at] = dealt.reshape(devices, rows, channels)


def gather_kernel(step, fields_ref, output_ref, grad_ref):
    devices, _, rows, channels = fields_ref.shape
    cells = devices * rows
    chosen = one_hot_rows(cells, step, devices, True)
    for at, ref in enumerate((output_ref, grad_ref)):
        field = fields_ref[:, at].reshape(cells, channels)
        ref[...] = jnp.dot(chosen, field, preferred_element_type=F32).astype(BF16).reshape(ref.shape)


def fetched(pairs, sems):
    copies = [pltpu.make_async_copy(source, to, sems.at[at]) for at, (source, to) in enumerate(pairs)]
    for copy in copies:
        copy.start()
    return copies


def by_tap(weight_ref, held_ref, sems, order):
    return fetched([(weight_ref.at[:, b], held_ref.at[:, b]) for b in order], sems)


def inner_kernel(band, step, place_ref, own_ref, one_ref, two_ref,
                 hidden_ref, pre_ref, mine_ref, kept_ref, give_ref,
                 one_held, two_held, stack_ref, first_ref, slope_ref, turned_ref, sems):
    x, y, core = place_ref[0], place_ref[1], place_ref[2]
    cells, channels = first_ref.shape
    first_weight = by_tap(one_ref, one_held, sems.at[0], range(3))
    half, rows = channels // 2, 32
    deep = half // 4

    def turn(at, field):
        turned = field.T
        for h in range(2):
            for z in range(4):
                begin = (2 * z + h) * deep if at < 2 else h * half + z * deep
                turned_ref[at * 2 + h, z * deep : (z + 1) * deep, :] = turned[begin : begin + deep]

    source = own_ref[:, 0].reshape(cells, channels)
    write_stack(source, stack_ref, band, step)
    first_ref[...] = convolved(stack_ref, one_held, band, cells, first_weight)
    second_weight = by_tap(two_ref, two_held, sems.at[1], (2, 1, 0))
    turn(0, source)

    def activate(at, carry):
        span = pl.ds(pl.multiple_of(at * rows, rows), rows)
        first = first_ref[span, :]
        cdf = 0.5 * (1.0 + lax.erf(first * (0.5**0.5)))
        density = jnp.exp(-0.5 * first * first) * ((2.0 * jnp.pi) ** -0.5)
        hidden_ref[span, :] = (first * cdf).astype(BF16)
        slope_ref[span, :] = cdf + first * density
        return carry

    lax.fori_loop(0, cells // rows, activate, 0)
    turn(1, hidden_ref[...])
    cot = own_ref[:, 1].reshape(cells, channels)
    write_stack(cot, stack_ref, band, step)
    turn(3, cot)
    pre_ref[...] = (slope_ref[...] * convolved_back(stack_ref, two_held, band, cells, second_weight)).astype(BF16)
    turn(2, pre_ref[...])

    for ref, last_ref, of, side in (
        (mine_ref, kept_ref, core, jnp.where(core == 0, x, y)),
        (give_ref, give_ref.at[3], 1 - core, jnp.where(core == 0, y, x)),
    ):
        ref[0] = turned_ref[6 * of]
        ref[1] = turned_ref[6 * of + 1]
        ref[2] = turned_ref[4 - 2 * of + 1 - side]
        last_ref[...] = turned_ref[4 - 2 * of + side]


def outer_kernel(band, step, own_ref, hidden_ref, pre_ref, one_ref, two_ref, out_ref, stack_ref, back_ref):
    cells, channels = hidden_ref.shape
    shape = (out_ref.shape[0],) + out_ref.shape[2:]
    write_stack(hidden_ref[...], stack_ref, band, step)
    write_stack(pre_ref[...], back_ref, band, step)
    second = convolved(stack_ref, two_ref, band, cells)
    source = own_ref[:, 0].reshape(cells, channels)
    out_ref[:, 0] = (source.astype(F32) + second).astype(BF16).reshape(shape)
    back = convolved_back(back_ref, one_ref, band, cells)
    cot = own_ref[:, 1].reshape(cells, channels)
    out_ref[:, 1] = (cot.astype(F32) + back).astype(BF16).reshape(shape)


def units(deep):
    count = deep // 16
    for unit in range(9 * count):
        yield unit // count, (unit % count) * 16, (unit // 4) * 16, unit % 4


def terms_of(band, step, place_ref, sources, whole_ref, moved_ref, write):
    x, y, core = place_ref[0], place_ref[1], place_ref[2]
    half, cells = sources[0][1].shape
    place = lax.broadcasted_iota(jnp.int32, (half, cells), 1) % band
    inside = {
        1: jnp.where(place < band - step, 1.0, 0.0).astype(BF16),
        -1: jnp.where(place >= step, 1.0, 0.0).astype(BF16),
    }
    for at, (ref, moving_ref) in enumerate(sources):
        columns = slice(at * cells, (at + 1) * cells)
        whole_ref[0, :, columns] = ref[0]
        whole_ref[1, :, columns] = ref[1]
        field = moving_ref[...]
        for a in range(-1, 2):
            for b in range(-1, 2):
                shift = (-(b * band + a * step)) % cells
                part = pltpu.roll(field, shift, 1) if shift else field
                if a:
                    part = part * inside[a]
                tap = (a + 1) * 3 + b + 1
                moved_ref[jnp.where(core == 0, 8 - tap, tap), :, columns] = part
    moved = moved_ref[...].reshape(9 * half, len(sources) * cells)
    stays = jnp.where(core == 0, y, x)
    for at, which in enumerate((1 - stays, stays)):
        whole = whole_ref[which]

        @pl.when(core == 0)
        def _():
            write(at, slice(None), lax.dot_general(
                whole, moved, (((1,), (1,)), ((), ())), preferred_element_type=F32
            ))

        @pl.when(core == 1)
        def _():
            terms = lax.dot_general(moved, whole, (((1,), (1,)), ((), ())), preferred_element_type=F32)
            for tap in range(9):
                rows = slice(tap * half, (tap + 1) * half)
                write(at, rows, terms[rows])


def near_kernel(band, step, place_ref, mine_ref, kept_ref, got_ref, sums_ref, whole_ref, moved_ref):
    def write(at, columns, terms):
        sums_ref[at, :, columns] = terms

    sources = ((mine_ref, kept_ref), (got_ref, got_ref.at[3]))
    terms_of(band, step, place_ref, sources, whole_ref, moved_ref, write)


def far_kernel(band, step, place_ref, sums_ref, far_ref, pair_ref, keep_ref, give_ref, whole_ref, moved_ref):
    def write(at, columns, terms):
        ref = (give_ref, keep_ref)[at]
        ref[:, columns] = (sums_ref[at, :, columns] + terms).astype(ref.dtype)

    sources = ((far_ref, far_ref.at[2]), (pair_ref, pair_ref.at[2]))
    terms_of(band, step, place_ref, sources, whole_ref, moved_ref, write)


def pack_kernel(place_ref, keep_ref, got_ref, *refs):
    out_refs, (sums_ref, send_ref, sems) = refs[:-3], refs[-3:]
    me = place_ref[3] * 2 + place_ref[2]
    half = keep_ref.shape[0]
    sums_ref[...] = keep_ref[...] + got_ref[...].astype(F32)
    deep, quarter = half // 4, half // 2
    height = send_ref.shape[1]
    for z in range(4):
        for core in range(2):
            blocks = [[] for _ in range(height // 16)]
            for tap, row, to, _ in units(deep):
                begin, first = z * deep + row, tap * half + core * quarter
                blocks[to // 16].append(sums_ref[begin : begin + 16, first : first + quarter])
            for to, parts in enumerate(blocks):
                while len(parts) < 4:
                    parts.append(jnp.zeros((16, quarter), F32))
                send_ref[z * 2 + core, to * 16 : (to + 1) * 16, :] = jnp.concatenate(parts, axis=1).astype(BF16)
    pairs = [(send_ref.at[me ^ away], ref) for away, ref in enumerate(out_refs)]
    for copy in fetched(pairs, sems):
        copy.wait()


def finish_kernel(scale, place_ref, *refs):
    parts, (one_ref, two_ref) = refs[:-2], refs[-2:]
    core = place_ref[2]
    deep, quarter = one_ref.shape[2:]
    sums = []
    for other in range(2):
        total = parts[other][...].astype(F32)
        for ref in parts[other + 2 :: 2]:
            total = total + ref[...].astype(F32)
        sums.append(total * scale)
    ours, theirs = sums
    for out_ref, total in (
        (one_ref, jnp.where(core == 0, ours, theirs)),
        (two_ref, jnp.where(core == 0, theirs, ours)),
    ):
        for tap, row, begin, slot in units(deep):
            out_ref[tap // 3, tap % 3, row : row + 16, :] = total[
                begin : begin + 16, slot * quarter : (slot + 1) * quarter
            ]


def fast_local(inputs, conv1_weight, conv2_weight, cotangent):
    rows, width, channels = inputs.shape
    every = ("z", "y", "x", "core")
    devices = lax.axis_size(every)
    step = width // devices
    cells = rows * width
    lat = lax.axis_size("x") * lax.axis_size("core")
    lon = devices // lat
    band = rows * lat * step
    half, deep = channels // 2, channels // lon
    height = -(-9 * (deep // 16) // 4) * 16
    scale = (rows * lat * width * lon) ** (-0.5)
    flops = 2 * 9 * cells * channels * channels
    vmem, hbm, smem = (pl.BlockSpec(memory_space=space) for space in (pltpu.VMEM, pltpu.HBM, pltpu.SMEM))

    def held(*shape, kind=BF16):
        return pltpu.VMEM(shape, kind)

    def shaped(*shape, kind=BF16):
        return jax.ShapeDtypeStruct(shape, kind)

    def kernel(body, specs, arguments, out_shape, scratch_shapes, work, megabytes):
        return pl.pallas_call(
            body,
            out_shape=out_shape,
            in_specs=specs,
            out_specs=jax.tree.map(lambda _: vmem, out_shape),
            scratch_shapes=scratch_shapes,
            compiler_params=pltpu.CompilerParams(vmem_limit_bytes=24 * 2**20),
            cost_estimate=pl.CostEstimate(flops=work, bytes_accessed=megabytes * 2**20, transcendentals=0),
        )(*arguments)

    def passed(piece, x, y, core):
        pairs = [(i, i ^ (4 * (i % 2 == y) + 2 * (i % 2 == x) + core)) for i in range(8)]
        return lax.ppermute(piece, ("y", "x", "core"), pairs)

    stack = held(cells + 2 * band, 3 * channels)
    weights = held(*conv1_weight.shape)
    dealt = shaped(devices, 2, rows * step, channels)
    own = kernel(
        functools.partial(deal_kernel, step),
        [hbm] * 2,
        [pltpu.with_memory_space_constraint(field, pltpu.HBM) for field in (inputs, cotangent)],
        dealt,
        [held(2, *inputs.shape), pltpu.SemaphoreType.DMA((2,))],
        10**9,
        3,
    )
    own = lax.all_to_all(own, every, 0, 0, tiled=True)
    place = jnp.stack([lax.axis_index(axis) for axis in ("x", "y", "core", "z")]).astype(jnp.int32)
    one, two = (pltpu.with_memory_space_constraint(w, pltpu.HBM) for w in (conv1_weight, conv2_weight))
    taps = pltpu.SemaphoreType.DMA((2, 3))
    hidden, pre_grad, mine, kept, give = kernel(
        functools.partial(inner_kernel, band, step),
        [smem, vmem, hbm, hbm],
        (place, own, one, two),
        (
            held(cells, channels),
            held(cells, channels),
            held(3, half, cells),
            held(half, cells),
            held(4, half, cells),
        ),
        [
            weights,
            weights,
            stack,
            held(cells, channels, kind=F32),
            held(cells, channels, kind=F32),
            held(8, half, cells),
            taps,
        ],
        2 * flops,
        10,
    )
    got = passed(give, None, None, 1)
    far, far_pair = passed(mine, 0, 1, 0), passed(got[:3], 0, 1, 0)
    hidden, pre_grad, got = lax.optimization_barrier((hidden, pre_grad, got))
    fields = kernel(
        functools.partial(outer_kernel, band, step),
        [vmem] * 5,
        (own, hidden, pre_grad, conv1_weight, conv2_weight),
        dealt,
        [stack, stack],
        2 * flops,
        9,
    )
    _, far, far_pair = lax.optimization_barrier((fields, far, far_pair))
    fields = lax.all_to_all(fields, every, 0, 0, tiled=True)
    output, input_grad = kernel(
        functools.partial(gather_kernel, step), [vmem], (fields,), (shaped(*inputs.shape),) * 2, [], 10**9, 3
    )
    room = [held(2, half, 2 * cells), held(9, half, 2 * cells)]
    near = kernel(
        functools.partial(near_kernel, band, step),
        [smem] + [vmem] * 3,
        (place, mine, kept, got),
        held(2, half, 9 * half, kind=F32),
        room,
        2 * flops,
        6,
    )
    keep, give = kernel(
        functools.partial(far_kernel, band, step),
        [smem] + [vmem] * 3,
        (place, near, far, far_pair),
        (held(half, 9 * half, kind=F32), held(half, 9 * half)),
        room,
        3 * flops,
        6,
    )
    terms = kernel(
        pack_kernel,
        [smem] + [vmem] * 2,
        (place, keep, passed(give, 1, 0, 0)),
        (held(height, channels),) * 8,
        [held(half, 9 * half, kind=F32), held(8, height, channels), pltpu.SemaphoreType.DMA((8,))],
        2 * flops,
        4,
    )
    parts = list(terms)
    for away in (6, 7, 4, 5, 2, 3, 1):
        parts[away] = lax.ppermute(terms[away], ("z", "core"), [(i, i ^ away) for i in range(8)])
    output, input_grad, parts = lax.optimization_barrier((output, input_grad, parts))
    grad = shaped(3, 3, deep, half // 2, kind=F32)
    conv1_grad, conv2_grad = kernel(
        functools.partial(finish_kernel, scale), [smem] + [vmem] * 8, (place, *parts), (grad, grad), [], 10**6, 2
    )
    return (output, input_grad, conv1_grad, conv2_grad)


def is_fast(mesh):
    return dict(mesh.shape) == {"lon": 8, "lat": 4}


def solution(mesh):
    body, lon, lat = local, "lon", "lat"
    if is_fast(mesh):
        lon, lat = ("z", "y"), ("x", "core")
        mesh = jax.sharding.Mesh(mesh.devices.reshape(4, 2, 2, 2), lon + lat)
        body = fast_local
    field, grad = P(lat, lon, None), P(None, None, lon, lat)
    return jax.shard_map(
        body,
        mesh=mesh,
        in_specs=(field, P(), P(), field),
        out_specs=(field, field, grad, grad),
        check_vma=False,
    )
```

```python
import functools

import jax
import jax.numpy as jnp
from jax import lax
from jax.experimental import pallas as pl
from jax.experimental.pallas import tpu as pltpu
from jax.sharding import PartitionSpec as P

F32, BF16 = jnp.float32, jnp.bfloat16


def passed_along(shard, axis, by):
    length = lax.axis_size(axis)
    return lax.ppermute(shard, axis, [(i, (i + by) % length) for i in range(length)])


def padded(shard, sides, width):
    for axis, dim in sides:
        size, length = (lax.axis_size(axis), shard.shape[dim])
        up = [(i, (i + 1) % size) for i in range(size - 1)]
        down = [(j, i) for i, j in up]
        last = lax.slice_in_dim(shard, length - width, length, axis=dim)
        initial = lax.slice_in_dim(shard, 0, width, axis=dim)
        before = lax.ppermute(last, axis, up)
        after = lax.ppermute(initial, axis, down)
        shard = jnp.concatenate([before, shard, after], axis=dim)
    return shard


def extend(field):
    western = passed_along(field, "lon", 1)
    eastern = passed_along(field, "lon", -1)
    widened = jnp.concatenate([western, field, eastern], axis=1)
    return padded(widened, (("lat", 0),), 1)


def windows(padded_field, count_of_rows, lon_width, channels, direction):
    pieces = []
    for lat_step in (-1, 0, 1):
        for longitude_stride in (-1, 0, 1):
            row_start = 1 + direction * lat_step
            column_begin = lon_width + direction * lon_width * longitude_stride
            pieces.append(
                padded_field[
                    row_start : row_start + count_of_rows, column_begin : column_begin + lon_width
                ]
            )
    stacked = jnp.concatenate(pieces, axis=2)
    return stacked.reshape(count_of_rows * lon_width, 9 * channels)


def full_terms(stacked, grad, scale, channels):
    product = lax.dot_general(
        stacked, grad, (((0,), (0,)), ((), ())), preferred_element_type=jnp.float32
    )
    return (product * scale).reshape(9, channels, channels)


def local(inputs, conv1_weight, conv2_weight, cotangent):
    count_of_rows, lon_width, channels = inputs.shape
    cells = count_of_rows * lon_width
    lon_count = lax.axis_size("lon")
    latitude_count = lax.axis_size("lat")
    scale = (count_of_rows * latitude_count * lon_width * lon_count) ** (-0.5)
    forward_one = conv1_weight.reshape(9 * channels, channels)
    forward_two = conv2_weight.reshape(9 * channels, channels)
    turned_one = jnp.swapaxes(conv1_weight, 2, 3).reshape(9 * channels, channels)
    turned_two = jnp.swapaxes(conv2_weight, 2, 3).reshape(9 * channels, channels)
    source_field, cot_field = (inputs, cotangent)

    def stack_of(field, direction):
        return windows(extend(field), count_of_rows, lon_width, channels, direction)

    def as_field(flat):
        return flat.reshape(count_of_rows, lon_width, channels)

    stack_input = stack_of(source_field, 1)
    first = jnp.dot(stack_input, forward_one, preferred_element_type=jnp.float32)
    cdf = 0.5 * (1.0 + jax.scipy.special.erf(first / jnp.sqrt(2.0)))
    hidden = (first * cdf).astype(jnp.bfloat16)
    stack_hidden = stack_of(as_field(hidden), 1)
    second = jnp.dot(stack_hidden, forward_two, preferred_element_type=jnp.float32)
    flat_input = source_field.reshape(cells, channels)
    output = (flat_input.astype(jnp.float32) + second).astype(jnp.bfloat16)
    flat_cot = cot_field.reshape(cells, channels)
    stacked_cotangent = stack_of(cot_field, -1)
    upstream = jnp.dot(stacked_cotangent, turned_two, preferred_element_type=jnp.float32)
    density = jnp.exp(-0.5 * first * first) / jnp.sqrt(2.0 * jnp.pi)
    pre_grad = (upstream * (cdf + first * density)).astype(jnp.bfloat16)
    stack_pre = stack_of(as_field(pre_grad), -1)
    back = jnp.dot(stack_pre, turned_one, preferred_element_type=jnp.float32)
    input_grad = (flat_cot.astype(jnp.float32) + back).astype(jnp.bfloat16)
    output = output.reshape(count_of_rows, lon_width, channels)
    input_grad = input_grad.reshape(count_of_rows, lon_width, channels)
    in_part = channels // lon_count
    out_part = channels // latitude_count
    terms_one = full_terms(stack_input, pre_grad, scale, channels)
    terms_two = full_terms(stack_hidden, flat_cot, scale, channels)
    partly = (
        lax.psum_scatter(terms_one, "lon", scatter_dimension=1, tiled=True),
        lax.psum_scatter(terms_two, "lon", scatter_dimension=1, tiled=True),
    )
    grad_one, grad_two = (
        lax.psum_scatter(partly[0], "lat", scatter_dimension=2, tiled=True),
        lax.psum_scatter(partly[1], "lat", scatter_dimension=2, tiled=True),
    )
    conv1_grad = grad_one.reshape(3, 3, in_part, out_part)
    conv2_grad = grad_two.reshape(3, 3, in_part, out_part)
    return (output, input_grad, conv1_grad, conv2_grad)


def write_stack(field, stack_ref, band, step):
    cells, channels = field.shape
    wide = field.astype(F32)
    place = lax.broadcasted_iota(jnp.int32, (cells, channels), 0) % band
    above = jnp.where(place >= step, pltpu.roll(wide, step, 0), 0.0).astype(BF16)
    below = jnp.where(place < band - step, pltpu.roll(wide, cells - step, 0), 0.0).astype(BF16)
    for at, part in enumerate((above, field, below)):
        columns = slice(at * channels, (at + 1) * channels)
        stack_ref[band : band + cells, columns] = part
        stack_ref[0:band, columns] = part[cells - band :]
        stack_ref[band + cells :, columns] = part[0:band]


def convolved(stack_ref, weight_ref, band, cells):
    total = None
    for b in range(3):
        channels = weight_ref.shape[2]
        tap = weight_ref[:, b].reshape(3 * channels, channels)
        term = jnp.dot(stack_ref[b * band : b * band + cells, :], tap, preferred_element_type=F32)
        total = term if total is None else total + term
    return total


def convolved_back(stack_ref, weight_ref, band, cells):
    total = None
    for b in range(3):
        tap = jnp.concatenate([weight_ref[2 - a, 2 - b] for a in range(3)], axis=1)
        term = lax.dot_general(
            stack_ref[b * band : b * band + cells, :],
            tap,
            (((1,), (1,)), ((), ())),
            preferred_element_type=F32,
        )
        total = term if total is None else total + term
    return total


def one_hot_rows(cells, step, devices, back):
    to = lax.broadcasted_iota(jnp.int32, (cells, cells), 1 if back else 0)
    source = lax.broadcasted_iota(jnp.int32, (cells, cells), 0 if back else 1)
    rows = cells // (devices * step)
    device, inner = lax.div(to, rows * step), lax.rem(to, rows * step)
    row, column = lax.div(inner, step), lax.rem(inner, step)
    return (source == (row * devices + device) * step + column).astype(BF16)


def deal_kernel(step, inputs_ref, cot_ref, out_ref, held_ref, sems):
    devices, _, rows, channels = out_ref.shape
    cells = devices * rows
    copies = fetched(((inputs_ref, held_ref.at[0]), (cot_ref, held_ref.at[1])), sems)
    chosen = one_hot_rows(cells, step, devices, False)
    for at, copy in enumerate(copies):
        copy.wait()
        field = held_ref[at].reshape(cells, channels)
        dealt = jnp.dot(chosen, field, preferred_element_type=F32).astype(BF16)
        out_ref[:, at] = dealt.reshape(devices, rows, channels)


def gather_kernel(step, fields_ref, output_ref, grad_ref):
    devices, _, rows, channels = fields_ref.shape
    cells = devices * rows
    chosen = one_hot_rows(cells, step, devices, True)
    for at, ref in enumerate((output_ref, grad_ref)):
        field = fields_ref[:, at].reshape(cells, channels)
        ref[...] = jnp.dot(chosen, field, preferred_element_type=F32).astype(BF16).reshape(ref.shape)


def fetched(pairs, sems):
    copies = [pltpu.make_async_copy(source, to, sems.at[at]) for at, (source, to) in enumerate(pairs)]
    for copy in copies:
        copy.start()
    return copies


def inner_kernel(band, step, place_ref, own_ref, one_ref, two_ref,
                 hidden_ref, pre_ref, mine_ref, kept_ref, give_ref,
                 stack_ref, first_ref, slope_ref, turned_ref):
    x, y, core = place_ref[0], place_ref[1], place_ref[2]
    cells, channels = first_ref.shape
    half, rows = channels // 2, 32
    deep = half // 4

    def turn(at, field):
        turned = field.T
        for h in range(2):
            for z in range(4):
                begin = (2 * z + h) * deep if at < 2 else h * half + z * deep
                turned_ref[at * 2 + h, z * deep : (z + 1) * deep, :] = turned[begin : begin + deep]

    source = own_ref[:, 0].reshape(cells, channels)
    write_stack(source, stack_ref, band, step)
    first_ref[...] = convolved(stack_ref, one_ref, band, cells)
    turn(0, source)

    def activate(at, carry):
        span = pl.ds(pl.multiple_of(at * rows, rows), rows)
        first = first_ref[span, :]
        cdf = 0.5 * (1.0 + lax.erf(first * (0.5**0.5)))
        density = jnp.exp(-0.5 * first * first) * ((2.0 * jnp.pi) ** -0.5)
        hidden_ref[span, :] = (first * cdf).astype(BF16)
        slope_ref[span, :] = cdf + first * density
        return carry

    lax.fori_loop(0, cells // rows, activate, 0)
    turn(1, hidden_ref[...])
    cot = own_ref[:, 1].reshape(cells, channels)
    write_stack(cot, stack_ref, band, step)
    turn(3, cot)
    pre_ref[...] = (slope_ref[...] * convolved_back(stack_ref, two_ref, band, cells)).astype(BF16)
    turn(2, pre_ref[...])

    for ref, last_ref, of, side in (
        (mine_ref, kept_ref, core, jnp.where(core == 0, x, y)),
        (give_ref, give_ref.at[3], 1 - core, jnp.where(core == 0, y, x)),
    ):
        ref[0] = turned_ref[6 * of]
        ref[1] = turned_ref[6 * of + 1]
        ref[2] = turned_ref[4 - 2 * of + 1 - side]
        last_ref[...] = turned_ref[4 - 2 * of + side]


def outer_kernel(band, step, own_ref, hidden_ref, pre_ref, one_ref, two_ref, out_ref, stack_ref, back_ref):
    cells, channels = hidden_ref.shape
    shape = (out_ref.shape[0],) + out_ref.shape[2:]
    write_stack(hidden_ref[...], stack_ref, band, step)
    write_stack(pre_ref[...], back_ref, band, step)
    second = convolved(stack_ref, two_ref, band, cells)
    source = own_ref[:, 0].reshape(cells, channels)
    out_ref[:, 0] = (source.astype(F32) + second).astype(BF16).reshape(shape)
    back = convolved_back(back_ref, one_ref, band, cells)
    cot = own_ref[:, 1].reshape(cells, channels)
    out_ref[:, 1] = (cot.astype(F32) + back).astype(BF16).reshape(shape)


def units(deep):
    count = deep // 16
    for unit in range(9 * count):
        yield unit // count, (unit % count) * 16, (unit // 4) * 16, unit % 4


def terms_of(band, step, place_ref, sources, whole_ref, moved_ref, write):
    x, y, core = place_ref[0], place_ref[1], place_ref[2]
    half, cells = sources[0][1].shape
    place = lax.broadcasted_iota(jnp.int32, (half, cells), 1) % band
    inside = {
        1: jnp.where(place < band - step, 1.0, 0.0).astype(BF16),
        -1: jnp.where(place >= step, 1.0, 0.0).astype(BF16),
    }
    for at, (ref, moving_ref) in enumerate(sources):
        columns = slice(at * cells, (at + 1) * cells)
        whole_ref[0, :, columns] = ref[0]
        whole_ref[1, :, columns] = ref[1]
        field = moving_ref[...]
        for a in range(-1, 2):
            for b in range(-1, 2):
                shift = (-(b * band + a * step)) % cells
                part = pltpu.roll(field, shift, 1) if shift else field
                if a:
                    part = part * inside[a]
                tap = (a + 1) * 3 + b + 1
                moved_ref[jnp.where(core == 0, 8 - tap, tap), :, columns] = part
    moved = moved_ref[...].reshape(9 * half, len(sources) * cells)
    stays = jnp.where(core == 0, y, x)
    for at, which in enumerate((1 - stays, stays)):
        whole = whole_ref[which]

        @pl.when(core == 0)
        def _():
            write(at, slice(None), lax.dot_general(
                whole, moved, (((1,), (1,)), ((), ())), preferred_element_type=F32
            ))

        @pl.when(core == 1)
        def _():
            terms = lax.dot_general(moved, whole, (((1,), (1,)), ((), ())), preferred_element_type=F32)
            for tap in range(9):
                rows = slice(tap * half, (tap + 1) * half)
                write(at, rows, terms[rows])


def near_kernel(band, step, place_ref, mine_ref, kept_ref, got_ref, sums_ref, whole_ref, moved_ref):
    def write(at, columns, terms):
        sums_ref[at, :, columns] = terms

    sources = ((mine_ref, kept_ref), (got_ref, got_ref.at[3]))
    terms_of(band, step, place_ref, sources, whole_ref, moved_ref, write)


def far_kernel(band, step, place_ref, sums_ref, far_ref, pair_ref, keep_ref, give_ref, whole_ref, moved_ref):
    def write(at, columns, terms):
        ref = (give_ref, keep_ref)[at]
        ref[:, columns] = (sums_ref[at, :, columns] + terms).astype(ref.dtype)

    sources = ((far_ref, far_ref.at[2]), (pair_ref, pair_ref.at[2]))
    terms_of(band, step, place_ref, sources, whole_ref, moved_ref, write)


def pack_kernel(place_ref, keep_ref, got_ref, *refs):
    out_refs, (sums_ref, send_ref, sems) = refs[:-3], refs[-3:]
    me = place_ref[3] * 2 + place_ref[2]
    half = keep_ref.shape[0]
    sums_ref[...] = keep_ref[...] + got_ref[...].astype(F32)
    deep, quarter = half // 4, half // 2
    height = send_ref.shape[1]
    for z in range(4):
        for core in range(2):
            blocks = [[] for _ in range(height // 16)]
            for tap, row, to, _ in units(deep):
                begin, first = z * deep + row, tap * half + core * quarter
                blocks[to // 16].append(sums_ref[begin : begin + 16, first : first + quarter])
            for to, parts in enumerate(blocks):
                while len(parts) < 4:
                    parts.append(jnp.zeros((16, quarter), F32))
                send_ref[z * 2 + core, to * 16 : (to + 1) * 16, :] = jnp.concatenate(parts, axis=1).astype(BF16)
    pairs = [(send_ref.at[me ^ away], ref) for away, ref in enumerate(out_refs)]
    for copy in fetched(pairs, sems):
        copy.wait()


def finish_kernel(scale, place_ref, *refs):
    parts, (one_ref, two_ref) = refs[:-2], refs[-2:]
    core = place_ref[2]
    deep, quarter = one_ref.shape[2:]
    sums = []
    for other in range(2):
        total = parts[other][...].astype(F32)
        for ref in parts[other + 2 :: 2]:
            total = total + ref[...].astype(F32)
        sums.append(total * scale)
    ours, theirs = sums
    for out_ref, total in (
        (one_ref, jnp.where(core == 0, ours, theirs)),
        (two_ref, jnp.where(core == 0, theirs, ours)),
    ):
        for tap, row, begin, slot in units(deep):
            out_ref[tap // 3, tap % 3, row : row + 16, :] = total[
                begin : begin + 16, slot * quarter : (slot + 1) * quarter
            ]


def fast_local(inputs, conv1_weight, conv2_weight, cotangent):
    rows, width, channels = inputs.shape
    every = ("z", "y", "x", "core")
    devices = lax.axis_size(every)
    step = width // devices
    cells = rows * width
    lat = lax.axis_size("x") * lax.axis_size("core")
    lon = devices // lat
    band = rows * lat * step
    half, deep = channels // 2, channels // lon
    height = -(-9 * (deep // 16) // 4) * 16
    scale = (rows * lat * width * lon) ** (-0.5)
    flops = 2 * 9 * cells * channels * channels
    vmem, hbm, smem = (pl.BlockSpec(memory_space=space) for space in (pltpu.VMEM, pltpu.HBM, pltpu.SMEM))

    def held(*shape, kind=BF16):
        return pltpu.VMEM(shape, kind)

    def shaped(*shape, kind=BF16):
        return jax.ShapeDtypeStruct(shape, kind)

    def kernel(body, specs, arguments, out_shape, scratch_shapes, work, megabytes):
        return pl.pallas_call(
            body,
            out_shape=out_shape,
            in_specs=specs,
            out_specs=jax.tree.map(lambda _: vmem, out_shape),
            scratch_shapes=scratch_shapes,
            compiler_params=pltpu.CompilerParams(vmem_limit_bytes=24 * 2**20),
            cost_estimate=pl.CostEstimate(flops=work, bytes_accessed=megabytes * 2**20, transcendentals=0),
        )(*arguments)

    def passed(piece, x, y, core):
        pairs = [(i, i ^ (4 * (i % 2 == y) + 2 * (i % 2 == x) + core)) for i in range(8)]
        return lax.ppermute(piece, ("y", "x", "core"), pairs)

    stack = held(cells + 2 * band, 3 * channels)
    dealt = shaped(devices, 2, rows * step, channels)
    own = kernel(
        functools.partial(deal_kernel, step),
        [hbm] * 2,
        [pltpu.with_memory_space_constraint(field, pltpu.HBM) for field in (inputs, cotangent)],
        dealt,
        [held(2, *inputs.shape), pltpu.SemaphoreType.DMA((2,))],
        10**9,
        3,
    )
    own = lax.all_to_all(own, every, 0, 0, tiled=True)
    place = jnp.stack([lax.axis_index(axis) for axis in ("x", "y", "core", "z")]).astype(jnp.int32)
    hidden, pre_grad, mine, kept, give = kernel(
        functools.partial(inner_kernel, band, step),
        [smem] + [vmem] * 3,
        (place, own, conv1_weight, conv2_weight),
        (
            held(cells, channels),
            held(cells, channels),
            held(3, half, cells),
            held(half, cells),
            held(4, half, cells),
        ),
        [
            stack,
            held(cells, channels, kind=F32),
            held(cells, channels, kind=F32),
            held(8, half, cells),
        ],
        2 * flops,
        10,
    )
    got = passed(give, None, None, 1)
    far, far_pair = passed(mine, 0, 1, 0), passed(got[:3], 0, 1, 0)
    hidden, pre_grad, got = lax.optimization_barrier((hidden, pre_grad, got))
    fields = kernel(
        functools.partial(outer_kernel, band, step),
        [vmem] * 5,
        (own, hidden, pre_grad, conv1_weight, conv2_weight),
        dealt,
        [stack, stack],
        2 * flops,
        9,
    )
    _, far, far_pair = lax.optimization_barrier((fields, far, far_pair))
    fields = lax.all_to_all(fields, every, 0, 0, tiled=True)
    output, input_grad = kernel(
        functools.partial(gather_kernel, step), [vmem], (fields,), (shaped(*inputs.shape),) * 2, [], 10**9, 3
    )
    room = [held(2, half, 2 * cells), held(9, half, 2 * cells)]
    near = kernel(
        functools.partial(near_kernel, band, step),
        [smem] + [vmem] * 3,
        (place, mine, kept, got),
        held(2, half, 9 * half, kind=F32),
        room,
        2 * flops,
        6,
    )
    keep, give = kernel(
        functools.partial(far_kernel, band, step),
        [smem] + [vmem] * 3,
        (place, near, far, far_pair),
        (held(half, 9 * half, kind=F32), held(half, 9 * half)),
        room,
        3 * flops,
        6,
    )
    terms = kernel(
        pack_kernel,
        [smem] + [vmem] * 2,
        (place, keep, passed(give, 1, 0, 0)),
        (held(height, channels),) * 8,
        [held(half, 9 * half, kind=F32), held(8, height, channels), pltpu.SemaphoreType.DMA((8,))],
        2 * flops,
        4,
    )
    parts = list(terms)
    for away in (6, 7, 4, 5, 2, 3, 1):
        parts[away] = lax.ppermute(terms[away], ("z", "core"), [(i, i ^ away) for i in range(8)])
    output, input_grad, parts = lax.optimization_barrier((output, input_grad, parts))
    grad = shaped(3, 3, deep, half // 2, kind=F32)
    conv1_grad, conv2_grad = kernel(
        functools.partial(finish_kernel, scale), [smem] + [vmem] * 8, (place, *parts), (grad, grad), [], 10**6, 2
    )
    return (output, input_grad, conv1_grad, conv2_grad)


def is_fast(mesh):
    return dict(mesh.shape) == {"lon": 8, "lat": 4}


def solution(mesh):
    body, lon, lat = local, "lon", "lat"
    if is_fast(mesh):
        lon, lat = ("z", "y"), ("x", "core")
        mesh = jax.sharding.Mesh(mesh.devices.reshape(4, 2, 2, 2), lon + lat)
        body = fast_local
    field, grad = P(lat, lon, None), P(None, None, lon, lat)
    return jax.shard_map(
        body,
        mesh=mesh,
        in_specs=(field, P(), P(), field),
        out_specs=(field, field, grad, grad),
        check_vma=False,
    )
```

```python
import functools

import jax
import jax.numpy as jnp
from jax import lax
from jax.experimental import pallas as pl
from jax.experimental.pallas import tpu as pltpu
from jax.sharding import PartitionSpec as P

F32, BF16 = jnp.float32, jnp.bfloat16


def passed_along(shard, axis, by):
    length = lax.axis_size(axis)
    return lax.ppermute(shard, axis, [(i, (i + by) % length) for i in range(length)])


def padded(shard, sides, width):
    for axis, dim in sides:
        size, length = (lax.axis_size(axis), shard.shape[dim])
        up = [(i, (i + 1) % size) for i in range(size - 1)]
        down = [(j, i) for i, j in up]
        last = lax.slice_in_dim(shard, length - width, length, axis=dim)
        initial = lax.slice_in_dim(shard, 0, width, axis=dim)
        before = lax.ppermute(last, axis, up)
        after = lax.ppermute(initial, axis, down)
        shard = jnp.concatenate([before, shard, after], axis=dim)
    return shard


def extend(field):
    western = passed_along(field, "lon", 1)
    eastern = passed_along(field, "lon", -1)
    widened = jnp.concatenate([western, field, eastern], axis=1)
    return padded(widened, (("lat", 0),), 1)


def windows(padded_field, count_of_rows, lon_width, channels, direction):
    pieces = []
    for lat_step in (-1, 0, 1):
        for longitude_stride in (-1, 0, 1):
            row_start = 1 + direction * lat_step
            column_begin = lon_width + direction * lon_width * longitude_stride
            pieces.append(
                padded_field[
                    row_start : row_start + count_of_rows, column_begin : column_begin + lon_width
                ]
            )
    stacked = jnp.concatenate(pieces, axis=2)
    return stacked.reshape(count_of_rows * lon_width, 9 * channels)


def full_terms(stacked, grad, scale, channels):
    product = lax.dot_general(
        stacked, grad, (((0,), (0,)), ((), ())), preferred_element_type=jnp.float32
    )
    return (product * scale).reshape(9, channels, channels)


def local(inputs, conv1_weight, conv2_weight, cotangent):
    count_of_rows, lon_width, channels = inputs.shape
    cells = count_of_rows * lon_width
    lon_count = lax.axis_size("lon")
    latitude_count = lax.axis_size("lat")
    scale = (count_of_rows * latitude_count * lon_width * lon_count) ** (-0.5)
    forward_one = conv1_weight.reshape(9 * channels, channels)
    forward_two = conv2_weight.reshape(9 * channels, channels)
    turned_one = jnp.swapaxes(conv1_weight, 2, 3).reshape(9 * channels, channels)
    turned_two = jnp.swapaxes(conv2_weight, 2, 3).reshape(9 * channels, channels)
    source_field, cot_field = (inputs, cotangent)

    def stack_of(field, direction):
        return windows(extend(field), count_of_rows, lon_width, channels, direction)

    def as_field(flat):
        return flat.reshape(count_of_rows, lon_width, channels)

    stack_input = stack_of(source_field, 1)
    first = jnp.dot(stack_input, forward_one, preferred_element_type=jnp.float32)
    cdf = 0.5 * (1.0 + jax.scipy.special.erf(first / jnp.sqrt(2.0)))
    hidden = (first * cdf).astype(jnp.bfloat16)
    stack_hidden = stack_of(as_field(hidden), 1)
    second = jnp.dot(stack_hidden, forward_two, preferred_element_type=jnp.float32)
    flat_input = source_field.reshape(cells, channels)
    output = (flat_input.astype(jnp.float32) + second).astype(jnp.bfloat16)
    flat_cot = cot_field.reshape(cells, channels)
    stacked_cotangent = stack_of(cot_field, -1)
    upstream = jnp.dot(stacked_cotangent, turned_two, preferred_element_type=jnp.float32)
    density = jnp.exp(-0.5 * first * first) / jnp.sqrt(2.0 * jnp.pi)
    pre_grad = (upstream * (cdf + first * density)).astype(jnp.bfloat16)
    stack_pre = stack_of(as_field(pre_grad), -1)
    back = jnp.dot(stack_pre, turned_one, preferred_element_type=jnp.float32)
    input_grad = (flat_cot.astype(jnp.float32) + back).astype(jnp.bfloat16)
    output = output.reshape(count_of_rows, lon_width, channels)
    input_grad = input_grad.reshape(count_of_rows, lon_width, channels)
    in_part = channels // lon_count
    out_part = channels // latitude_count
    terms_one = full_terms(stack_input, pre_grad, scale, channels)
    terms_two = full_terms(stack_hidden, flat_cot, scale, channels)
    partly = (
        lax.psum_scatter(terms_one, "lon", scatter_dimension=1, tiled=True),
        lax.psum_scatter(terms_two, "lon", scatter_dimension=1, tiled=True),
    )
    grad_one, grad_two = (
        lax.psum_scatter(partly[0], "lat", scatter_dimension=2, tiled=True),
        lax.psum_scatter(partly[1], "lat", scatter_dimension=2, tiled=True),
    )
    conv1_grad = grad_one.reshape(3, 3, in_part, out_part)
    conv2_grad = grad_two.reshape(3, 3, in_part, out_part)
    return (output, input_grad, conv1_grad, conv2_grad)


def write_stack(field, stack_ref, band, step):
    cells, channels = field.shape
    wide = field.astype(F32)
    place = lax.broadcasted_iota(jnp.int32, (cells, channels), 0) % band
    above = jnp.where(place >= step, pltpu.roll(wide, step, 0), 0.0).astype(BF16)
    below = jnp.where(place < band - step, pltpu.roll(wide, cells - step, 0), 0.0).astype(BF16)
    for at, part in enumerate((above, field, below)):
        columns = slice(at * channels, (at + 1) * channels)
        stack_ref[band : band + cells, columns] = part
        stack_ref[0:band, columns] = part[cells - band :]
        stack_ref[band + cells :, columns] = part[0:band]


def convolved(stack_ref, weight_ref, band, cells, copies=None):
    total = None
    for b in range(3):
        if copies:
            copies[b].wait()
        channels = weight_ref.shape[2]
        tap = weight_ref[:, b].reshape(3 * channels, channels)
        term = jnp.dot(stack_ref[b * band : b * band + cells, :], tap, preferred_element_type=F32)
        total = term if total is None else total + term
    return total


def convolved_back(stack_ref, weight_ref, band, cells, copies=None):
    total = None
    for b in range(3):
        if copies:
            copies[b].wait()
        tap = jnp.concatenate([weight_ref[2 - a, 2 - b] for a in range(3)], axis=1)
        term = lax.dot_general(
            stack_ref[b * band : b * band + cells, :],
            tap,
            (((1,), (1,)), ((), ())),
            preferred_element_type=F32,
        )
        total = term if total is None else total + term
    return total


def one_hot_rows(cells, step, devices, back):
    to = lax.broadcasted_iota(jnp.int32, (cells, cells), 1 if back else 0)
    source = lax.broadcasted_iota(jnp.int32, (cells, cells), 0 if back else 1)
    rows = cells // (devices * step)
    device, row, column = to // (rows * step), (to // step) % rows, to % step
    return (source == (row * devices + device) * step + column).astype(BF16)


def deal_kernel(step, inputs_ref, cot_ref, out_ref, held_ref, sems):
    devices, _, rows, channels = out_ref.shape
    cells = devices * rows
    copies = fetched(((inputs_ref, held_ref.at[0]), (cot_ref, held_ref.at[1])), sems)
    chosen = one_hot_rows(cells, step, devices, False)
    for at, copy in enumerate(copies):
        copy.wait()
        field = held_ref[at].reshape(cells, channels)
        dealt = jnp.dot(chosen, field, preferred_element_type=F32).astype(BF16)
        out_ref[:, at] = dealt.reshape(devices, rows, channels)


def gather_kernel(step, fields_ref, output_ref, grad_ref):
    devices, _, rows, channels = fields_ref.shape
    cells = devices * rows
    chosen = one_hot_rows(cells, step, devices, True)
    for at, ref in enumerate((output_ref, grad_ref)):
        field = fields_ref[:, at].reshape(cells, channels)
        ref[...] = jnp.dot(chosen, field, preferred_element_type=F32).astype(BF16).reshape(ref.shape)


def fetched(pairs, sems):
    copies = [pltpu.make_async_copy(source, to, sems.at[at]) for at, (source, to) in enumerate(pairs)]
    for copy in copies:
        copy.start()
    return copies


def by_tap(weight_ref, held_ref, sems, order):
    return fetched([(weight_ref.at[:, b], held_ref.at[:, b]) for b in order], sems)


def inner_kernel(band, step, place_ref, own_ref, one_ref, two_ref,
                 hidden_ref, pre_ref, mine_ref, kept_ref, give_ref,
                 one_held, two_held, stack_ref, cot_stack_ref, first_ref, slope_ref, turned_ref, sems):
    x, y, core = place_ref[0], place_ref[1], place_ref[2]
    cells, channels = first_ref.shape
    first_weight = by_tap(one_ref, one_held, sems.at[0], range(3))
    half, rows = channels // 2, 32
    deep = half // 4

    def turn(at, field):
        turned = field.T
        for h in range(2):
            for z in range(4):
                begin = (2 * z + h) * deep if at < 2 else h * half + z * deep
                turned_ref[at * 2 + h, z * deep : (z + 1) * deep, :] = turned[begin : begin + deep]

    source = own_ref[:, 0].reshape(cells, channels)
    cot = own_ref[:, 1].reshape(cells, channels)
    write_stack(source, stack_ref, band, step)
    write_stack(cot, cot_stack_ref, band, step)
    turn(0, source)
    turn(3, cot)
    first_ref[...] = convolved(stack_ref, one_held, band, cells, first_weight)
    second_weight = by_tap(two_ref, two_held, sems.at[1], (2, 1, 0))

    def activate(at, carry):
        span = pl.ds(pl.multiple_of(at * rows, rows), rows)
        first = first_ref[span, :]
        cdf = 0.5 * (1.0 + lax.erf(first * (0.5**0.5)))
        density = jnp.exp(-0.5 * first * first) * ((2.0 * jnp.pi) ** -0.5)
        hidden_ref[span, :] = (first * cdf).astype(BF16)
        slope_ref[span, :] = cdf + first * density
        return carry

    lax.fori_loop(0, cells // rows, activate, 0)
    turn(1, hidden_ref[...])
    pre_ref[...] = (slope_ref[...] * convolved_back(cot_stack_ref, two_held, band, cells, second_weight)).astype(BF16)
    turn(2, pre_ref[...])

    for ref, last_ref, of, side in (
        (mine_ref, kept_ref, core, jnp.where(core == 0, x, y)),
        (give_ref, give_ref.at[3], 1 - core, jnp.where(core == 0, y, x)),
    ):
        ref[0] = turned_ref[6 * of]
        ref[1] = turned_ref[6 * of + 1]
        ref[2] = turned_ref[4 - 2 * of + 1 - side]
        last_ref[...] = turned_ref[4 - 2 * of + side]


def outer_kernel(band, step, own_ref, hidden_ref, pre_ref, one_ref, two_ref, out_ref, stack_ref, back_ref):
    cells, channels = hidden_ref.shape
    shape = (out_ref.shape[0],) + out_ref.shape[2:]
    write_stack(hidden_ref[...], stack_ref, band, step)
    write_stack(pre_ref[...], back_ref, band, step)
    second = convolved(stack_ref, two_ref, band, cells)
    source = own_ref[:, 0].reshape(cells, channels)
    out_ref[:, 0] = (source.astype(F32) + second).astype(BF16).reshape(shape)
    back = convolved_back(back_ref, one_ref, band, cells)
    cot = own_ref[:, 1].reshape(cells, channels)
    out_ref[:, 1] = (cot.astype(F32) + back).astype(BF16).reshape(shape)


def units(deep):
    count = deep // 16
    for unit in range(9 * count):
        yield unit // count, (unit % count) * 16, (unit // 4) * 16, unit % 4


def terms_of(band, step, place_ref, sources, whole_ref, moved_ref, write):
    x, y, core = place_ref[0], place_ref[1], place_ref[2]
    half, cells = sources[0][1].shape
    place = lax.broadcasted_iota(jnp.int32, (half, cells), 1) % band
    inside = {
        1: jnp.where(place < band - step, 1.0, 0.0).astype(BF16),
        -1: jnp.where(place >= step, 1.0, 0.0).astype(BF16),
    }
    for at, (ref, moving_ref) in enumerate(sources):
        columns = slice(at * cells, (at + 1) * cells)
        whole_ref[0, :, columns] = ref[0]
        whole_ref[1, :, columns] = ref[1]
        field = moving_ref[...]
        for a in range(-1, 2):
            for b in range(-1, 2):
                shift = (-(b * band + a * step)) % cells
                part = pltpu.roll(field, shift, 1) if shift else field
                if a:
                    part = part * inside[a]
                tap = (a + 1) * 3 + b + 1
                moved_ref[jnp.where(core == 0, 8 - tap, tap), :, columns] = part
    moved = moved_ref[...].reshape(9 * half, len(sources) * cells)
    stays = jnp.where(core == 0, y, x)
    for at, which in enumerate((1 - stays, stays)):
        whole = whole_ref[which]

        @pl.when(core == 0)
        def _():
            write(at, slice(None), lax.dot_general(
                whole, moved, (((1,), (1,)), ((), ())), preferred_element_type=F32
            ))

        @pl.when(core == 1)
        def _():
            terms = lax.dot_general(moved, whole, (((1,), (1,)), ((), ())), preferred_element_type=F32)
            for tap in range(9):
                rows = slice(tap * half, (tap + 1) * half)
                write(at, rows, terms[rows])


def near_kernel(band, step, place_ref, mine_ref, kept_ref, got_ref, sums_ref, whole_ref, moved_ref):
    def write(at, columns, terms):
        sums_ref[at, :, columns] = terms

    sources = ((mine_ref, kept_ref), (got_ref, got_ref.at[3]))
    terms_of(band, step, place_ref, sources, whole_ref, moved_ref, write)


def far_kernel(band, step, place_ref, sums_ref, far_ref, pair_ref, keep_ref, give_ref, whole_ref, moved_ref):
    def write(at, columns, terms):
        ref = (give_ref, keep_ref)[at]
        ref[:, columns] = (sums_ref[at, :, columns] + terms).astype(ref.dtype)

    sources = ((far_ref, far_ref.at[2]), (pair_ref, pair_ref.at[2]))
    terms_of(band, step, place_ref, sources, whole_ref, moved_ref, write)


def pack_kernel(place_ref, keep_ref, got_ref, *refs):
    out_refs, (sums_ref, send_ref, sems) = refs[:-3], refs[-3:]
    me = place_ref[3] * 2 + place_ref[2]
    half = keep_ref.shape[0]
    sums_ref[...] = (keep_ref[...] + got_ref[...].astype(F32)).astype(BF16)
    deep, quarter = half // 4, half // 2
    height = send_ref.shape[1]
    for z in range(4):
        for core in range(2):
            blocks = [[] for _ in range(height // 16)]
            for tap, row, to, _ in units(deep):
                begin, first = z * deep + row, tap * half + core * quarter
                blocks[to // 16].append(sums_ref[begin : begin + 16, first : first + quarter])
            for to, parts in enumerate(blocks):
                while len(parts) < 4:
                    parts.append(jnp.zeros((16, quarter), BF16))
                send_ref[z * 2 + core, to * 16 : (to + 1) * 16, :] = jnp.concatenate(parts, axis=1)
    pairs = [(send_ref.at[me ^ away], ref) for away, ref in enumerate(out_refs)]
    for copy in fetched(pairs, sems):
        copy.wait()


def finish_kernel(scale, place_ref, *refs):
    parts, (one_ref, two_ref) = refs[:-2], refs[-2:]
    core = place_ref[2]
    deep, quarter = one_ref.shape[2:]
    sums = []
    for other in range(2):
        total = parts[other][...].astype(F32)
        for ref in parts[other + 2 :: 2]:
            total = total + ref[...].astype(F32)
        sums.append(total * scale)
    ours, theirs = sums
    for out_ref, total in (
        (one_ref, jnp.where(core == 0, ours, theirs)),
        (two_ref, jnp.where(core == 0, theirs, ours)),
    ):
        for tap, row, begin, slot in units(deep):
            out_ref[tap // 3, tap % 3, row : row + 16, :] = total[
                begin : begin + 16, slot * quarter : (slot + 1) * quarter
            ]


def fast_local(inputs, conv1_weight, conv2_weight, cotangent):
    rows, width, channels = inputs.shape
    every = ("z", "y", "x", "core")
    devices = lax.axis_size(every)
    step = width // devices
    cells = rows * width
    lat = lax.axis_size("x") * lax.axis_size("core")
    lon = devices // lat
    band = rows * lat * step
    half, deep = channels // 2, channels // lon
    height = -(-9 * (deep // 16) // 4) * 16
    scale = (rows * lat * width * lon) ** (-0.5)
    flops = 2 * 9 * cells * channels * channels
    vmem, hbm, smem = (pl.BlockSpec(memory_space=space) for space in (pltpu.VMEM, pltpu.HBM, pltpu.SMEM))

    def held(*shape, kind=BF16):
        return pltpu.VMEM(shape, kind)

    def shaped(*shape, kind=BF16):
        return jax.ShapeDtypeStruct(shape, kind)

    def kernel(body, specs, arguments, out_shape, scratch_shapes, work, megabytes):
        return pl.pallas_call(
            body,
            out_shape=out_shape,
            in_specs=specs,
            out_specs=jax.tree.map(lambda _: vmem, out_shape),
            scratch_shapes=scratch_shapes,
            compiler_params=pltpu.CompilerParams(vmem_limit_bytes=24 * 2**20),
            cost_estimate=pl.CostEstimate(flops=work, bytes_accessed=megabytes * 2**20, transcendentals=0),
        )(*arguments)

    def passed(piece, x, y, core):
        pairs = [(i, i ^ (4 * (i % 2 == y) + 2 * (i % 2 == x) + core)) for i in range(8)]
        return lax.ppermute(piece, ("y", "x", "core"), pairs)

    stack = held(cells + 2 * band, 3 * channels)
    weights = held(*conv1_weight.shape)
    dealt = shaped(devices, 2, rows * step, channels)
    own = kernel(
        functools.partial(deal_kernel, step),
        [hbm] * 2,
        [pltpu.with_memory_space_constraint(field, pltpu.HBM) for field in (inputs, cotangent)],
        dealt,
        [held(2, *inputs.shape), pltpu.SemaphoreType.DMA((2,))],
        10**9,
        3,
    )
    own = lax.all_to_all(own, every, 0, 0, tiled=True)
    place = jnp.stack([lax.axis_index(axis) for axis in ("x", "y", "core", "z")]).astype(jnp.int32)
    one, two = (pltpu.with_memory_space_constraint(w, pltpu.HBM) for w in (conv1_weight, conv2_weight))
    taps = pltpu.SemaphoreType.DMA((2, 3))
    hidden, pre_grad, mine, kept, give = kernel(
        functools.partial(inner_kernel, band, step),
        [smem, vmem, hbm, hbm],
        (place, own, one, two),
        (
            held(cells, channels),
            held(cells, channels),
            held(3, half, cells),
            held(half, cells),
            held(4, half, cells),
        ),
        [
            weights,
            weights,
            stack,
            stack,
            held(cells, channels, kind=F32),
            held(cells, channels, kind=F32),
            held(8, half, cells),
            taps,
        ],
        2 * flops,
        10,
    )
    got = passed(give, None, None, 1)
    far, far_pair = passed(mine, 0, 1, 0), passed(got[:3], 0, 1, 0)
    hidden, pre_grad, got = lax.optimization_barrier((hidden, pre_grad, got))
    fields = kernel(
        functools.partial(outer_kernel, band, step),
        [vmem] * 5,
        (own, hidden, pre_grad, conv1_weight, conv2_weight),
        dealt,
        [stack, stack],
        2 * flops,
        9,
    )
    _, far, far_pair = lax.optimization_barrier((fields, far, far_pair))
    fields = lax.all_to_all(fields, every, 0, 0, tiled=True)
    output, input_grad = kernel(
        functools.partial(gather_kernel, step), [vmem], (fields,), (shaped(*inputs.shape),) * 2, [], 10**9, 3
    )
    room = [held(2, half, 2 * cells), held(9, half, 2 * cells)]
    near = kernel(
        functools.partial(near_kernel, band, step),
        [smem] + [vmem] * 3,
        (place, mine, kept, got),
        held(2, half, 9 * half, kind=F32),
        room,
        2 * flops,
        6,
    )
    keep, give = kernel(
        functools.partial(far_kernel, band, step),
        [smem] + [vmem] * 3,
        (place, near, far, far_pair),
        (held(half, 9 * half, kind=F32), held(half, 9 * half)),
        room,
        3 * flops,
        6,
    )
    terms = kernel(
        pack_kernel,
        [smem] + [vmem] * 2,
        (place, keep, passed(give, 1, 0, 0)),
        (held(height, channels),) * 8,
        [held(half, 9 * half), held(8, height, channels), pltpu.SemaphoreType.DMA((8,))],
        2 * flops,
        4,
    )
    parts = list(terms)
    for away in (6, 7, 4, 5, 2, 3, 1):
        parts[away] = lax.ppermute(terms[away], ("z", "core"), [(i, i ^ away) for i in range(8)])
    output, input_grad, parts = lax.optimization_barrier((output, input_grad, parts))
    grad = shaped(3, 3, deep, half // 2, kind=F32)
    conv1_grad, conv2_grad = kernel(
        functools.partial(finish_kernel, scale), [smem] + [vmem] * 8, (place, *parts), (grad, grad), [], 10**6, 2
    )
    return (output, input_grad, conv1_grad, conv2_grad)


def is_fast(mesh):
    return dict(mesh.shape) == {"lon": 8, "lat": 4}


def solution(mesh):
    body, lon, lat = local, "lon", "lat"
    if is_fast(mesh):
        lon, lat = ("z", "y"), ("x", "core")
        mesh = jax.sharding.Mesh(mesh.devices.reshape(4, 2, 2, 2), lon + lat)
        body = fast_local
    field, grad = P(lat, lon, None), P(None, None, lon, lat)
    return jax.shard_map(
        body,
        mesh=mesh,
        in_specs=(field, P(), P(), field),
        out_specs=(field, field, grad, grad),
        check_vma=False,
    )
```

```python
import functools

import jax
import jax.numpy as jnp
from jax import lax
from jax.experimental import pallas as pl
from jax.experimental.pallas import tpu as pltpu
from jax.sharding import PartitionSpec as P

F32, BF16 = jnp.float32, jnp.bfloat16


def passed_along(shard, axis, by):
    length = lax.axis_size(axis)
    return lax.ppermute(shard, axis, [(i, (i + by) % length) for i in range(length)])


def padded(shard, sides, width):
    for axis, dim in sides:
        size, length = (lax.axis_size(axis), shard.shape[dim])
        up = [(i, (i + 1) % size) for i in range(size - 1)]
        down = [(j, i) for i, j in up]
        last = lax.slice_in_dim(shard, length - width, length, axis=dim)
        initial = lax.slice_in_dim(shard, 0, width, axis=dim)
        before = lax.ppermute(last, axis, up)
        after = lax.ppermute(initial, axis, down)
        shard = jnp.concatenate([before, shard, after], axis=dim)
    return shard


def extend(field):
    western = passed_along(field, "lon", 1)
    eastern = passed_along(field, "lon", -1)
    widened = jnp.concatenate([western, field, eastern], axis=1)
    return padded(widened, (("lat", 0),), 1)


def windows(padded_field, count_of_rows, lon_width, channels, direction):
    pieces = []
    for lat_step in (-1, 0, 1):
        for longitude_stride in (-1, 0, 1):
            row_start = 1 + direction * lat_step
            column_begin = lon_width + direction * lon_width * longitude_stride
            pieces.append(
                padded_field[
                    row_start : row_start + count_of_rows, column_begin : column_begin + lon_width
                ]
            )
    stacked = jnp.concatenate(pieces, axis=2)
    return stacked.reshape(count_of_rows * lon_width, 9 * channels)


def full_terms(stacked, grad, scale, channels):
    product = lax.dot_general(
        stacked, grad, (((0,), (0,)), ((), ())), preferred_element_type=jnp.float32
    )
    return (product * scale).reshape(9, channels, channels)


def local(inputs, conv1_weight, conv2_weight, cotangent):
    count_of_rows, lon_width, channels = inputs.shape
    cells = count_of_rows * lon_width
    lon_count = lax.axis_size("lon")
    latitude_count = lax.axis_size("lat")
    scale = (count_of_rows * latitude_count * lon_width * lon_count) ** (-0.5)
    forward_one = conv1_weight.reshape(9 * channels, channels)
    forward_two = conv2_weight.reshape(9 * channels, channels)
    turned_one = jnp.swapaxes(conv1_weight, 2, 3).reshape(9 * channels, channels)
    turned_two = jnp.swapaxes(conv2_weight, 2, 3).reshape(9 * channels, channels)
    source_field, cot_field = (inputs, cotangent)

    def stack_of(field, direction):
        return windows(extend(field), count_of_rows, lon_width, channels, direction)

    def as_field(flat):
        return flat.reshape(count_of_rows, lon_width, channels)

    stack_input = stack_of(source_field, 1)
    first = jnp.dot(stack_input, forward_one, preferred_element_type=jnp.float32)
    cdf = 0.5 * (1.0 + jax.scipy.special.erf(first / jnp.sqrt(2.0)))
    hidden = (first * cdf).astype(jnp.bfloat16)
    stack_hidden = stack_of(as_field(hidden), 1)
    second = jnp.dot(stack_hidden, forward_two, preferred_element_type=jnp.float32)
    flat_input = source_field.reshape(cells, channels)
    output = (flat_input.astype(jnp.float32) + second).astype(jnp.bfloat16)
    flat_cot = cot_field.reshape(cells, channels)
    stacked_cotangent = stack_of(cot_field, -1)
    upstream = jnp.dot(stacked_cotangent, turned_two, preferred_element_type=jnp.float32)
    density = jnp.exp(-0.5 * first * first) / jnp.sqrt(2.0 * jnp.pi)
    pre_grad = (upstream * (cdf + first * density)).astype(jnp.bfloat16)
    stack_pre = stack_of(as_field(pre_grad), -1)
    back = jnp.dot(stack_pre, turned_one, preferred_element_type=jnp.float32)
    input_grad = (flat_cot.astype(jnp.float32) + back).astype(jnp.bfloat16)
    output = output.reshape(count_of_rows, lon_width, channels)
    input_grad = input_grad.reshape(count_of_rows, lon_width, channels)
    in_part = channels // lon_count
    out_part = channels // latitude_count
    terms_one = full_terms(stack_input, pre_grad, scale, channels)
    terms_two = full_terms(stack_hidden, flat_cot, scale, channels)
    partly = (
        lax.psum_scatter(terms_one, "lon", scatter_dimension=1, tiled=True),
        lax.psum_scatter(terms_two, "lon", scatter_dimension=1, tiled=True),
    )
    grad_one, grad_two = (
        lax.psum_scatter(partly[0], "lat", scatter_dimension=2, tiled=True),
        lax.psum_scatter(partly[1], "lat", scatter_dimension=2, tiled=True),
    )
    conv1_grad = grad_one.reshape(3, 3, in_part, out_part)
    conv2_grad = grad_two.reshape(3, 3, in_part, out_part)
    return (output, input_grad, conv1_grad, conv2_grad)


def write_stack(field, stack_ref, band, step):
    cells, channels = field.shape
    wide = field.astype(F32)
    place = lax.broadcasted_iota(jnp.int32, (cells, channels), 0) % band
    above = jnp.where(place >= step, pltpu.roll(wide, step, 0), 0.0).astype(BF16)
    below = jnp.where(place < band - step, pltpu.roll(wide, cells - step, 0), 0.0).astype(BF16)
    for at, part in enumerate((above, field, below)):
        columns = slice(at * channels, (at + 1) * channels)
        stack_ref[band : band + cells, columns] = part
        stack_ref[0:band, columns] = part[cells - band :]
        stack_ref[band + cells :, columns] = part[0:band]


def convolved(stack_ref, weight_ref, band, cells, copies=None):
    total = None
    for b in range(3):
        if copies:
            copies[b].wait()
        channels = weight_ref.shape[2]
        tap = weight_ref[:, b].reshape(3 * channels, channels)
        term = jnp.dot(stack_ref[b * band : b * band + cells, :], tap, preferred_element_type=F32)
        total = term if total is None else total + term
    return total


def convolved_back(stack_ref, weight_ref, band, cells, copies=None):
    total = None
    for b in range(3):
        if copies:
            copies[b].wait()
        tap = jnp.concatenate([weight_ref[2 - a, 2 - b] for a in range(3)], axis=1)
        term = lax.dot_general(
            stack_ref[b * band : b * band + cells, :],
            tap,
            (((1,), (1,)), ((), ())),
            preferred_element_type=F32,
        )
        total = term if total is None else total + term
    return total


def one_hot_rows(cells, step, devices, back):
    to = lax.broadcasted_iota(jnp.int32, (cells, cells), 1 if back else 0)
    source = lax.broadcasted_iota(jnp.int32, (cells, cells), 0 if back else 1)
    rows = cells // (devices * step)
    device, row, column = to // (rows * step), (to // step) % rows, to % step
    return (source == (row * devices + device) * step + column).astype(BF16)


def deal_kernel(step, inputs_ref, cot_ref, out_ref, held_ref, sems):
    devices, _, rows, channels = out_ref.shape
    cells = devices * rows
    copies = fetched(((inputs_ref, held_ref.at[0]), (cot_ref, held_ref.at[1])), sems)
    chosen = one_hot_rows(cells, step, devices, False)
    for at, copy in enumerate(copies):
        copy.wait()
        field = held_ref[at].reshape(cells, channels)
        dealt = jnp.dot(chosen, field, preferred_element_type=F32).astype(BF16)
        out_ref[:, at] = dealt.reshape(devices, rows, channels)


def gather_kernel(step, fields_ref, output_ref, grad_ref):
    devices, _, rows, channels = fields_ref.shape
    cells = devices * rows
    chosen = one_hot_rows(cells, step, devices, True)
    for at, ref in enumerate((output_ref, grad_ref)):
        field = fields_ref[:, at].reshape(cells, channels)
        ref[...] = jnp.dot(chosen, field, preferred_element_type=F32).astype(BF16).reshape(ref.shape)


def fetched(pairs, sems):
    copies = [pltpu.make_async_copy(source, to, sems.at[at]) for at, (source, to) in enumerate(pairs)]
    for copy in copies:
        copy.start()
    return copies


def by_tap(weight_ref, held_ref, sems, order):
    return fetched([(weight_ref.at[:, b], held_ref.at[:, b]) for b in order], sems)


def inner_kernel(band, step, place_ref, own_ref, one_ref, two_ref,
                 hidden_ref, pre_ref, mine_ref, kept_ref, give_ref, cross_ref,
                 one_held, two_held, stack_ref, first_ref, slope_ref, turned_ref, sems):
    x, y, core = place_ref[0], place_ref[1], place_ref[2]
    cells, channels = first_ref.shape
    first_weight = by_tap(one_ref, one_held, sems.at[0], range(3))
    half, rows = channels // 2, 32
    deep = half // 4

    def turn(at, field):
        turned = field.T
        for h in range(2):
            for z in range(4):
                begin = (2 * z + h) * deep if at < 2 else h * half + z * deep
                turned_ref[at * 2 + h, z * deep : (z + 1) * deep, :] = turned[begin : begin + deep]

    source = own_ref[:, 0].reshape(cells, channels)
    write_stack(source, stack_ref, band, step)
    first_ref[...] = convolved(stack_ref, one_held, band, cells, first_weight)
    second_weight = by_tap(two_ref, two_held, sems.at[1], (2, 1, 0))
    turn(0, source)

    def activate(at, carry):
        span = pl.ds(pl.multiple_of(at * rows, rows), rows)
        first = first_ref[span, :]
        cdf = 0.5 * (1.0 + lax.erf(first * (0.5**0.5)))
        density = jnp.exp(-0.5 * first * first) * ((2.0 * jnp.pi) ** -0.5)
        hidden_ref[span, :] = (first * cdf).astype(BF16)
        slope_ref[span, :] = cdf + first * density
        return carry

    lax.fori_loop(0, cells // rows, activate, 0)
    turn(1, hidden_ref[...])
    cot = own_ref[:, 1].reshape(cells, channels)
    write_stack(cot, stack_ref, band, step)
    turn(3, cot)
    pre_ref[...] = (slope_ref[...] * convolved_back(stack_ref, two_held, band, cells, second_weight)).astype(BF16)
    turn(2, pre_ref[...])

    for ref, of, half_of in (
        (mine_ref, core, jnp.where(core == 0, 1 - x, 1 - y)),
        (give_ref, 1 - core, jnp.where(core == 0, y, x)),
        (cross_ref, 1 - core, jnp.where(core == 0, 1 - y, 1 - x)),
    ):
        ref[0] = turned_ref[6 * of]
        ref[1] = turned_ref[6 * of + 1]
        ref[2] = turned_ref[4 - 2 * of + half_of]
    kept_ref[...] = turned_ref[4 - 2 * core + jnp.where(core == 0, x, y)]


def outer_kernel(band, step, own_ref, hidden_ref, pre_ref, one_ref, two_ref, out_ref, stack_ref, back_ref):
    cells, channels = hidden_ref.shape
    shape = (out_ref.shape[0],) + out_ref.shape[2:]
    write_stack(hidden_ref[...], stack_ref, band, step)
    write_stack(pre_ref[...], back_ref, band, step)
    second = convolved(stack_ref, two_ref, band, cells)
    source = own_ref[:, 0].reshape(cells, channels)
    out_ref[:, 0] = (source.astype(F32) + second).astype(BF16).reshape(shape)
    back = convolved_back(back_ref, one_ref, band, cells)
    cot = own_ref[:, 1].reshape(cells, channels)
    out_ref[:, 1] = (cot.astype(F32) + back).astype(BF16).reshape(shape)


def units(deep):
    count = deep // 16
    for unit in range(9 * count):
        yield unit // count, (unit % count) * 16, (unit // 4) * 16, unit % 4


def terms_of(band, step, place_ref, sources, whole_ref, moved_ref, write):
    x, y, core = place_ref[0], place_ref[1], place_ref[2]
    half, cells = sources[0][1].shape
    place = lax.broadcasted_iota(jnp.int32, (half, cells), 1) % band
    inside = {
        1: jnp.where(place < band - step, 1.0, 0.0).astype(BF16),
        -1: jnp.where(place >= step, 1.0, 0.0).astype(BF16),
    }
    for at, (ref, moving_ref) in enumerate(sources):
        columns = slice(at * cells, (at + 1) * cells)
        whole_ref[0, :, columns] = ref[0]
        whole_ref[1, :, columns] = ref[1]
        field = moving_ref[...]
        for a in range(-1, 2):
            for b in range(-1, 2):
                shift = (-(b * band + a * step)) % cells
                part = pltpu.roll(field, shift, 1) if shift else field
                if a:
                    part = part * inside[a]
                tap = (a + 1) * 3 + b + 1
                moved_ref[jnp.where(core == 0, 8 - tap, tap), :, columns] = part
    moved = moved_ref[...].reshape(9 * half, len(sources) * cells)
    stays = jnp.where(core == 0, y, x)
    for at, which in enumerate((1 - stays, stays)):
        whole = whole_ref[which]

        @pl.when(core == 0)
        def _():
            write(at, slice(None), lax.dot_general(
                whole, moved, (((1,), (1,)), ((), ())), preferred_element_type=F32
            ))

        @pl.when(core == 1)
        def _():
            terms = lax.dot_general(moved, whole, (((1,), (1,)), ((), ())), preferred_element_type=F32)
            for tap in range(9):
                rows = slice(tap * half, (tap + 1) * half)
                write(at, rows, terms[rows])


def near_kernel(band, step, place_ref, mine_ref, kept_ref, got_ref, sums_ref, whole_ref, moved_ref):
    def write(at, columns, terms):
        sums_ref[at, :, columns] = terms

    sources = ((mine_ref, kept_ref), (got_ref, got_ref.at[2]))
    terms_of(band, step, place_ref, sources, whole_ref, moved_ref, write)


def far_kernel(band, step, place_ref, sums_ref, far_ref, pair_ref, keep_ref, give_ref, whole_ref, moved_ref):
    def write(at, columns, terms):
        ref = (give_ref, keep_ref)[at]
        ref[:, columns] = (sums_ref[at, :, columns] + terms).astype(ref.dtype)

    sources = ((far_ref, far_ref.at[2]), (pair_ref, pair_ref.at[2]))
    terms_of(band, step, place_ref, sources, whole_ref, moved_ref, write)


def pack_kernel(place_ref, keep_ref, got_ref, *refs):
    out_refs, (sums_ref, send_ref, sems) = refs[:-3], refs[-3:]
    me = place_ref[3] * 2 + place_ref[2]
    half = keep_ref.shape[0]
    sums_ref[...] = (keep_ref[...] + got_ref[...].astype(F32)).astype(BF16)
    deep, quarter = half // 4, half // 2
    height = send_ref.shape[1]
    for z in range(4):
        for core in range(2):
            blocks = [[] for _ in range(height // 16)]
            for tap, row, to, _ in units(deep):
                begin, first = z * deep + row, tap * half + core * quarter
                blocks[to // 16].append(sums_ref[begin : begin + 16, first : first + quarter])
            for to, parts in enumerate(blocks):
                while len(parts) < 4:
                    parts.append(jnp.zeros((16, quarter), BF16))
                send_ref[z * 2 + core, to * 16 : (to + 1) * 16, :] = jnp.concatenate(parts, axis=1)
    pairs = [(send_ref.at[me ^ away], ref) for away, ref in enumerate(out_refs)]
    for copy in fetched(pairs, sems):
        copy.wait()


def finish_kernel(scale, place_ref, *refs):
    parts, (one_ref, two_ref) = refs[:-2], refs[-2:]
    core = place_ref[2]
    deep, quarter = one_ref.shape[2:]
    sums = []
    for other in range(2):
        total = parts[other][...].astype(F32)
        for ref in parts[other + 2 :: 2]:
            total = total + ref[...].astype(F32)
        sums.append(total * scale)
    ours, theirs = sums
    for out_ref, total in (
        (one_ref, jnp.where(core == 0, ours, theirs)),
        (two_ref, jnp.where(core == 0, theirs, ours)),
    ):
        for tap, row, begin, slot in units(deep):
            out_ref[tap // 3, tap % 3, row : row + 16, :] = total[
                begin : begin + 16, slot * quarter : (slot + 1) * quarter
            ]


def fast_local(inputs, conv1_weight, conv2_weight, cotangent):
    rows, width, channels = inputs.shape
    every = ("z", "y", "x", "core")
    devices = lax.axis_size(every)
    step = width // devices
    cells = rows * width
    lat = lax.axis_size("x") * lax.axis_size("core")
    lon = devices // lat
    band = rows * lat * step
    half, deep = channels // 2, channels // lon
    height = -(-9 * (deep // 16) // 4) * 16
    scale = (rows * lat * width * lon) ** (-0.5)
    flops = 2 * 9 * cells * channels * channels
    vmem, hbm, smem = (pl.BlockSpec(memory_space=space) for space in (pltpu.VMEM, pltpu.HBM, pltpu.SMEM))

    def held(*shape, kind=BF16):
        return pltpu.VMEM(shape, kind)

    def shaped(*shape, kind=BF16):
        return jax.ShapeDtypeStruct(shape, kind)

    def kernel(body, specs, arguments, out_shape, scratch_shapes, work, megabytes):
        return pl.pallas_call(
            body,
            out_shape=out_shape,
            in_specs=specs,
            out_specs=jax.tree.map(lambda _: vmem, out_shape),
            scratch_shapes=scratch_shapes,
            compiler_params=pltpu.CompilerParams(vmem_limit_bytes=24 * 2**20),
            cost_estimate=pl.CostEstimate(flops=work, bytes_accessed=megabytes * 2**20, transcendentals=0),
        )(*arguments)

    def passed(piece, x, y, core):
        pairs = [(i, i ^ (4 * (i % 2 == y) + 2 * (i % 2 == x) + core)) for i in range(8)]
        return lax.ppermute(piece, ("y", "x", "core"), pairs)

    stack = held(cells + 2 * band, 3 * channels)
    weights = held(*conv1_weight.shape)
    dealt = shaped(devices, 2, rows * step, channels)
    own = kernel(
        functools.partial(deal_kernel, step),
        [hbm] * 2,
        [pltpu.with_memory_space_constraint(field, pltpu.HBM) for field in (inputs, cotangent)],
        dealt,
        [held(2, *inputs.shape), pltpu.SemaphoreType.DMA((2,))],
        10**9,
        3,
    )
    own = lax.all_to_all(own, every, 0, 0, tiled=True)
    place = jnp.stack([lax.axis_index(axis) for axis in ("x", "y", "core", "z")]).astype(jnp.int32)
    one, two = (pltpu.with_memory_space_constraint(w, pltpu.HBM) for w in (conv1_weight, conv2_weight))
    taps = pltpu.SemaphoreType.DMA((2, 3))
    hidden, pre_grad, mine, kept, give, cross = kernel(
        functools.partial(inner_kernel, band, step),
        [smem, vmem, hbm, hbm],
        (place, own, one, two),
        (
            held(cells, channels),
            held(cells, channels),
            held(3, half, cells),
            held(half, cells),
            held(3, half, cells),
            held(3, half, cells),
        ),
        [
            weights,
            weights,
            stack,
            held(cells, channels, kind=F32),
            held(cells, channels, kind=F32),
            held(8, half, cells),
            taps,
        ],
        2 * flops,
        10,
    )
    got = passed(give, None, None, 1)
    far, far_pair = passed(mine, 0, 1, 0), passed(cross, 1, 0, 1)
    hidden, pre_grad, got = lax.optimization_barrier((hidden, pre_grad, got))
    fields = kernel(
        functools.partial(outer_kernel, band, step),
        [vmem] * 5,
        (own, hidden, pre_grad, conv1_weight, conv2_weight),
        dealt,
        [stack, stack],
        2 * flops,
        9,
    )
    _, far, far_pair = lax.optimization_barrier((fields, far, far_pair))
    fields = lax.all_to_all(fields, every, 0, 0, tiled=True)
    output, input_grad = kernel(
        functools.partial(gather_kernel, step), [vmem], (fields,), (shaped(*inputs.shape),) * 2, [], 10**9, 3
    )
    room = [held(2, half, 2 * cells), held(9, half, 2 * cells)]
    near = kernel(
        functools.partial(near_kernel, band, step),
        [smem] + [vmem] * 3,
        (place, mine, kept, got),
        held(2, half, 9 * half, kind=F32),
        room,
        2 * flops,
        6,
    )
    keep, give = kernel(
        functools.partial(far_kernel, band, step),
        [smem] + [vmem] * 3,
        (place, near, far, far_pair),
        (held(half, 9 * half, kind=F32), held(half, 9 * half)),
        room,
        3 * flops,
        6,
    )
    terms = kernel(
        pack_kernel,
        [smem] + [vmem] * 2,
        (place, keep, passed(give, 1, 0, 0)),
        (held(height, channels),) * 8,
        [held(half, 9 * half), held(8, height, channels), pltpu.SemaphoreType.DMA((8,))],
        2 * flops,
        4,
    )
    parts = list(terms)
    for away in (6, 7, 4, 5, 2, 3, 1):
        parts[away] = lax.ppermute(terms[away], ("z", "core"), [(i, i ^ away) for i in range(8)])
    output, input_grad, parts = lax.optimization_barrier((output, input_grad, parts))
    grad = shaped(3, 3, deep, half // 2, kind=F32)
    conv1_grad, conv2_grad = kernel(
        functools.partial(finish_kernel, scale), [smem] + [vmem] * 8, (place, *parts), (grad, grad), [], 10**6, 2
    )
    return (output, input_grad, conv1_grad, conv2_grad)


def is_fast(mesh):
    return dict(mesh.shape) == {"lon": 8, "lat": 4}


def solution(mesh):
    body, lon, lat = local, "lon", "lat"
    if is_fast(mesh):
        lon, lat = ("z", "y"), ("x", "core")
        mesh = jax.sharding.Mesh(mesh.devices.reshape(4, 2, 2, 2), lon + lat)
        body = fast_local
    field, grad = P(lat, lon, None), P(None, None, lon, lat)
    return jax.shard_map(
        body,
        mesh=mesh,
        in_specs=(field, P(), P(), field),
        out_specs=(field, field, grad, grad),
        check_vma=False,
    )
```

```python
import functools

import jax
import jax.numpy as jnp
from jax import lax
from jax.experimental import pallas as pl
from jax.experimental.pallas import tpu as pltpu
from jax.sharding import PartitionSpec as P

F32, BF16 = jnp.float32, jnp.bfloat16


def passed_along(shard, axis, by):
    length = lax.axis_size(axis)
    return lax.ppermute(shard, axis, [(i, (i + by) % length) for i in range(length)])


def padded(shard, sides, width):
    for axis, dim in sides:
        size, length = (lax.axis_size(axis), shard.shape[dim])
        up = [(i, (i + 1) % size) for i in range(size - 1)]
        down = [(j, i) for i, j in up]
        last = lax.slice_in_dim(shard, length - width, length, axis=dim)
        initial = lax.slice_in_dim(shard, 0, width, axis=dim)
        before = lax.ppermute(last, axis, up)
        after = lax.ppermute(initial, axis, down)
        shard = jnp.concatenate([before, shard, after], axis=dim)
    return shard


def extend(field):
    western = passed_along(field, "lon", 1)
    eastern = passed_along(field, "lon", -1)
    widened = jnp.concatenate([western, field, eastern], axis=1)
    return padded(widened, (("lat", 0),), 1)


def windows(padded_field, count_of_rows, lon_width, channels, direction):
    pieces = []
    for lat_step in (-1, 0, 1):
        for longitude_stride in (-1, 0, 1):
            row_start = 1 + direction * lat_step
            column_begin = lon_width + direction * lon_width * longitude_stride
            pieces.append(
                padded_field[
                    row_start : row_start + count_of_rows, column_begin : column_begin + lon_width
                ]
            )
    stacked = jnp.concatenate(pieces, axis=2)
    return stacked.reshape(count_of_rows * lon_width, 9 * channels)


def full_terms(stacked, grad, scale, channels):
    product = lax.dot_general(
        stacked, grad, (((0,), (0,)), ((), ())), preferred_element_type=jnp.float32
    )
    return (product * scale).reshape(9, channels, channels)


def local(inputs, conv1_weight, conv2_weight, cotangent):
    count_of_rows, lon_width, channels = inputs.shape
    cells = count_of_rows * lon_width
    lon_count = lax.axis_size("lon")
    latitude_count = lax.axis_size("lat")
    scale = (count_of_rows * latitude_count * lon_width * lon_count) ** (-0.5)
    forward_one = conv1_weight.reshape(9 * channels, channels)
    forward_two = conv2_weight.reshape(9 * channels, channels)
    turned_one = jnp.swapaxes(conv1_weight, 2, 3).reshape(9 * channels, channels)
    turned_two = jnp.swapaxes(conv2_weight, 2, 3).reshape(9 * channels, channels)
    source_field, cot_field = (inputs, cotangent)

    def stack_of(field, direction):
        return windows(extend(field), count_of_rows, lon_width, channels, direction)

    def as_field(flat):
        return flat.reshape(count_of_rows, lon_width, channels)

    stack_input = stack_of(source_field, 1)
    first = jnp.dot(stack_input, forward_one, preferred_element_type=jnp.float32)
    cdf = 0.5 * (1.0 + jax.scipy.special.erf(first / jnp.sqrt(2.0)))
    hidden = (first * cdf).astype(jnp.bfloat16)
    stack_hidden = stack_of(as_field(hidden), 1)
    second = jnp.dot(stack_hidden, forward_two, preferred_element_type=jnp.float32)
    flat_input = source_field.reshape(cells, channels)
    output = (flat_input.astype(jnp.float32) + second).astype(jnp.bfloat16)
    flat_cot = cot_field.reshape(cells, channels)
    stacked_cotangent = stack_of(cot_field, -1)
    upstream = jnp.dot(stacked_cotangent, turned_two, preferred_element_type=jnp.float32)
    density = jnp.exp(-0.5 * first * first) / jnp.sqrt(2.0 * jnp.pi)
    pre_grad = (upstream * (cdf + first * density)).astype(jnp.bfloat16)
    stack_pre = stack_of(as_field(pre_grad), -1)
    back = jnp.dot(stack_pre, turned_one, preferred_element_type=jnp.float32)
    input_grad = (flat_cot.astype(jnp.float32) + back).astype(jnp.bfloat16)
    output = output.reshape(count_of_rows, lon_width, channels)
    input_grad = input_grad.reshape(count_of_rows, lon_width, channels)
    in_part = channels // lon_count
    out_part = channels // latitude_count
    terms_one = full_terms(stack_input, pre_grad, scale, channels)
    terms_two = full_terms(stack_hidden, flat_cot, scale, channels)
    partly = (
        lax.psum_scatter(terms_one, "lon", scatter_dimension=1, tiled=True),
        lax.psum_scatter(terms_two, "lon", scatter_dimension=1, tiled=True),
    )
    grad_one, grad_two = (
        lax.psum_scatter(partly[0], "lat", scatter_dimension=2, tiled=True),
        lax.psum_scatter(partly[1], "lat", scatter_dimension=2, tiled=True),
    )
    conv1_grad = grad_one.reshape(3, 3, in_part, out_part)
    conv2_grad = grad_two.reshape(3, 3, in_part, out_part)
    return (output, input_grad, conv1_grad, conv2_grad)


def write_stack(field, stack_ref, band, step):
    cells, channels = field.shape
    wide = field.astype(F32)
    place = lax.broadcasted_iota(jnp.int32, (cells, channels), 0) % band
    above = jnp.where(place >= step, pltpu.roll(wide, step, 0), 0.0).astype(BF16)
    below = jnp.where(place < band - step, pltpu.roll(wide, cells - step, 0), 0.0).astype(BF16)
    for at, part in enumerate((above, field, below)):
        columns = slice(at * channels, (at + 1) * channels)
        stack_ref[band : band + cells, columns] = part
        stack_ref[0:band, columns] = part[cells - band :]
        stack_ref[band + cells :, columns] = part[0:band]


def convolved(stack_ref, weight_ref, band, cells, copies=None):
    total = None
    for b in range(3):
        if copies:
            copies[b].wait()
        channels = weight_ref.shape[2]
        tap = weight_ref[:, b].reshape(3 * channels, channels)
        term = jnp.dot(stack_ref[b * band : b * band + cells, :], tap, preferred_element_type=F32)
        total = term if total is None else total + term
    return total


def convolved_back(stack_ref, weight_ref, band, cells, copies=None):
    total = None
    for b in range(3):
        if copies:
            copies[b].wait()
        tap = jnp.concatenate([weight_ref[2 - a, 2 - b] for a in range(3)], axis=1)
        term = lax.dot_general(
            stack_ref[b * band : b * band + cells, :],
            tap,
            (((1,), (1,)), ((), ())),
            preferred_element_type=F32,
        )
        total = term if total is None else total + term
    return total


def one_hot_rows(cells, step, devices, back):
    to = lax.broadcasted_iota(jnp.int32, (cells, cells), 1 if back else 0)
    source = lax.broadcasted_iota(jnp.int32, (cells, cells), 0 if back else 1)
    rows = cells // (devices * step)
    device, row, column = to // (rows * step), (to // step) % rows, to % step
    return (source == (row * devices + device) * step + column).astype(BF16)


def deal_kernel(step, inputs_ref, cot_ref, out_ref, held_ref, sems):
    devices, _, rows, channels = out_ref.shape
    cells = devices * rows
    copies = fetched(((inputs_ref, held_ref.at[0]), (cot_ref, held_ref.at[1])), sems)
    chosen = one_hot_rows(cells, step, devices, False)
    for at, copy in enumerate(copies):
        copy.wait()
        field = held_ref[at].reshape(cells, channels)
        dealt = jnp.dot(chosen, field, preferred_element_type=F32).astype(BF16)
        out_ref[:, at] = dealt.reshape(devices, rows, channels)


def gather_kernel(step, fields_ref, output_ref, grad_ref):
    devices, _, rows, channels = fields_ref.shape
    cells = devices * rows
    chosen = one_hot_rows(cells, step, devices, True)
    for at, ref in enumerate((output_ref, grad_ref)):
        field = fields_ref[:, at].reshape(cells, channels)
        ref[...] = jnp.dot(chosen, field, preferred_element_type=F32).astype(BF16).reshape(ref.shape)


def fetched(pairs, sems):
    copies = [pltpu.make_async_copy(source, to, sems.at[at]) for at, (source, to) in enumerate(pairs)]
    for copy in copies:
        copy.start()
    return copies


def by_tap(weight_ref, held_ref, sems, order):
    return fetched([(weight_ref.at[:, b], held_ref.at[:, b]) for b in order], sems)


def inner_kernel(band, step, place_ref, own_ref, one_ref, two_ref,
                 hidden_ref, pre_ref, mine_ref, kept_ref, give_ref, cross_ref,
                 one_held, two_held, stack_ref, first_ref, slope_ref, turned_ref, sems):
    x, y, core = place_ref[0], place_ref[1], place_ref[2]
    cells, channels = first_ref.shape
    first_weight = by_tap(one_ref, one_held, sems.at[0], range(3))
    half, rows = channels // 2, 32
    deep = half // 4

    def turn(at, field):
        turned = field.T
        for h in range(2):
            for z in range(4):
                begin = (2 * z + h) * deep if at < 2 else h * half + z * deep
                turned_ref[at * 2 + h, z * deep : (z + 1) * deep, :] = turned[begin : begin + deep]

    source = own_ref[:, 0].reshape(cells, channels)
    write_stack(source, stack_ref, band, step)
    first_ref[...] = convolved(stack_ref, one_held, band, cells, first_weight)
    second_weight = by_tap(two_ref, two_held, sems.at[1], (2, 1, 0))
    turn(0, source)

    def activate(at, carry):
        span = pl.ds(pl.multiple_of(at * rows, rows), rows)
        first = first_ref[span, :]
        cdf = 0.5 * (1.0 + lax.erf(first * (0.5**0.5)))
        density = jnp.exp(-0.5 * first * first) * ((2.0 * jnp.pi) ** -0.5)
        hidden_ref[span, :] = (first * cdf).astype(BF16)
        slope_ref[span, :] = cdf + first * density
        return carry

    lax.fori_loop(0, cells // rows, activate, 0)
    turn(1, hidden_ref[...])
    cot = own_ref[:, 1].reshape(cells, channels)
    write_stack(cot, stack_ref, band, step)
    turn(3, cot)
    pre_ref[...] = (slope_ref[...] * convolved_back(stack_ref, two_held, band, cells, second_weight)).astype(BF16)
    turn(2, pre_ref[...])

    for ref, of, half_of in (
        (mine_ref, core, jnp.where(core == 0, 1 - x, 1 - y)),
        (give_ref, 1 - core, jnp.where(core == 0, y, x)),
        (cross_ref, 1 - core, jnp.where(core == 0, 1 - y, 1 - x)),
    ):
        ref[0] = turned_ref[6 * of]
        ref[1] = turned_ref[6 * of + 1]
        ref[2] = turned_ref[4 - 2 * of + half_of]
    kept_ref[...] = turned_ref[4 - 2 * core + jnp.where(core == 0, x, y)]


def outer_kernel(band, step, own_ref, hidden_ref, pre_ref, one_ref, two_ref, out_ref, stack_ref, back_ref):
    cells, channels = hidden_ref.shape
    shape = (out_ref.shape[0],) + out_ref.shape[2:]
    write_stack(hidden_ref[...], stack_ref, band, step)
    write_stack(pre_ref[...], back_ref, band, step)
    second = convolved(stack_ref, two_ref, band, cells)
    source = own_ref[:, 0].reshape(cells, channels)
    out_ref[:, 0] = (source.astype(F32) + second).astype(BF16).reshape(shape)
    back = convolved_back(back_ref, one_ref, band, cells)
    cot = own_ref[:, 1].reshape(cells, channels)
    out_ref[:, 1] = (cot.astype(F32) + back).astype(BF16).reshape(shape)


def units(deep):
    count = deep // 16
    for unit in range(9 * count):
        yield unit // count, (unit % count) * 16, (unit // 4) * 16, unit % 4


def terms_of(band, step, place_ref, sources, whole_ref, moved_ref, write):
    x, y, core = place_ref[0], place_ref[1], place_ref[2]
    half, cells = sources[0][1].shape
    place = lax.broadcasted_iota(jnp.int32, (half, cells), 1) % band
    inside = {
        1: jnp.where(place < band - step, 1.0, 0.0).astype(BF16),
        -1: jnp.where(place >= step, 1.0, 0.0).astype(BF16),
    }
    for at, (ref, moving_ref) in enumerate(sources):
        columns = slice(at * cells, (at + 1) * cells)
        whole_ref[0, :, columns] = ref[0]
        whole_ref[1, :, columns] = ref[1]
        field = moving_ref[...]
        for a in range(-1, 2):
            for b in range(-1, 2):
                shift = (-(b * band + a * step)) % cells
                part = pltpu.roll(field, shift, 1) if shift else field
                if a:
                    part = part * inside[a]
                tap = (a + 1) * 3 + b + 1
                moved_ref[jnp.where(core == 0, 8 - tap, tap), :, columns] = part
    moved = moved_ref[...].reshape(9 * half, len(sources) * cells)
    stays = jnp.where(core == 0, y, x)
    for at, which in enumerate((1 - stays, stays)):
        whole = whole_ref[which]

        @pl.when(core == 0)
        def _():
            write(at, slice(None), lax.dot_general(
                whole, moved, (((1,), (1,)), ((), ())), preferred_element_type=F32
            ))

        @pl.when(core == 1)
        def _():
            terms = lax.dot_general(moved, whole, (((1,), (1,)), ((), ())), preferred_element_type=F32)
            for tap in range(9):
                rows = slice(tap * half, (tap + 1) * half)
                write(at, rows, terms[rows])


def near_kernel(band, step, place_ref, mine_ref, kept_ref, got_ref, sums_ref, whole_ref, moved_ref):
    def write(at, columns, terms):
        sums_ref[at, :, columns] = terms

    sources = ((mine_ref, kept_ref), (got_ref, got_ref.at[2]))
    terms_of(band, step, place_ref, sources, whole_ref, moved_ref, write)


def far_kernel(band, step, place_ref, sums_ref, far_ref, pair_ref, keep_ref, give_ref, whole_ref, moved_ref):
    def write(at, columns, terms):
        ref = (give_ref, keep_ref)[at]
        ref[:, columns] = (sums_ref[at, :, columns] + terms).astype(ref.dtype)

    sources = ((far_ref, far_ref.at[2]), (pair_ref, pair_ref.at[2]))
    terms_of(band, step, place_ref, sources, whole_ref, moved_ref, write)


def pack_kernel(place_ref, keep_ref, got_ref, *refs):
    out_refs, (sums_ref, send_ref, sems) = refs[:-3], refs[-3:]
    me = place_ref[3] * 2 + place_ref[2]
    half = keep_ref.shape[0]
    sums_ref[...] = (keep_ref[...] + got_ref[...].astype(F32)).astype(BF16)
    deep, quarter = half // 4, half // 2
    height = send_ref.shape[1]
    for z in range(4):
        for core in range(2):
            blocks = [[] for _ in range(height // 16)]
            for tap, row, to, _ in units(deep):
                begin, first = z * deep + row, tap * half + core * quarter
                blocks[to // 16].append(sums_ref[begin : begin + 16, first : first + quarter])
            for to, parts in enumerate(blocks):
                while len(parts) < 4:
                    parts.append(jnp.zeros((16, quarter), BF16))
                send_ref[z * 2 + core, to * 16 : (to + 1) * 16, :] = jnp.concatenate(parts, axis=1)
    pairs = [(send_ref.at[me ^ away], ref) for away, ref in enumerate(out_refs)]
    for copy in fetched(pairs, sems):
        copy.wait()


def finish_kernel(scale, place_ref, *refs):
    parts, (one_ref, two_ref) = refs[:-2], refs[-2:]
    core = place_ref[2]
    deep, quarter = one_ref.shape[2:]
    sums = []
    for other in range(2):
        total = parts[other][...].astype(F32)
        for ref in parts[other + 2 :: 2]:
            total = total + ref[...].astype(F32)
        sums.append(total * scale)
    ours, theirs = sums
    for out_ref, total in (
        (one_ref, jnp.where(core == 0, ours, theirs)),
        (two_ref, jnp.where(core == 0, theirs, ours)),
    ):
        for tap, row, begin, slot in units(deep):
            out_ref[tap // 3, tap % 3, row : row + 16, :] = total[
                begin : begin + 16, slot * quarter : (slot + 1) * quarter
            ]


def fast_local(inputs, conv1_weight, conv2_weight, cotangent):
    rows, width, channels = inputs.shape
    every = ("z", "y", "x", "core")
    devices = lax.axis_size(every)
    step = width // devices
    cells = rows * width
    lat = lax.axis_size("x") * lax.axis_size("core")
    lon = devices // lat
    band = rows * lat * step
    half, deep = channels // 2, channels // lon
    height = -(-9 * (deep // 16) // 4) * 16
    scale = (rows * lat * width * lon) ** (-0.5)
    flops = 2 * 9 * cells * channels * channels
    vmem, hbm, smem = (pl.BlockSpec(memory_space=space) for space in (pltpu.VMEM, pltpu.HBM, pltpu.SMEM))

    def held(*shape, kind=BF16):
        return pltpu.VMEM(shape, kind)

    def shaped(*shape, kind=BF16):
        return jax.ShapeDtypeStruct(shape, kind)

    def kernel(body, specs, arguments, out_shape, scratch_shapes, work, megabytes):
        return pl.pallas_call(
            body,
            out_shape=out_shape,
            in_specs=specs,
            out_specs=jax.tree.map(lambda _: vmem, out_shape),
            scratch_shapes=scratch_shapes,
            compiler_params=pltpu.CompilerParams(vmem_limit_bytes=24 * 2**20),
            cost_estimate=pl.CostEstimate(flops=work, bytes_accessed=megabytes * 2**20, transcendentals=0),
        )(*arguments)

    def passed(piece, x, y, core):
        pairs = [(i, i ^ (4 * (i % 2 == y) + 2 * (i % 2 == x) + core)) for i in range(8)]
        return lax.ppermute(piece, ("y", "x", "core"), pairs)

    stack = held(cells + 2 * band, 3 * channels)
    weights = held(*conv1_weight.shape)
    dealt = shaped(devices, 2, rows * step, channels)
    own = kernel(
        functools.partial(deal_kernel, step),
        [hbm] * 2,
        [pltpu.with_memory_space_constraint(field, pltpu.HBM) for field in (inputs, cotangent)],
        dealt,
        [held(2, *inputs.shape), pltpu.SemaphoreType.DMA((2,))],
        10**9,
        3,
    )
    own = lax.all_to_all(own, every, 0, 0, tiled=True)
    place = jnp.stack([lax.axis_index(axis) for axis in ("x", "y", "core", "z")]).astype(jnp.int32)
    one, two = (pltpu.with_memory_space_constraint(w, pltpu.HBM) for w in (conv1_weight, conv2_weight))
    taps = pltpu.SemaphoreType.DMA((2, 3))
    hidden, pre_grad, mine, kept, give, cross = kernel(
        functools.partial(inner_kernel, band, step),
        [smem, vmem, hbm, hbm],
        (place, own, one, two),
        (
            held(cells, channels),
            held(cells, channels),
            held(3, half, cells),
            held(half, cells),
            held(3, half, cells),
            held(3, half, cells),
        ),
        [
            weights,
            weights,
            stack,
            held(cells, channels, kind=F32),
            held(cells, channels, kind=F32),
            held(8, half, cells),
            taps,
        ],
        2 * flops,
        10,
    )
    got = passed(give, None, None, 1)
    far, far_pair = passed(mine, 0, 1, 0), passed(cross, 1, 0, 1)
    room = [held(2, half, 2 * cells), held(9, half, 2 * cells)]
    near = kernel(
        functools.partial(near_kernel, band, step),
        [smem] + [vmem] * 3,
        (place, mine, kept, got),
        held(2, half, 9 * half, kind=F32),
        room,
        2 * flops,
        6,
    )
    hidden, pre_grad, near = lax.optimization_barrier((hidden, pre_grad, near))
    fields = kernel(
        functools.partial(outer_kernel, band, step),
        [vmem] * 5,
        (own, hidden, pre_grad, conv1_weight, conv2_weight),
        dealt,
        [stack, stack],
        2 * flops,
        9,
    )
    _, far, far_pair = lax.optimization_barrier((fields, far, far_pair))
    fields = lax.all_to_all(fields, every, 0, 0, tiled=True)
    output, input_grad = kernel(
        functools.partial(gather_kernel, step), [vmem], (fields,), (shaped(*inputs.shape),) * 2, [], 10**9, 3
    )
    keep, give = kernel(
        functools.partial(far_kernel, band, step),
        [smem] + [vmem] * 3,
        (place, near, far, far_pair),
        (held(half, 9 * half, kind=F32), held(half, 9 * half)),
        room,
        3 * flops,
        6,
    )
    terms = kernel(
        pack_kernel,
        [smem] + [vmem] * 2,
        (place, keep, passed(give, 1, 0, 0)),
        (held(height, channels),) * 8,
        [held(half, 9 * half), held(8, height, channels), pltpu.SemaphoreType.DMA((8,))],
        2 * flops,
        4,
    )
    parts = list(terms)
    for away in (6, 7, 4, 5, 2, 3, 1):
        parts[away] = lax.ppermute(terms[away], ("z", "core"), [(i, i ^ away) for i in range(8)])
    output, input_grad, parts = lax.optimization_barrier((output, input_grad, parts))
    grad = shaped(3, 3, deep, half // 2, kind=F32)
    conv1_grad, conv2_grad = kernel(
        functools.partial(finish_kernel, scale), [smem] + [vmem] * 8, (place, *parts), (grad, grad), [], 10**6, 2
    )
    return (output, input_grad, conv1_grad, conv2_grad)


def is_fast(mesh):
    return dict(mesh.shape) == {"lon": 8, "lat": 4}


def solution(mesh):
    body, lon, lat = local, "lon", "lat"
    if is_fast(mesh):
        lon, lat = ("z", "y"), ("x", "core")
        mesh = jax.sharding.Mesh(mesh.devices.reshape(4, 2, 2, 2), lon + lat)
        body = fast_local
    field, grad = P(lat, lon, None), P(None, None, lon, lat)
    return jax.shard_map(
        body,
        mesh=mesh,
        in_specs=(field, P(), P(), field),
        out_specs=(field, field, grad, grad),
        check_vma=False,
    )
```

```python
import functools

import jax
import jax.numpy as jnp
from jax import lax
from jax.experimental import pallas as pl
from jax.experimental.pallas import tpu as pltpu
from jax.sharding import PartitionSpec as P

F32, BF16 = jnp.float32, jnp.bfloat16


def passed_along(shard, axis, by):
    length = lax.axis_size(axis)
    return lax.ppermute(shard, axis, [(i, (i + by) % length) for i in range(length)])


def padded(shard, sides, width):
    for axis, dim in sides:
        size, length = (lax.axis_size(axis), shard.shape[dim])
        up = [(i, (i + 1) % size) for i in range(size - 1)]
        down = [(j, i) for i, j in up]
        last = lax.slice_in_dim(shard, length - width, length, axis=dim)
        initial = lax.slice_in_dim(shard, 0, width, axis=dim)
        before = lax.ppermute(last, axis, up)
        after = lax.ppermute(initial, axis, down)
        shard = jnp.concatenate([before, shard, after], axis=dim)
    return shard


def extend(field):
    western = passed_along(field, "lon", 1)
    eastern = passed_along(field, "lon", -1)
    widened = jnp.concatenate([western, field, eastern], axis=1)
    return padded(widened, (("lat", 0),), 1)


def windows(padded_field, count_of_rows, lon_width, channels, direction):
    pieces = []
    for lat_step in (-1, 0, 1):
        for longitude_stride in (-1, 0, 1):
            row_start = 1 + direction * lat_step
            column_begin = lon_width + direction * lon_width * longitude_stride
            pieces.append(
                padded_field[
                    row_start : row_start + count_of_rows, column_begin : column_begin + lon_width
                ]
            )
    stacked = jnp.concatenate(pieces, axis=2)
    return stacked.reshape(count_of_rows * lon_width, 9 * channels)


def full_terms(stacked, grad, scale, channels):
    product = lax.dot_general(
        stacked, grad, (((0,), (0,)), ((), ())), preferred_element_type=jnp.float32
    )
    return (product * scale).reshape(9, channels, channels)


def local(inputs, conv1_weight, conv2_weight, cotangent):
    count_of_rows, lon_width, channels = inputs.shape
    cells = count_of_rows * lon_width
    lon_count = lax.axis_size("lon")
    latitude_count = lax.axis_size("lat")
    scale = (count_of_rows * latitude_count * lon_width * lon_count) ** (-0.5)
    forward_one = conv1_weight.reshape(9 * channels, channels)
    forward_two = conv2_weight.reshape(9 * channels, channels)
    turned_one = jnp.swapaxes(conv1_weight, 2, 3).reshape(9 * channels, channels)
    turned_two = jnp.swapaxes(conv2_weight, 2, 3).reshape(9 * channels, channels)
    source_field, cot_field = (inputs, cotangent)

    def stack_of(field, direction):
        return windows(extend(field), count_of_rows, lon_width, channels, direction)

    def as_field(flat):
        return flat.reshape(count_of_rows, lon_width, channels)

    stack_input = stack_of(source_field, 1)
    first = jnp.dot(stack_input, forward_one, preferred_element_type=jnp.float32)
    cdf = 0.5 * (1.0 + jax.scipy.special.erf(first / jnp.sqrt(2.0)))
    hidden = (first * cdf).astype(jnp.bfloat16)
    stack_hidden = stack_of(as_field(hidden), 1)
    second = jnp.dot(stack_hidden, forward_two, preferred_element_type=jnp.float32)
    flat_input = source_field.reshape(cells, channels)
    output = (flat_input.astype(jnp.float32) + second).astype(jnp.bfloat16)
    flat_cot = cot_field.reshape(cells, channels)
    stacked_cotangent = stack_of(cot_field, -1)
    upstream = jnp.dot(stacked_cotangent, turned_two, preferred_element_type=jnp.float32)
    density = jnp.exp(-0.5 * first * first) / jnp.sqrt(2.0 * jnp.pi)
    pre_grad = (upstream * (cdf + first * density)).astype(jnp.bfloat16)
    stack_pre = stack_of(as_field(pre_grad), -1)
    back = jnp.dot(stack_pre, turned_one, preferred_element_type=jnp.float32)
    input_grad = (flat_cot.astype(jnp.float32) + back).astype(jnp.bfloat16)
    output = output.reshape(count_of_rows, lon_width, channels)
    input_grad = input_grad.reshape(count_of_rows, lon_width, channels)
    in_part = channels // lon_count
    out_part = channels // latitude_count
    terms_one = full_terms(stack_input, pre_grad, scale, channels)
    terms_two = full_terms(stack_hidden, flat_cot, scale, channels)
    partly = (
        lax.psum_scatter(terms_one, "lon", scatter_dimension=1, tiled=True),
        lax.psum_scatter(terms_two, "lon", scatter_dimension=1, tiled=True),
    )
    grad_one, grad_two = (
        lax.psum_scatter(partly[0], "lat", scatter_dimension=2, tiled=True),
        lax.psum_scatter(partly[1], "lat", scatter_dimension=2, tiled=True),
    )
    conv1_grad = grad_one.reshape(3, 3, in_part, out_part)
    conv2_grad = grad_two.reshape(3, 3, in_part, out_part)
    return (output, input_grad, conv1_grad, conv2_grad)


def write_stack(field, stack_ref, band, step):
    cells, channels = field.shape
    wide = field.astype(F32)
    place = lax.broadcasted_iota(jnp.int32, (cells, channels), 0) % band
    above = jnp.where(place >= step, pltpu.roll(wide, step, 0), 0.0).astype(BF16)
    below = jnp.where(place < band - step, pltpu.roll(wide, cells - step, 0), 0.0).astype(BF16)
    for at, part in enumerate((above, field, below)):
        columns = slice(at * channels, (at + 1) * channels)
        stack_ref[band : band + cells, columns] = part
        stack_ref[0:band, columns] = part[cells - band :]
        stack_ref[band + cells :, columns] = part[0:band]


def convolved(stack_ref, weight_ref, band, cells, copies=None):
    total = None
    for b in range(3):
        if copies:
            copies[b].wait()
        channels = weight_ref.shape[2]
        tap = weight_ref[:, b].reshape(3 * channels, channels)
        term = jnp.dot(stack_ref[b * band : b * band + cells, :], tap, preferred_element_type=F32)
        total = term if total is None else total + term
    return total


def convolved_back(stack_ref, weight_ref, band, cells, copies=None):
    total = None
    for b in range(3):
        if copies:
            copies[b].wait()
        tap = jnp.concatenate([weight_ref[2 - a, 2 - b] for a in range(3)], axis=1)
        term = lax.dot_general(
            stack_ref[b * band : b * band + cells, :],
            tap,
            (((1,), (1,)), ((), ())),
            preferred_element_type=F32,
        )
        total = term if total is None else total + term
    return total


def one_hot_rows(cells, step, devices, back):
    to = lax.broadcasted_iota(jnp.int32, (cells, cells), 1 if back else 0)
    source = lax.broadcasted_iota(jnp.int32, (cells, cells), 0 if back else 1)
    rows = cells // (devices * step)
    device, row, column = to // (rows * step), (to // step) % rows, to % step
    return (source == (row * devices + device) * step + column).astype(BF16)


def deal_kernel(step, inputs_ref, cot_ref, out_ref, held_ref, sems):
    devices, _, rows, channels = out_ref.shape
    cells = devices * rows
    copies = fetched(((inputs_ref, held_ref.at[0]), (cot_ref, held_ref.at[1])), sems)
    chosen = one_hot_rows(cells, step, devices, False)
    for at, copy in enumerate(copies):
        copy.wait()
        field = held_ref[at].reshape(cells, channels)
        dealt = jnp.dot(chosen, field, preferred_element_type=F32).astype(BF16)
        out_ref[:, at] = dealt.reshape(devices, rows, channels)


def gather_kernel(step, fields_ref, output_ref, grad_ref):
    devices, _, rows, channels = fields_ref.shape
    cells = devices * rows
    chosen = one_hot_rows(cells, step, devices, True)
    for at, ref in enumerate((output_ref, grad_ref)):
        field = fields_ref[:, at].reshape(cells, channels)
        ref[...] = jnp.dot(chosen, field, preferred_element_type=F32).astype(BF16).reshape(ref.shape)


def fetched(pairs, sems):
    copies = [pltpu.make_async_copy(source, to, sems.at[at]) for at, (source, to) in enumerate(pairs)]
    for copy in copies:
        copy.start()
    return copies


def by_tap(weight_ref, held_ref, sems, order):
    return fetched([(weight_ref.at[:, b], held_ref.at[:, b]) for b in order], sems)


def inner_kernel(band, step, place_ref, own_ref, one_ref, two_ref,
                 hidden_ref, pre_ref, mine_ref, kept_ref, give_ref, cross_ref,
                 one_held, two_held, stack_ref, first_ref, slope_ref, turned_ref, sems):
    x, y, core = place_ref[0], place_ref[1], place_ref[2]
    cells, channels = first_ref.shape
    first_weight = by_tap(one_ref, one_held, sems.at[0], range(3))
    half, rows = channels // 2, 32
    deep = half // 4

    def turn(at, field):
        turned = field.T
        for h in range(2):
            for z in range(4):
                begin = (2 * z + h) * deep if at < 2 else h * half + z * deep
                turned_ref[at * 2 + h, z * deep : (z + 1) * deep, :] = turned[begin : begin + deep]

    source = own_ref[:, 0].reshape(cells, channels)
    write_stack(source, stack_ref, band, step)
    first_ref[...] = convolved(stack_ref, one_held, band, cells, first_weight)
    second_weight = by_tap(two_ref, two_held, sems.at[1], (2, 1, 0))
    turn(0, source)

    def activate(at, carry):
        span = pl.ds(pl.multiple_of(at * rows, rows), rows)
        first = first_ref[span, :]
        cdf = 0.5 * (1.0 + lax.erf(first * (0.5**0.5)))
        density = jnp.exp(-0.5 * first * first) * ((2.0 * jnp.pi) ** -0.5)
        hidden_ref[span, :] = (first * cdf).astype(BF16)
        slope_ref[span, :] = cdf + first * density
        return carry

    lax.fori_loop(0, cells // rows, activate, 0)
    turn(1, hidden_ref[...])
    cot = own_ref[:, 1].reshape(cells, channels)
    write_stack(cot, stack_ref, band, step)
    turn(3, cot)
    pre_ref[...] = (slope_ref[...] * convolved_back(stack_ref, two_held, band, cells, second_weight)).astype(BF16)
    turn(2, pre_ref[...])

    for ref, of, half_of in (
        (mine_ref, core, jnp.where(core == 0, 1 - x, 1 - y)),
        (give_ref, 1 - core, jnp.where(core == 0, y, x)),
        (cross_ref, 1 - core, jnp.where(core == 0, 1 - y, 1 - x)),
    ):
        ref[0] = turned_ref[6 * of]
        ref[1] = turned_ref[6 * of + 1]
        ref[2] = turned_ref[4 - 2 * of + half_of]
    kept_ref[...] = turned_ref[4 - 2 * core + jnp.where(core == 0, x, y)]


def outer_kernel(band, step, own_ref, hidden_ref, pre_ref, one_ref, two_ref, out_ref, stack_ref, back_ref):
    cells, channels = hidden_ref.shape
    shape = (out_ref.shape[0],) + out_ref.shape[2:]
    write_stack(hidden_ref[...], stack_ref, band, step)
    write_stack(pre_ref[...], back_ref, band, step)
    second = convolved(stack_ref, two_ref, band, cells)
    source = own_ref[:, 0].reshape(cells, channels)
    out_ref[:, 0] = (source.astype(F32) + second).astype(BF16).reshape(shape)
    back = convolved_back(back_ref, one_ref, band, cells)
    cot = own_ref[:, 1].reshape(cells, channels)
    out_ref[:, 1] = (cot.astype(F32) + back).astype(BF16).reshape(shape)


def units(deep):
    count = deep // 16
    for unit in range(9 * count):
        yield unit // count, (unit % count) * 16, (unit // 4) * 16, unit % 4


def terms_of(band, step, place_ref, sources, whole_ref, moved_ref, write):
    x, y, core = place_ref[0], place_ref[1], place_ref[2]
    half, cells = sources[0][1].shape
    place = lax.broadcasted_iota(jnp.int32, (half, cells), 1) % band
    inside = {
        1: jnp.where(place < band - step, 1.0, 0.0).astype(BF16),
        -1: jnp.where(place >= step, 1.0, 0.0).astype(BF16),
    }
    for at, (ref, moving_ref) in enumerate(sources):
        columns = slice(at * cells, (at + 1) * cells)
        whole_ref[0, :, columns] = ref[0]
        whole_ref[1, :, columns] = ref[1]
        field = moving_ref[...]
        for a in range(-1, 2):
            for b in range(-1, 2):
                shift = (-(b * band + a * step)) % cells
                part = pltpu.roll(field, shift, 1) if shift else field
                if a:
                    part = part * inside[a]
                tap = (a + 1) * 3 + b + 1
                moved_ref[jnp.where(core == 0, 8 - tap, tap), :, columns] = part
    moved = moved_ref[...].reshape(9 * half, len(sources) * cells)
    stays = jnp.where(core == 0, y, x)
    for at, which in enumerate((1 - stays, stays)):
        whole = whole_ref[which]

        @pl.when(core == 0)
        def _():
            write(at, slice(None), lax.dot_general(
                whole, moved, (((1,), (1,)), ((), ())), preferred_element_type=F32
            ))

        @pl.when(core == 1)
        def _():
            terms = lax.dot_general(moved, whole, (((1,), (1,)), ((), ())), preferred_element_type=F32)
            for tap in range(9):
                rows = slice(tap * half, (tap + 1) * half)
                write(at, rows, terms[rows])


def near_kernel(band, step, place_ref, mine_ref, kept_ref, got_ref, sums_ref, whole_ref, moved_ref):
    def write(at, columns, terms):
        sums_ref[at, :, columns] = terms

    sources = ((mine_ref, kept_ref), (got_ref, got_ref.at[2]))
    terms_of(band, step, place_ref, sources, whole_ref, moved_ref, write)


def far_kernel(band, step, place_ref, sums_ref, far_ref, pair_ref, keep_ref, give_ref, whole_ref, moved_ref):
    def write(at, columns, terms):
        ref = (give_ref, keep_ref)[at]
        ref[:, columns] = (sums_ref[at, :, columns] + terms).astype(ref.dtype)

    sources = ((far_ref, far_ref.at[2]), (pair_ref, pair_ref.at[2]))
    terms_of(band, step, place_ref, sources, whole_ref, moved_ref, write)


def pack_kernel(place_ref, keep_ref, got_ref, *refs):
    out_refs, (sums_ref, send_ref, sems) = refs[:-3], refs[-3:]
    me = place_ref[3] * 2 + place_ref[2]
    half = keep_ref.shape[0]
    sums_ref[...] = (keep_ref[...] + got_ref[...].astype(F32)).astype(BF16)
    deep, quarter = half // 4, half // 2
    height = send_ref.shape[1]
    for z in range(4):
        for core in range(2):
            blocks = [[] for _ in range(height // 16)]
            for tap, row, to, _ in units(deep):
                begin, first = z * deep + row, tap * half + core * quarter
                blocks[to // 16].append(sums_ref[begin : begin + 16, first : first + quarter])
            for to, parts in enumerate(blocks):
                while len(parts) < 4:
                    parts.append(jnp.zeros((16, quarter), BF16))
                send_ref[z * 2 + core, to * 16 : (to + 1) * 16, :] = jnp.concatenate(parts, axis=1)
    pairs = [(send_ref.at[me ^ away], ref) for away, ref in enumerate(out_refs)]
    for copy in fetched(pairs, sems):
        copy.wait()


def finish_kernel(scale, place_ref, *refs):
    parts, (one_ref, two_ref) = refs[:-2], refs[-2:]
    core = place_ref[2]
    deep, quarter = one_ref.shape[2:]
    sums = []
    for other in range(2):
        total = parts[other][...].astype(F32)
        for ref in parts[other + 2 :: 2]:
            total = total + ref[...].astype(F32)
        sums.append(total * scale)
    ours, theirs = sums
    for out_ref, total in (
        (one_ref, jnp.where(core == 0, ours, theirs)),
        (two_ref, jnp.where(core == 0, theirs, ours)),
    ):
        for tap, row, begin, slot in units(deep):
            out_ref[tap // 3, tap % 3, row : row + 16, :] = total[
                begin : begin + 16, slot * quarter : (slot + 1) * quarter
            ]


def fast_local(inputs, conv1_weight, conv2_weight, cotangent):
    rows, width, channels = inputs.shape
    every = ("z", "y", "x", "core")
    devices = lax.axis_size(every)
    step = width // devices
    cells = rows * width
    lat = lax.axis_size("x") * lax.axis_size("core")
    lon = devices // lat
    band = rows * lat * step
    half, deep = channels // 2, channels // lon
    height = -(-9 * (deep // 16) // 4) * 16
    scale = (rows * lat * width * lon) ** (-0.5)
    flops = 2 * 9 * cells * channels * channels
    vmem, hbm, smem = (pl.BlockSpec(memory_space=space) for space in (pltpu.VMEM, pltpu.HBM, pltpu.SMEM))

    def held(*shape, kind=BF16):
        return pltpu.VMEM(shape, kind)

    def shaped(*shape, kind=BF16):
        return jax.ShapeDtypeStruct(shape, kind)

    def kernel(body, specs, arguments, out_shape, scratch_shapes, work, megabytes):
        return pl.pallas_call(
            body,
            out_shape=out_shape,
            in_specs=specs,
            out_specs=jax.tree.map(lambda _: vmem, out_shape),
            scratch_shapes=scratch_shapes,
            compiler_params=pltpu.CompilerParams(vmem_limit_bytes=15 * 2**20),
            cost_estimate=pl.CostEstimate(flops=work, bytes_accessed=megabytes * 2**20, transcendentals=0),
        )(*arguments)

    def passed(piece, x, y, core):
        pairs = [(i, i ^ (4 * (i % 2 == y) + 2 * (i % 2 == x) + core)) for i in range(8)]
        return lax.ppermute(piece, ("y", "x", "core"), pairs)

    stack = held(cells + 2 * band, 3 * channels)
    weights = held(*conv1_weight.shape)
    dealt = shaped(devices, 2, rows * step, channels)
    own = kernel(
        functools.partial(deal_kernel, step),
        [hbm] * 2,
        [pltpu.with_memory_space_constraint(field, pltpu.HBM) for field in (inputs, cotangent)],
        dealt,
        [held(2, *inputs.shape), pltpu.SemaphoreType.DMA((2,))],
        10**9,
        3,
    )
    own = lax.all_to_all(own, every, 0, 0, tiled=True)
    place = jnp.stack([lax.axis_index(axis) for axis in ("x", "y", "core", "z")]).astype(jnp.int32)
    one, two = (pltpu.with_memory_space_constraint(w, pltpu.HBM) for w in (conv1_weight, conv2_weight))
    taps = pltpu.SemaphoreType.DMA((2, 3))
    hidden, pre_grad, mine, kept, give, cross = kernel(
        functools.partial(inner_kernel, band, step),
        [smem, vmem, hbm, hbm],
        (place, own, one, two),
        (
            held(cells, channels),
            held(cells, channels),
            held(3, half, cells),
            held(half, cells),
            held(3, half, cells),
            held(3, half, cells),
        ),
        [
            weights,
            weights,
            stack,
            held(cells, channels, kind=F32),
            held(cells, channels, kind=F32),
            held(8, half, cells),
            taps,
        ],
        2 * flops,
        10,
    )
    got = passed(give, None, None, 1)
    far, far_pair = passed(mine, 0, 1, 0), passed(cross, 1, 0, 1)
    room = [held(2, half, 2 * cells), held(9, half, 2 * cells)]
    near = kernel(
        functools.partial(near_kernel, band, step),
        [smem] + [vmem] * 3,
        (place, mine, kept, got),
        held(2, half, 9 * half, kind=F32),
        room,
        2 * flops,
        6,
    )
    hidden, pre_grad, near = lax.optimization_barrier((hidden, pre_grad, near))
    fields = kernel(
        functools.partial(outer_kernel, band, step),
        [vmem] * 5,
        (own, hidden, pre_grad, conv1_weight, conv2_weight),
        dealt,
        [stack, stack],
        2 * flops,
        9,
    )
    _, far, far_pair = lax.optimization_barrier((fields, far, far_pair))
    fields = lax.all_to_all(fields, every, 0, 0, tiled=True)
    output, input_grad = kernel(
        functools.partial(gather_kernel, step), [vmem], (fields,), (shaped(*inputs.shape),) * 2, [], 10**9, 3
    )
    keep, give = kernel(
        functools.partial(far_kernel, band, step),
        [smem] + [vmem] * 3,
        (place, near, far, far_pair),
        (held(half, 9 * half, kind=F32), held(half, 9 * half)),
        room,
        3 * flops,
        6,
    )
    terms = kernel(
        pack_kernel,
        [smem] + [vmem] * 2,
        (place, keep, passed(give, 1, 0, 0)),
        (held(height, channels),) * 8,
        [held(half, 9 * half), held(8, height, channels), pltpu.SemaphoreType.DMA((8,))],
        2 * flops,
        4,
    )
    parts = list(terms)
    for away in (6, 7, 4, 5, 2, 3, 1):
        parts[away] = lax.ppermute(terms[away], ("z", "core"), [(i, i ^ away) for i in range(8)])
    output, input_grad, parts = lax.optimization_barrier((output, input_grad, parts))
    grad = shaped(3, 3, deep, half // 2, kind=F32)
    conv1_grad, conv2_grad = kernel(
        functools.partial(finish_kernel, scale), [smem] + [vmem] * 8, (place, *parts), (grad, grad), [], 10**6, 2
    )
    return (output, input_grad, conv1_grad, conv2_grad)


def is_fast(mesh):
    return dict(mesh.shape) == {"lon": 8, "lat": 4}


def solution(mesh):
    body, lon, lat = local, "lon", "lat"
    if is_fast(mesh):
        lon, lat = ("z", "y"), ("x", "core")
        mesh = jax.sharding.Mesh(mesh.devices.reshape(4, 2, 2, 2), lon + lat)
        body = fast_local
    field, grad = P(lat, lon, None), P(None, None, lon, lat)
    return jax.shard_map(
        body,
        mesh=mesh,
        in_specs=(field, P(), P(), field),
        out_specs=(field, field, grad, grad),
        check_vma=False,
    )
```
